32 devices in a mesh: dp: 8 (over y, x, core), seq: 4 (over z).
Axes of the slice: x: 2, y: 2, z: 4, core: 2. Of those that a mesh axis runs over, the one named last changes fastest.
Arguments:
- block_in: bfloat16 [16, 1024, 2048], P('dp', 'seq'), may hold values from -6 to 6
- doc_starts: int32 [16, 1024], P('dp', 'seq'), may hold values from 0 to 1, as said below
- out_grad: bfloat16 [16, 1024, 2048], P('dp', 'seq'), may hold values from -6 to 6
- w_mix: bfloat16 [2048, 8192], P(('dp', 'seq')), may hold values from -0.125 to 0.125
- w_out: bfloat16 [2048, 2048], P(('dp', 'seq')), may hold values from -0.1875 to 0.1875
- w_gu: bfloat16 [2048, 11264], P(('dp', 'seq')), may hold values from -0.125 to 0.125
- w_down: bfloat16 [5632, 2048], P(('dp', 'seq')), may hold values from -0.109375 to 0.109375
- attn_gain: bfloat16 [2048], P(('dp', 'seq')), may hold values from 0.5 to 1.5
- ffn_gain: bfloat16 [2048], P(('dp', 'seq')), may hold values from 0.5 to 1.5
- group_gain: bfloat16 [128], P(('dp', 'seq')), may hold values from 0.5 to 1.5
- lower_logit: bfloat16 [2048], P(('dp', 'seq')), may hold values from 3 to 10
Outputs:
- block_out: bfloat16 [16, 1024, 2048], P('dp', 'seq')
- in_grad: float32 [16, 1024, 2048], P('dp', 'seq')
- grad_mix: float32 [2048, 8192], P(('dp', 'seq'))
- grad_out: float32 [2048, 2048], P(('dp', 'seq'))
- grad_gu: float32 [2048, 11264], P(('dp', 'seq'))
- grad_down: float32 [5632, 2048], P(('dp', 'seq'))
- grad_attn_gain: float32 [2048], P(('dp', 'seq'))
- grad_ffn_gain: float32 [2048], P(('dp', 'seq'))
- grad_group: float32 [128], P(('dp', 'seq'))
- grad_logit: float32 [2048], P(('dp', 'seq'))
The draws below stay inside these ranges and needn't reach their ends.
Inputs may be any that keep to these rules, and one draw needn't show every extreme that they name: `doc_starts`: position 0 of every sequence is 1. In each group of 2 consecutive sequences, one sequence has no start at positions 128 to 895.
All inputs are finite; a program needn't handle non-finite values.
Results may differ from the reference program's by a relative error of at most 0.014.
Values may be sent and summed in bfloat16 or wider, within the bound.
No kernel may reach another device: no remote copies, remote signals or barrier semaphores. Data moves between devices by JAX's collectives and lax.ppermute only.
A program may use at most 512 MiB of HBM per device.

```python
import jax
import jax.numpy as jnp
from jax import lax

D = 2048
FF = 5632
HEAD = 128
STRETCH = 128
MICRO = 2
PIECE = 256
SEQS = 16
SEQLEN = 1024
N_DP = 8


def draw_doc_starts(key, part):
    key = jax.random.fold_in(key, 11)
    key_level, key_roll, key_pick = jax.random.split(key, 3)
    levels = jax.random.randint(key_level, (SEQS, SEQLEN // STRETCH, 1), 0, 4)
    limits = 8 * jnp.power(4, levels)
    limits = jnp.broadcast_to(limits, (SEQS, SEQLEN // STRETCH, STRETCH)).reshape(SEQS, SEQLEN)
    rolls = jax.random.randint(key_roll, (SEQS, SEQLEN), 0, 1 << 20) % limits
    starts = (rolls == 0).astype(jnp.int32)
    picked = jax.random.randint(key_pick, (SEQS // MICRO, 1), 0, MICRO)
    member_index = jnp.arange(SEQS, dtype=jnp.int32).reshape(SEQS // MICRO, MICRO) % MICRO
    chosen = (member_index == picked).reshape(SEQS)
    positions = jnp.arange(SEQLEN, dtype=jnp.int32)
    middle = (positions >= PIECE // 2) & (positions < SEQLEN - PIECE // 2)
    starts = jnp.where(chosen[:, None] & middle[None, :], 0, starts)
    starts = jnp.where(positions[None, :] == 0, 1, starts)
    return starts.astype(jnp.int32)


def draw_lower_logit(key, part):
    key = jax.random.fold_in(key, 23)
    values = jax.random.uniform(key, (D,), jnp.float32, 3.0, 10.0)
    return values.astype(jnp.bfloat16)


def block_scale(own_key, shape, shards, least, largest):
    factor_of = 1.0
    for position, parts in shards:
        steps = jax.random.uniform(jax.random.fold_in(jax.random.fold_in(own_key, 6), position), (parts,), jnp.float32, least / len(shards), largest / len(shards))
        factor_of = factor_of * jnp.repeat(jnp.exp(steps), shape[position] // parts).reshape((-1,) + (1,) * (len(shape) - 1 - position))
    return factor_of


def normal_values(rng, extent, width, limit, shards=(), kind=jnp.bfloat16):
    array = jax.random.normal(rng, extent, jnp.float32) * width
    if len(shards) > 0:
        array = block_scale(rng, extent, shards, -0.22, 0.18) * array
    return jnp.clip(array, min=-limit, max=limit).astype(kind)


def setup_inputs(seed: int = 0) -> dict:
    streams_of = jax.random.split(jax.random.key(seed), 12)
    block_in = normal_values(streams_of[0], (SEQS, SEQLEN, D), 1.0, 6.0, ((0, 8), (1, 4)))
    doc_starts = draw_doc_starts(jax.random.fold_in(streams_of[11], 71), 0)
    out_grad = normal_values(streams_of[2], (SEQS, SEQLEN, D), 1.0, 6.0, ((0, 8), (1, 4)))
    w_mix = normal_values(streams_of[3], (D, 4 * D), D ** -0.5, 0.125, ((0, 32),))
    w_out = normal_values(streams_of[4], (D, D), (D // 2) ** -0.5, 0.1875, ((0, 32),))
    w_gu = normal_values(streams_of[5], (D, 2 * FF), D ** -0.5, 0.125, ((0, 32),))
    w_down = normal_values(streams_of[6], (FF, D), (FF // 2) ** -0.5, 0.109375, ((0, 32),))
    attn_gain = jnp.clip(1.0 + 0.1 * jax.random.normal(streams_of[7], (D,), jnp.float32), 0.5, 1.5).astype(jnp.bfloat16)
    ffn_gain = jnp.clip(1.0 + 0.1 * jax.random.normal(streams_of[8], (D,), jnp.float32), 0.5, 1.5).astype(jnp.bfloat16)
    group_gain = jnp.clip(1.0 + 0.1 * jax.random.normal(streams_of[9], (HEAD,), jnp.float32), 0.5, 1.5).astype(jnp.bfloat16)
    lower_logit = draw_lower_logit(jax.random.fold_in(streams_of[11], 71), 0)
    return dict(block_in=block_in, doc_starts=doc_starts, out_grad=out_grad, w_mix=w_mix, w_out=w_out, w_gu=w_gu, w_down=w_down, attn_gain=attn_gain, ffn_gain=ffn_gain, group_gain=group_gain, lower_logit=lower_logit)


EPSILON = 1e-06
PRECISE = lax.Precision.HIGHEST

@jax.custom_vjp
def low(v):
    return lax.optimization_barrier(v.astype(jnp.bfloat16)).astype(jnp.float32)

@jax.custom_vjp
def low_back(v):
    return v

def low_keep(v):
    return (low(v), None)

def low_pass(kept, grad):
    return (grad,)

def back_keep(v):
    return (v, None)

def back_low(kept, grad):
    return (low(grad),)
low.defvjp(low_keep, low_pass)
low_back.defvjp(back_keep, back_low)

def matmul(left, right):
    return jnp.einsum('gtd,df->gtf', left, right, precision=PRECISE)

def rms_scale(tensor):
    return lax.rsqrt(lax.optimization_barrier(jnp.mean(tensor * tensor, axis=-1, keepdims=True)) + EPSILON)

def stretch_step(carry_state, inputs):
    queries, keys_in, values, logdecay, starts = inputs
    head_size = queries.shape[-1]
    running = jnp.cumsum(logdecay, axis=2)
    doc_count = jnp.cumsum(starts, axis=1)
    alive_mask = (doc_count == 0).astype(jnp.float32)
    positions = jnp.arange(queries.shape[2])
    causal = positions[:, None] >= positions[None, :]
    same_doc = ((doc_count[:, :, None] == doc_count[:, None, :]) & causal[None]).astype(jnp.float32)
    q_decayed = queries * jnp.exp(running)
    k_grown = keys_in * jnp.exp(-running)
    scores = jnp.einsum('mhte,mhse->mhts', q_decayed, k_grown, precision=PRECISE) * same_doc[:, None]
    inside = jnp.einsum('mhts,mhse->mhte', scores, values, precision=PRECISE)
    carried = jnp.einsum('mhte,mhef->mhtf', q_decayed, carry_state, precision=PRECISE) * alive_mask[:, None, :, None]
    mixed_out = (inside + carried) * head_size ** (-0.5)
    final_sum = running[:, :, -1:, :]
    tail_mask = (doc_count == doc_count[:, -1:]).astype(jnp.float32)
    k_last = keys_in * jnp.exp(final_sum - running) * tail_mask[:, None, :, None]
    fade_out = jnp.exp(final_sum[:, :, 0, :]) * alive_mask[:, None, -1:]
    new_state = fade_out[..., None] * carry_state + jnp.einsum('mhse,mhsf->mhef', k_last, values, precision=PRECISE)
    return (new_state, mixed_out)

def recurrence(queries, keys_in, values, logdecay, starts):
    groups, length, features = queries.shape
    blocks = length // STRETCH

    def to_blocks(tensor):
        shaped = tensor.reshape(groups, blocks, STRETCH, features // HEAD, HEAD)
        return jnp.transpose(shaped, (1, 0, 3, 2, 4))
    start_blocks = jnp.transpose(starts.reshape(groups, blocks, STRETCH), (1, 0, 2))
    initial = jnp.zeros((groups, features // HEAD, HEAD, HEAD), jnp.float32)
    _, outputs = lax.scan(jax.checkpoint(stretch_step), initial, (to_blocks(queries), to_blocks(keys_in), to_blocks(values), to_blocks(logdecay), start_blocks))
    return jnp.transpose(outputs, (1, 0, 3, 2, 4)).reshape(groups, length, features)

def layer(block_f, w_mix, w_out, w_gu, w_down, attn_gain, ffn_gain, group_gain, lower_logit, starts):
    features = block_f.shape[-1]
    normed = low(block_f * rms_scale(block_f) * attn_gain)
    projected = low_back(matmul(normed, w_mix))
    q_pre, f_pre, v_pre, o_pre = jnp.split(projected, 4, axis=-1)
    lower_bound = jax.nn.sigmoid(lower_logit)
    opened = jax.nn.sigmoid(f_pre)
    closed = jax.nn.sigmoid(-f_pre)
    decays = lower_bound + (1.0 - lower_bound) * opened
    keys_in = (1.0 - lower_bound) * closed
    mixed_out = recurrence(jax.nn.silu(q_pre), keys_in, v_pre, jnp.log(decays), starts)
    heads_view = mixed_out.reshape(mixed_out.shape[:-1] + (features // HEAD, HEAD))
    unit_norm = heads_view * rms_scale(heads_view)
    gated_out = low((unit_norm * group_gain).reshape(mixed_out.shape) * jax.nn.silu(o_pre))
    residual = block_f + low_back(matmul(gated_out, w_out))
    normed2 = low(residual * rms_scale(residual) * ffn_gain)
    gate_up = low_back(matmul(normed2, w_gu))
    gate_pre, up_pre = jnp.split(gate_up, 2, axis=-1)
    hidden = low(jax.nn.silu(gate_pre) * up_pre)
    return residual + low_back(matmul(hidden, w_down))

def reference(block_in, doc_starts, out_grad, w_mix, w_out, w_gu, w_down, attn_gain, ffn_gain, group_gain, lower_logit):
    weights = tuple((member.astype(jnp.float32) for member in (w_mix, w_out, w_gu, w_down, attn_gain, ffn_gain, group_gain, lower_logit)))
    inputs_all = block_in.astype(jnp.float32).reshape(N_DP, MICRO, SEQLEN, D)
    starts_all = doc_starts.reshape(N_DP, MICRO, SEQLEN)
    cotangents = out_grad.astype(jnp.float32).reshape(N_DP, MICRO, SEQLEN, D)

    def one_group(totals, entries):
        block_f, starts, cotangent = entries

        def forward(block_v, *params):
            return layer(block_v, *params, starts)
        result, pullback = jax.vjp(forward, block_f, *weights)
        pulled = pullback(cotangent)
        totals = tuple((summed + addend for summed, addend in zip(totals, pulled[1:])))
        return (totals, (result.astype(jnp.bfloat16), pulled[0]))
    zeros_init = tuple((jnp.zeros_like(member) for member in weights))
    totals, (outputs, in_grads) = lax.scan(one_group, zeros_init, (inputs_all, starts_all, cotangents))
    grad_mix, grad_out, grad_gu, grad_down, grad_attn_gain, grad_ffn_gain, grad_group, grad_logit = totals
    block_out = outputs.reshape(SEQS, SEQLEN, D)
    in_grad = in_grads.reshape(SEQS, SEQLEN, D)
    return (block_out, in_grad, grad_mix, grad_out, grad_gu, grad_down, grad_attn_gain, grad_ffn_gain, grad_group, grad_logit)
```

```python
import jax
import jax.numpy as jnp
from jax import lax
from jax.experimental import pallas as pl
from jax.experimental.pallas import tpu as pltpu
from jax.sharding import PartitionSpec as P

HEAD = 128
TEAM = 4
EPSILON = 1e-06
SCALE = HEAD**-0.5
F32 = jnp.float32
BF16 = jnp.bfloat16
VMEM_LIMIT = 60 * 1024 * 1024


class Places:
    def __init__(self, n_dp, n_seq):
        self.n_dp, self.ny, self.nz = n_dp, n_dp // TEAM, n_seq
        place = lax.axis_index("dp")
        self.rank, self.y, self.z = place % TEAM, place // TEAM, lax.axis_index("seq")

    def swap(self, value, bits):
        return lax.ppermute(value, "dp", [(i, i ^ bits) for i in range(self.n_dp)])

    def hop(self, value, axis, pairs):
        if axis == "z":
            return lax.ppermute(value, "seq", pairs)
        spread = [(a * TEAM + r, b * TEAM + r) for a, b in pairs for r in range(TEAM)]
        return lax.ppermute(value, "dp", spread)

    def along(self, axis):
        return (self.ny, self.y) if axis == "y" else (self.nz, self.z)

    def by_rank(self, stack):
        odd, high = (self.rank & 1) == 1, (self.rank & 2) == 2
        stack = jnp.where(odd, jnp.concatenate([stack[1:2], stack[0:1], stack[3:4], stack[2:3]]), stack)
        return jnp.where(high, jnp.concatenate([stack[2:], stack[:2]]), stack)

    def team_gather(self, own):
        one, two = self.swap(own, 1), self.swap(own, 2)
        return [own, one, two, self.swap(two, 1)]

    def team_sum(self, parts):
        near = self.swap(jnp.stack([parts[1], parts[3]]), 1)
        far = (parts[2].astype(F32) + near[1].astype(F32)).astype(BF16)
        mine = parts[0].astype(F32) + near[0].astype(F32)
        return mine + self.swap(far, 2).astype(F32)

    def team_trade(self, stack):
        sent = self.by_rank(stack)
        got = [sent[0]] + [self.swap(sent[j], j) for j in range(1, TEAM)]
        return self.by_rank(jnp.stack(got))

    def gather_line(self, own, axis):
        n, here = self.along(axis)
        found = [(here, own)]
        if n == 2:
            return found + [(1 - here, self.hop(own, axis, [(0, 1), (1, 0)]))]
        ups, downs, up, down = [], [], own, own
        for _ in range(n - 1):
            up = self.hop(up, axis, [(i, i + 1) for i in range(n - 1)])
            down = self.hop(down, axis, [(i + 1, i) for i in range(n - 1)])
            ups.append(up)
            downs.append(down)
        for k in range(n - 1):
            found.append(((here + n - 1 - k) % n, ups[k] + downs[n - 2 - k]))
        return found

    def sum_line(self, piece, axis):
        n, here = self.along(axis)
        if n == 2:
            other = self.hop(piece(1 - here), axis, [(0, 1), (1, 0)])
            return piece(here).astype(F32) + other.astype(F32)
        total = None
        for sign in (1, -1):
            place = here if sign == 1 else n - 1 - here
            moving = None
            for k in range(n - 1):
                slot = (n - 1 - k + place) % n
                share = piece(slot if sign == 1 else n - 1 - slot)
                if moving is not None:
                    share = (share.astype(F32) + moving.astype(F32)).astype(BF16)
                pairs = [(i, i + 1) for i in range(min(k + 1, n - 1))]
                if sign == -1:
                    pairs = [(n - 1 - a, n - 1 - b) for a, b in pairs]
                moving = self.hop(share.astype(BF16), axis, pairs)
            total = moving.astype(F32) if total is None else total + moving.astype(F32)
        return piece(here).astype(F32) + total

    def gather_rows(self, own):
        s, rows, n = own.shape
        whole = jnp.zeros((self.ny, s, self.nz, rows, n), own.dtype)
        for z, value in self.gather_line(own, "z"):
            for y, there in self.gather_line(value, "y"):
                whole = lax.dynamic_update_slice(whole, there[None, :, None], (y, 0, z, 0, 0))
        return whole


def nn(a, b):
    return jnp.dot(a, b, preferred_element_type=F32)


def nt(a, b):
    return lax.dot_general(a, b, (((1,), (1,)), ((), ())), preferred_element_type=F32)


def tn(a, b):
    return lax.dot_general(a, b, (((0,), (0,)), ((), ())), preferred_element_type=F32)


def add_up(matrix, value):
    high = value.astype(BF16)
    rest = value - high.astype(F32)
    mid = rest.astype(BF16)
    low = (rest - mid.astype(F32)).astype(BF16)
    return nn(matrix, high) + nn(matrix, mid) + nn(matrix, low)


def triangle(n, lower):
    row = lax.broadcasted_iota(jnp.int32, (n, n), 0)
    col = lax.broadcasted_iota(jnp.int32, (n, n), 1)
    return row >= col if lower else row <= col


def sigmoid(z):
    return 1.0 / (1.0 + jnp.exp(-z))


def gates(f_pre, lower):
    small = jnp.exp(-jnp.abs(f_pre))
    big_part = 1.0 / (1.0 + small)
    small_part = small * big_part
    positive = f_pre >= 0
    opened = jnp.where(positive, big_part, small_part)
    closed = jnp.where(positive, small_part, big_part)
    return opened, closed, lower + (1.0 - lower) * opened


def wide_blocks(width):
    step = 512
    return [(a, min(a + step, width)) for a in range(0, width, step)]


def mix_kernel(x_ref, gain_ref, w_ref, lower_ref, row_ref, col_ref, *refs):
    normed_ref, proj_ref, run_ref, qd_ref, kg_ref, ins_ref, leave_ref, fade_ref = refs[-8:]
    channels = lower_ref.shape[1]
    x = x_ref[0].astype(F32)
    scale = lax.rsqrt(jnp.mean(x * x, axis=-1, keepdims=True) + EPSILON)
    normed_ref[0] = (x * scale * gain_ref[...]).astype(BF16)
    for a, b in wide_blocks(4 * channels):
        proj_ref[0, :, a:b] = nn(normed_ref[0], w_ref[:, a:b])
    lower = lower_ref[...]
    q_pre = proj_ref[0, :, 0:channels]
    f_pre = proj_ref[0, :, channels : 2 * channels]
    _, closed, decays = gates(f_pre, lower)
    keys = (1.0 - lower) * closed
    length = x.shape[0]
    causal = triangle(length, True)
    running = add_up(causal.astype(BF16), jnp.log(decays))
    run_ref[0] = running
    row, col = row_ref[0], col_ref[0]
    alive = (col[length - 1 :] == 0).astype(F32)
    tail = (col == col[length - 1 :]).astype(F32)
    final = running[length - 1 :]
    fade_ref[0] = jnp.exp(final) * alive
    qd_ref[0] = (q_pre * sigmoid(q_pre) * jnp.exp(running)).astype(BF16)
    kg_ref[0] = (keys * jnp.exp(-running)).astype(BF16)
    last = (keys * jnp.exp(final - running) * tail).astype(BF16)
    mask = jnp.where(causal & (col == row), 1.0, 0.0)
    for h in range(channels // HEAD):
        cut = slice(h * HEAD, (h + 1) * HEAD)
        values = proj_ref[0, :, 2 * channels + h * HEAD : 2 * channels + (h + 1) * HEAD].astype(BF16)
        scores = (nt(qd_ref[0, :, cut], kg_ref[0, :, cut]) * mask).astype(BF16)
        ins_ref[0, :, cut] = nn(scores, values) * SCALE
        leave_ref[0, h] = tn(last[:, cut], values)


def out_kernel(ins_ref, qd_ref, o_ref, state_ref, col_ref, group_ref, w_ref, *refs):
    mixed_ref, gated_ref, part_ref = refs[-3:]
    channels = ins_ref.shape[2]
    alive = (col_ref[0] == 0).astype(F32) * SCALE
    for h in range(channels // HEAD):
        cut = slice(h * HEAD, (h + 1) * HEAD)
        mixed = ins_ref[0, :, cut] + alive * nn(qd_ref[0, :, cut], state_ref[0, h])
        mixed_ref[0, :, cut] = mixed
        scale = lax.rsqrt(jnp.mean(mixed * mixed, axis=-1, keepdims=True) + EPSILON)
        o_pre = o_ref[0, :, cut]
        gated_ref[0, :, cut] = (mixed * scale * group_ref[...] * (o_pre * sigmoid(o_pre))).astype(BF16)
    for a, b in wide_blocks(w_ref.shape[1]):
        part_ref[0, :, a:b] = nn(gated_ref[0], w_ref[:, a:b]).astype(BF16)


def up_kernel(x_ref, w_ref, *refs):
    hidden_ref, first_ref, second_ref = refs[-3:]
    width = hidden_ref.shape[2]
    for a, b in wide_blocks(width):
        gate = nn(x_ref[0], w_ref[:, a:b])
        up = nn(x_ref[0], w_ref[:, width + a : width + b])
        s = sigmoid(gate)
        silu = gate * s
        hidden_ref[0, :, a:b] = (silu * up).astype(BF16)
        first_ref[0, :, a:b] = (up * (s * (1.0 + gate * (1.0 - s)))).astype(BF16)
        second_ref[0, :, a:b] = silu.astype(BF16)


def down_back_kernel(cot_ref, down_ref, w_ref, first_ref, second_ref, *refs):
    both_ref, part_ref = refs[-2:]
    width = first_ref.shape[2]
    for a, b in wide_blocks(width):
        d_hidden = nt(cot_ref[0], down_ref[a:b, :])
        both_ref[0, :, a:b] = (d_hidden * first_ref[0, :, a:b].astype(F32)).astype(BF16)
        both_ref[0, :, width + a : width + b] = (d_hidden * second_ref[0, :, a:b].astype(F32)).astype(BF16)
    for a, b in wide_blocks(part_ref.shape[2]):
        part_ref[0, :, a:b] = nt(both_ref[0], w_ref[a:b, :]).astype(BF16)


def out_back_kernel(branch_ref, w_ref, mixed_ref, o_ref, qd_ref, col_ref, group_ref, *refs):
    d_o_ref, g_ref, toward_ref, sum_ref = refs[-4:]
    channels = mixed_ref.shape[2]
    alive = (col_ref[0] == 0).astype(F32)
    group = group_ref[...]
    d_gated_all = nt(branch_ref[0], w_ref[...])
    for h in range(channels // HEAD):
        cut = slice(h * HEAD, (h + 1) * HEAD)
        d_gated = d_gated_all[:, cut]
        mixed = mixed_ref[0, :, cut]
        scale = lax.rsqrt(jnp.mean(mixed * mixed, axis=-1, keepdims=True) + EPSILON)
        unit = mixed * scale
        o_pre = o_ref[0, :, cut]
        s = sigmoid(o_pre)
        silu = o_pre * s
        both = d_gated * unit
        d_o_ref[0, :, cut] = (both * group * (s * (1.0 + o_pre * (1.0 - s)))).astype(BF16)
        sum_ref[0, :, cut] = jnp.sum(both * silu, axis=0, keepdims=True)
        d_unit = d_gated * group * silu
        d_mixed = scale * (d_unit - unit * jnp.mean(d_unit * unit, axis=-1, keepdims=True))
        g = (d_mixed * SCALE).astype(BF16)
        g_ref[0, :, cut] = g
        reach = (qd_ref[0, :, cut].astype(F32) * alive).astype(BF16)
        toward_ref[0, h] = tn(reach, g)


def mix_back_kernel(
    q_ref, f_ref, v_ref, run_ref, qd_ref, kg_ref, g_ref, state_ref, adjoint_ref, d_o_ref, lower_ref, row_ref, col_ref, *refs
):
    proj_ref, sum_ref = refs[-2:]
    channels = lower_ref.shape[1]
    length = row_ref.shape[2]
    lower = lower_ref[...]
    row, col = row_ref[0], col_ref[0]
    alive = (col == 0).astype(F32)
    alive_end = alive[length - 1 :]
    tail = (col == col[length - 1 :]).astype(F32)
    mask = jnp.where(triangle(length, True) & (col == row), 1.0, 0.0)
    later = triangle(length, False).astype(BF16)
    eye = lax.broadcasted_iota(jnp.int32, (HEAD, HEAD), 0) == lax.broadcasted_iota(jnp.int32, (HEAD, HEAD), 1)
    for h in range(channels // HEAD):
        cut = slice(h * HEAD, (h + 1) * HEAD)
        q_pre, f_pre = q_ref[0, :, cut], f_ref[0, :, cut]
        values = v_ref[0, :, cut].astype(BF16)
        running = run_ref[0, :, cut]
        qd, kg, g = qd_ref[0, :, cut], kg_ref[0, :, cut], g_ref[0, :, cut]
        state, adjoint = state_ref[0, h], adjoint_ref[0, h]
        low = lower[:, cut]
        opened, closed, decays = gates(f_pre, low)
        keys = (1.0 - low) * closed
        final = running[length - 1 :]
        last_factor = jnp.exp(final - running) * tail
        last = (keys * last_factor).astype(BF16)
        scores = (nt(qd, kg) * mask).astype(BF16)
        d_values = tn(scores, g) + nn(last, adjoint)
        d_scores = (nt(g, values) * mask).astype(BF16)
        d_qd = nn(d_scores, kg) + alive * nt(g, state)
        d_kg = tn(d_scores, qd)
        d_last = nt(values, adjoint)
        part_last = d_last * last.astype(F32)
        moved = d_qd * qd.astype(F32) - d_kg * kg.astype(F32) - part_last
        passed = jnp.sum(adjoint.astype(F32) * state.astype(F32), axis=1, keepdims=True)
        passed = jnp.sum(jnp.where(eye, passed, 0.0), axis=0, keepdims=True)
        d_final = jnp.sum(part_last, axis=0, keepdims=True) + passed * jnp.exp(final) * alive_end
        d_log = add_up(later, moved) + d_final
        d_queries = d_qd * jnp.exp(running)
        d_keys = d_kg * jnp.exp(-running) + d_last * last_factor
        common = d_log / decays - d_keys
        s = sigmoid(q_pre)
        proj_ref[0, :, cut] = (d_queries * (s * (1.0 + q_pre * (1.0 - s)))).astype(BF16)
        proj_ref[0, :, channels + h * HEAD : channels + (h + 1) * HEAD] = (
            (1.0 - low) * opened * closed * common
        ).astype(BF16)
        proj_ref[0, :, 2 * channels + h * HEAD : 2 * channels + (h + 1) * HEAD] = d_values.astype(BF16)
        sum_ref[0, :, cut] = jnp.sum(closed * common, axis=0, keepdims=True)
    proj_ref[0, :, 3 * channels :] = d_o_ref[0]


def over_sequences(kernel, name, chunk, count, total, ins, outs, shared, flops):
    del name

    def spec(shape, kind):
        if kind == "whole":
            return pl.BlockSpec(shape, lambda j: (0,) * len(shape), pipeline_mode=pl.Buffered(1))
        offset = chunk * count if kind == "all" or isinstance(kind, tuple) and kind[0] == "all" else 0
        if isinstance(kind, tuple):
            _, width, at = kind
            return pl.BlockSpec((1, shape[1], width), lambda j: (offset + j, 0, at))
        return pl.BlockSpec((1,) + shape[1:], lambda j: (offset + j,) + (0,) * (len(shape) - 1))

    arrays = [a for a, _ in ins]
    in_specs = [spec(a.shape, kind) for a, kind in ins]
    aliases = {}
    for i, held in enumerate(shared):
        if held is not None:
            aliases[len(arrays)] = i
            arrays.append(held)
            in_specs.append(pl.BlockSpec(memory_space=pl.ANY))
    size = sum(a.size * a.dtype.itemsize for a in arrays)
    return pl.pallas_call(
        kernel,
        grid=(count,),
        in_specs=in_specs,
        out_specs=[spec(shape, kind) for shape, _, kind in outs],
        out_shape=[jax.ShapeDtypeStruct(shape, kind) for shape, kind, _ in outs],
        input_output_aliases=aliases,
        compiler_params=pltpu.CompilerParams(vmem_limit_bytes=VMEM_LIMIT),
        cost_estimate=pl.CostEstimate(flops=flops, bytes_accessed=size, transcendentals=0),
    )(*arrays)


def build(n_dp, n_seq):
    def local(block_in, doc_starts, out_grad, w_mix, w_out, w_gu, w_down, attn_gain, ffn_gain, group_gain, lower_logit):
        at = Places(n_dp, n_seq)
        ny, nz = at.ny, at.nz
        micro, length, features = block_in.shape
        rows = w_mix.shape[0]
        own_channels = ny * nz * rows
        heads = own_channels // HEAD
        strip = own_channels // ny
        ff_rows = w_down.shape[0]
        own_ff = ny * nz * ff_rows
        ff_strip = nz * ff_rows
        total = micro * TEAM
        tokens = total * length

        mix_parts = jnp.transpose(w_mix.reshape(rows, 4, ny, TEAM, strip), (3, 0, 1, 2, 4))
        mix_own = at.team_trade(mix_parts.reshape(TEAM, rows, 4 * own_channels))
        gu_parts = jnp.transpose(w_gu.reshape(rows, 2, ny, TEAM, ff_strip), (3, 0, 1, 2, 4))
        gu_own = at.team_trade(gu_parts.reshape(TEAM, rows, 2 * own_ff))
        whole_mix = at.gather_rows(mix_own).reshape(features, 4 * own_channels)

        scales = jnp.concatenate([attn_gain, ffn_gain, lower_logit, group_gain])
        scales = jnp.pad(scales, (0, -scales.shape[0] % HEAD))
        scales = at.by_rank(jnp.stack(at.team_gather(scales)))
        scales = at.gather_rows(scales[:, None, :]).reshape(ny * TEAM * nz, -1).astype(F32)
        attn_scale = scales[:, :rows].reshape(1, features)
        ffn_scale = scales[:, rows : 2 * rows].reshape(1, features)
        logits = scales[:, 2 * rows : 3 * rows].reshape(ny, TEAM, nz * rows)
        own_logit = lax.dynamic_index_in_dim(logits, at.rank, 1, False).reshape(1, own_channels)
        group_scale = scales[:, 3 * rows : 3 * rows + group_gain.shape[0]].reshape(1, HEAD)
        bound = jax.nn.sigmoid(own_logit)

        starts = jnp.stack(at.team_gather(doc_starts.astype(BF16)), axis=1)
        upto = (jnp.arange(length)[:, None] <= jnp.arange(length)[None, :]).astype(BF16)
        counts = jnp.dot(starts.reshape(total, length), upto, preferred_element_type=F32)
        count_row = counts.reshape(total, 1, length)
        count_col = counts.reshape(total, length, 1)

        inputs = [jnp.stack(at.team_gather(block_in[c])) for c in range(micro)]
        whole_out = at.gather_rows(w_out[None]).reshape(own_channels, features)
        cotangent = jnp.concatenate([jnp.stack(at.team_gather(out_grad[c])) for c in range(micro)])
        whole_gu = at.gather_rows(gu_own).reshape(features, 2 * own_ff)
        whole_down = at.gather_rows(w_down[None]).reshape(own_ff, features)

        def run(kernel, name, chunk, ins, outs, shared, flops):
            return over_sequences(kernel, name, chunk, TEAM, total, ins, outs, shared, flops)

        def pass_on(leaving, fade, sign):
            factor = fade.reshape(TEAM, heads, HEAD)[..., None]
            entering = jnp.zeros(leaving.shape, F32)
            for k in range(nz - 1):
                pair = (k, k + 1) if sign == 1 else (nz - 1 - k, nz - 2 - k)
                entering = entering + at.hop((factor * entering + leaving).astype(BF16), "z", [pair]).astype(F32)
            return entering.astype(BF16)

        span = (total, length)
        part = (TEAM, length)
        wide = 4 * own_channels
        per_matmul = 2 * TEAM * length * features

        normed = gated = hidden = first = second = None
        proj = running = qd = kg = mixed = None
        entering, residual, normed2 = [], [], []
        fades = []
        for c in range(micro):
            rows_c, cols_c = (a[c * TEAM : (c + 1) * TEAM] for a in (count_row, count_col))
            normed, proj, running, qd, kg, inside, leaving, fade = run(
                mix_kernel, "mix", c,
                [(inputs[c], "part"), (attn_scale, "whole"), (whole_mix, "whole"), (bound, "whole"), (rows_c, "part"), (cols_c, "part")],
                [
                    (span + (features,), BF16, "all"),
                    (span + (wide,), F32, "all"),
                    (span + (own_channels,), F32, "all"),
                    (span + (own_channels,), BF16, "all"),
                    (span + (own_channels,), BF16, "all"),
                    (part + (own_channels,), F32, "part"),
                    (TEAM_STATES := (TEAM, heads, HEAD, HEAD), F32, "part"),
                    ((TEAM, 1, own_channels), F32, "part"),
                ],
                [normed, proj, running, qd, kg],
                per_matmul * wide,
            )
            fades.append(fade)
            entering.append(pass_on(leaving, fade, 1))
            mixed, gated, partial = run(
                out_kernel, "out", c,
                [
                    (inside, "part"), (qd, "all"), (proj, ("all", own_channels, 3)), (entering[c], "part"), (cols_c, "part"),
                    (group_scale, "whole"), (whole_out, "whole"),
                ],
                [(span + (own_channels,), F32, "all"), (span + (own_channels,), BF16, "all"), (part + (features,), BF16, "part")],
                [mixed, gated],
                per_matmul * own_channels,
            )
            residual.append(block_in[c].astype(F32) + at.team_sum(partial))
            rms_two = lax.rsqrt(jnp.mean(residual[c] * residual[c], axis=-1, keepdims=True) + EPSILON)
            normed2.append(jnp.stack(at.team_gather((residual[c] * rms_two * ffn_scale).astype(BF16))))
            hidden, first, second = run(
                up_kernel, "up", c,
                [(normed2[c], "part"), (whole_gu, "whole")],
                [(span + (own_ff,), BF16, "all")] * 3,
                [hidden, first, second],
                per_matmul * 2 * own_ff,
            )

        both = d_proj = None
        d_residual, d_branch, gain_sums = [], [], []
        for c in range(micro):
            both, partial = run(
                down_back_kernel, "down_back", c,
                [(cotangent, "all"), (whole_down, "whole"), (whole_gu, "whole"), (first, "all"), (second, "all")],
                [(span + (2 * own_ff,), BF16, "all"), (part + (features,), BF16, "part")],
                [both],
                per_matmul * 3 * own_ff,
            )
            d_normed2 = at.team_sum(partial)
            res = residual[c]
            rms_two = lax.rsqrt(jnp.mean(res * res, axis=-1, keepdims=True) + EPSILON)
            gain_sums.append(jnp.sum(d_normed2 * res * rms_two, axis=0))
            scaled = d_normed2 * ffn_scale
            d_residual.append(
                out_grad[c].astype(F32)
                + rms_two * (scaled - res * rms_two * rms_two * jnp.mean(scaled * res, axis=-1, keepdims=True))
            )
            d_branch.append(jnp.stack(at.team_gather(d_residual[c].astype(BF16))))

        def flat(a):
            return a.reshape(tokens, a.shape[-1])

        def column_piece(left, right, count):
            size = left.shape[1] // count
            if count == 2:
                return lambda j: tn(lax.dynamic_slice_in_dim(left, j * size, size, 1), right)
            product = tn(left, right).reshape(count, size, right.shape[1])
            return lambda j: lax.dynamic_index_in_dim(product, j, 0, False)

        def weight_sum(left, right, blocks):
            piece = column_piece(left, right, ny)
            sent = at.sum_line(lambda j: piece(j).astype(BF16), "y") if ny != 2 else None
            if sent is None:
                other = at.hop(piece(1 - at.y).astype(BF16), "y", [(0, 1), (1, 0)])
                sent = piece(at.y) + other.astype(F32)
            sent = sent.astype(BF16).reshape(blocks, nz, -1, right.shape[1])
            return at.sum_line(lambda j: lax.dynamic_index_in_dim(sent, j, 1, False), "z")

        grad_down = weight_sum(flat(hidden), flat(cotangent), 1)[0]
        gu_sum = weight_sum(flat(jnp.concatenate(normed2)), flat(both), TEAM)

        group_sums, logit_sums = [], []
        for c in range(micro):
            rows_c, cols_c = (a[c * TEAM : (c + 1) * TEAM] for a in (count_row, count_col))
            d_o, g, toward, group_sum = run(
                out_back_kernel, "out_back", c,
                [
                    (d_branch[c], "part"), (whole_out, "whole"), (mixed, "all"), (proj, ("all", own_channels, 3)), (qd, "all"),
                    (cols_c, "part"), (group_scale, "whole"),
                ],
                [
                    (part + (own_channels,), BF16, "part"), (part + (own_channels,), BF16, "part"),
                    (TEAM_STATES, F32, "part"), ((TEAM, 1, own_channels), F32, "part"),
                ],
                [],
                per_matmul * own_channels,
            )
            group_sums.append(group_sum)
            adjoint = pass_on(toward, fades[c], -1)
            d_proj, logit_sum = run(
                mix_back_kernel, "mix_back", c,
                [
                    (proj, ("all", own_channels, 0)), (proj, ("all", own_channels, 1)), (proj, ("all", own_channels, 2)),
                    (running, "all"), (qd, "all"), (kg, "all"), (g, "part"), (entering[c], "part"), (adjoint, "part"),
                    (d_o, "part"), (bound, "whole"), (rows_c, "part"), (cols_c, "part"),
                ],
                [(span + (wide,), BF16, "all"), ((TEAM, 1, own_channels), F32, "part")],
                [d_proj],
                per_matmul * own_channels,
            )
            logit_sums.append(logit_sum)

        mix_sum = weight_sum(flat(normed), flat(d_proj), TEAM)
        grad_out = weight_sum(flat(gated), flat(jnp.concatenate(d_branch)), 1)[0]
        d_normed_parts = times_transpose(flat(d_proj), whole_mix).astype(BF16).reshape(micro, TEAM, length, features)
        ffn_parts = nn(flat(hidden), whole_down).astype(BF16).reshape(micro, TEAM, length, features)

        def out_of_team(summed, count):
            got = at.team_trade(summed.astype(BF16)).astype(F32)
            width = got.shape[2] // (count * ny)
            got = got.reshape(TEAM, rows, count, ny, width)
            return jnp.transpose(got, (1, 2, 3, 0, 4)).reshape(rows, -1)

        grad_mix = out_of_team(mix_sum, 4)
        grad_gu = out_of_team(gu_sum, 2)

        d_normed = at.team_sum([d_normed_parts[:, j] for j in range(TEAM)])
        ffn_out = at.team_sum([ffn_parts[:, j] for j in range(TEAM)])
        block_out = (jnp.stack(residual) + ffn_out).astype(BF16)
        x = block_in.astype(F32)
        rms_one = lax.rsqrt(jnp.mean(x * x, axis=-1, keepdims=True) + EPSILON)
        attn_sum = jnp.sum(d_normed * x * rms_one, axis=(0, 1))
        scaled = d_normed * attn_scale
        in_grad = jnp.stack(d_residual) + rms_one * (
            scaled - x * rms_one * rms_one * jnp.mean(scaled * x, axis=-1, keepdims=True)
        )

        logit_sum = bound[0] * (1.0 - bound[0]) * sum(jnp.sum(a, axis=(0, 1)) for a in logit_sums)
        logit_all = jnp.where(
            jnp.arange(TEAM)[None, :, None] == at.rank, logit_sum.reshape(ny, 1, strip), 0.0
        ).reshape(features)
        group_all = jnp.sum(sum(jnp.sum(a, axis=(0, 1)) for a in group_sums).reshape(heads, HEAD), axis=0)
        sums = lax.psum(jnp.concatenate([attn_sum, sum(gain_sums), logit_all, group_all]), ("dp", "seq"))
        here = lax.axis_index("dp") * nz + at.z

        def mine(start, size):
            return lax.dynamic_slice_in_dim(sums, start + here * size, size)

        return (
            block_out,
            in_grad,
            grad_mix,
            grad_out,
            grad_gu,
            grad_down,
            mine(0, rows),
            mine(features, rows),
            mine(3 * features, group_gain.shape[0]),
            mine(2 * features, rows),
        )

    return local


def times_transpose(left, right):
    return nt(left, right)


def solution(mesh):
    tokens = P("dp", "seq", None)
    matrix = P(("dp", "seq"), None)
    vector = P(("dp", "seq"))
    return jax.shard_map(
        build(mesh.shape["dp"], mesh.shape["seq"]),
        mesh=mesh,
        in_specs=(tokens, P("dp", "seq"), tokens) + (matrix,) * 4 + (vector,) * 4,
        out_specs=(tokens, tokens) + (matrix,) * 4 + (vector,) * 4,
        check_vma=False,
    )
```

```python
from functools import partial

import jax
import jax.numpy as jnp
from jax import lax
from jax.experimental import pallas as pl
from jax.experimental.pallas import tpu as pltpu
from jax.sharding import Mesh, PartitionSpec as P

HEAD = 128
TEAM = 4
EPSILON = 1e-06
SCALE = HEAD**-0.5
F32 = jnp.float32
BF16 = jnp.bfloat16
VMEM_LIMIT = 60 * 1024 * 1024


class Places:
    def __init__(self, ny, nz):
        self.ny, self.nz = ny, nz
        self.rank, self.y, self.z = lax.axis_index("team"), lax.axis_index("y"), lax.axis_index("seq")

    def swap(self, value, bits):
        return lax.ppermute(value, "team", [(i, i ^ bits) for i in range(TEAM)])

    def swap_y(self, value, bits):
        return lax.ppermute(value, "y", [(i, i ^ bits) for i in range(self.ny)])

    def swap_z(self, value, bits):
        return lax.ppermute(value, "seq", [(i, i ^ bits) for i in range(self.nz)])

    def by_rank(self, stack):
        odd, high = (self.rank & 1) == 1, (self.rank & 2) == 2
        stack = jnp.where(odd, jnp.concatenate([stack[1:2], stack[0:1], stack[3:4], stack[2:3]]), stack)
        return jnp.where(high, jnp.concatenate([stack[2:], stack[:2]]), stack)

    def team_gather(self, own):
        one, two = self.swap(own, 1), self.swap(own, 2)
        return [own, one, two, self.swap(two, 1)]

    def team_sum(self, even, odd, first_held, *held):
        near = self.swap(after(odd, *first_held), 1)
        sent = (even[:, 1].astype(F32) + after(near, *held)[:, 1].astype(F32)).astype(BF16)
        return even[:, 0].astype(F32) + near[:, 0].astype(F32) + self.swap(sent, 2).astype(F32), sent


    def gather_blocks(self, own):
        found = {(0, 0): own}
        for step in [1 << i for i in reversed(range(self.nz.bit_length() - 1))]:
            found.update({(0, dz ^ step): self.swap_z(v, step) for (_, dz), v in list(found.items())})
        for step in [1 << i for i in range(self.ny.bit_length() - 1)]:
            found.update({(dy ^ step, dz): self.swap_y(v, step) for (dy, dz), v in list(found.items())})
        return found

    def everyone_sum(self, value):
        for step in (2, 1):
            value = value + self.swap(value, step)
        for step in [1 << i for i in reversed(range(self.ny.bit_length() - 1))]:
            value = value + self.swap_y(value, step)
        for step in [1 << i for i in reversed(range(self.nz.bit_length() - 1))]:
            value = value + self.swap_z(value, step)
        return value


class Weight:
    def __init__(self, at, found):
        self.ny, self.nz = at.ny, at.nz
        if isinstance(found, dict):
            self.s, self.rows, self.n = found[0, 0].shape
            self.keys, self.blocks = list(found), list(found.values())
        else:
            self.s, self.rows, self.n = found.shape[1:]
            self.keys, self.blocks = None, [found]
        self.height = self.ny * self.nz * self.s * self.rows
        self.split = self.rows % 16 == 0
        if not self.split:
            if self.keys:
                found = jnp.zeros((self.ny, self.nz) + self.blocks[0].shape, BF16)
                for (dy, dz), block in zip(self.keys, self.blocks):
                    found = lax.dynamic_update_slice(found, block[None, None], (at.y ^ dy, at.z ^ dz, 0, 0, 0))
            found = found.reshape(self.ny, self.nz, self.s, self.rows, self.n)
            self.blocks = [jnp.swapaxes(found, 1, 2).reshape(self.height, self.n)]

    @property
    def copies(self):
        return self.ny * self.nz * self.s if self.split else 1

    def load(self, refs, place_ref, into, sems):
        for copy in self.copies_of(refs, place_ref, into, sems):
            copy.start()

    def copies_of(self, refs, place_ref, into, sems):
        if not self.split:
            return [pltpu.make_async_copy(refs[0], into, sems.at[0])]
        rank, y, z = place_ref[0], place_ref[1], place_ref[2]
        if self.keys:
            blocks = [(y ^ dy, z ^ dz, ref) for (dy, dz), ref in zip(self.keys, refs)]
        else:
            blocks = [(i // self.nz, i % self.nz, refs[0].at[i]) for i in range(self.ny * self.nz)]
        copies = []
        for there_y, there_z, ref in blocks:
            for j in range(self.s):
                s = rank ^ j if self.s > 1 else 0
                row = ((there_y * self.s + s) * self.nz + there_z) * self.rows
                if not isinstance(row, int):
                    row = pl.multiple_of(row, self.rows)
                copies.append(pltpu.make_async_copy(ref.at[j], into.at[pl.ds(row, self.rows)], sems.at[len(copies)]))
        return copies


def nn(a, b):
    return jnp.dot(a, b, preferred_element_type=F32)


def nt(a, b):
    return lax.dot_general(a, b, (((1,), (1,)), ((), ())), preferred_element_type=F32)


def tn(a, b):
    return lax.dot_general(a, b, (((0,), (0,)), ((), ())), preferred_element_type=F32)


def add_up(matrix, value):
    high = value.astype(BF16)
    rest = value - high.astype(F32)
    mid = rest.astype(BF16)
    low = (rest - mid.astype(F32)).astype(BF16)
    return nn(matrix, high) + nn(matrix, mid) + nn(matrix, low)


def triangle(n, lower):
    row = lax.broadcasted_iota(jnp.int32, (n, n), 0)
    col = lax.broadcasted_iota(jnp.int32, (n, n), 1)
    return row >= col if lower else row <= col


def sigmoid(z):
    return 1.0 / (1.0 + jnp.exp(-z))


def gates(f_pre, lower):
    small = jnp.exp(-jnp.abs(f_pre))
    big_part = 1.0 / (1.0 + small)
    small_part = small * big_part
    positive = f_pre >= 0
    opened = jnp.where(positive, big_part, small_part)
    closed = jnp.where(positive, small_part, big_part)
    return opened, closed, lower + (1.0 - lower) * opened


def wide_blocks(width):
    step = 512
    return [(a, min(a + step, width)) for a in range(0, width, step)]


def take_piece(step, piece_refs, into_ref):
    for j, ref in enumerate(piece_refs):

        @pl.when(step == j)
        def _(ref=ref):
            into_ref[0] = ref[...]


def put_share(step, even_ref, odd_ref, a, b, value):
    value = value.astype(BF16)

    @pl.when(step % 2 == 0)
    def _():
        even_ref[0, :, a:b] = value

    @pl.when(step % 2 == 1)
    def _():
        odd_ref[0, :, a:b] = value


def pick_kernel(strip, place_ref, w_ref, extra_ref, *out_refs):
    rank = place_ref[0]
    count = w_ref.shape[1] // (TEAM * strip)
    for j, out_ref in enumerate(out_refs):
        for k in range(count):
            at = pl.multiple_of((k * TEAM + (rank ^ j)) * strip, strip)
            out_ref[:, k * strip : (k + 1) * strip] = w_ref[:, pl.ds(at, strip)]
        out_ref[:, count * strip :] = extra_ref[...]


def mix_kernel(strip, step, fetch, piece_refs, place_ref, row_ref, col_ref, *refs):
    normed_ref, proj_ref, run_ref, qd_ref, kg_ref, ins_ref, leave_ref, fade_ref, scales_ref, lower_ref = refs
    channels = lower_ref.shape[1]
    (w_ref,) = fetch()

    @pl.when(step == 0)
    def _():
        row = lax.broadcasted_iota(jnp.int32, (8, HEAD), 0)
        col = lax.broadcasted_iota(jnp.int32, (8, HEAD), 1)
        pick = jnp.where(row == col, 1.0, 0.0).astype(BF16)
        scales_ref[...] = nt(pick, w_ref[:, 4 * channels :])
        for k in range(channels // strip):
            at = pl.multiple_of((k * TEAM + place_ref[0]) * strip, strip)
            lower_ref[:, k * strip : (k + 1) * strip] = sigmoid(scales_ref[2:3, pl.ds(at, strip)])

    gain = scales_ref[0:1]
    take_piece(step, piece_refs, normed_ref)
    x = normed_ref[0].astype(F32)
    scale = lax.rsqrt(jnp.mean(x * x, axis=-1, keepdims=True) + EPSILON)
    normed_ref[0] = (x * scale * gain).astype(BF16)
    for a, b in wide_blocks(4 * channels):
        proj_ref[0, :, a:b] = nn(normed_ref[0], w_ref[:, a:b])
    lower = lower_ref[...]
    q_pre = proj_ref[0, :, 0:channels]
    f_pre = proj_ref[0, :, channels : 2 * channels]
    _, closed, decays = gates(f_pre, lower)
    keys = (1.0 - lower) * closed
    length = x.shape[0]
    causal = triangle(length, True)
    running = add_up(causal.astype(BF16), jnp.log(decays))
    run_ref[0] = running
    row, col = row_ref[0], col_ref[0]
    alive = (col[length - 1 :] == 0).astype(F32)
    tail = (col == col[length - 1 :]).astype(F32)
    final = running[length - 1 :]
    fade_ref[0] = jnp.exp(final) * alive
    qd_ref[0] = (q_pre * sigmoid(q_pre) * jnp.exp(running)).astype(BF16)
    kg_ref[0] = (keys * jnp.exp(-running)).astype(BF16)
    last = (keys * jnp.exp(final - running) * tail).astype(BF16)
    mask = jnp.where(causal & (col == row), 1.0, 0.0)
    for h in range(channels // HEAD):
        cut = slice(h * HEAD, (h + 1) * HEAD)
        values = proj_ref[0, :, 2 * channels + h * HEAD : 2 * channels + (h + 1) * HEAD].astype(BF16)
        scores = (nt(qd_ref[0, :, cut], kg_ref[0, :, cut]) * mask).astype(BF16)
        ins_ref[0, :, cut] = nn(scores, values) * SCALE
        leave_ref[0, h] = tn(last[:, cut], values)


def out_kernel(step, fetch, piece_refs, ins_ref, qd_ref, o_ref, state_ref, col_ref, group_ref, *refs):
    mixed_ref, gated_ref, even_ref, odd_ref = refs
    channels = ins_ref.shape[2]
    alive = (col_ref[0] == 0).astype(F32) * SCALE
    for h in range(channels // HEAD):
        cut = slice(h * HEAD, (h + 1) * HEAD)
        mixed = ins_ref[0, :, cut] + alive * nn(qd_ref[0, :, cut], state_ref[0, h])
        mixed_ref[0, :, cut] = mixed
        scale = lax.rsqrt(jnp.mean(mixed * mixed, axis=-1, keepdims=True) + EPSILON)
        o_pre = o_ref[0, :, cut]
        gated_ref[0, :, cut] = (mixed * scale * group_ref[...] * (o_pre * sigmoid(o_pre))).astype(BF16)
    (w_ref,) = fetch()
    for a, b in wide_blocks(w_ref.shape[1]):
        put_share(step, even_ref, odd_ref, a, b, nn(gated_ref[0], w_ref[:, a:b]))


def up_kernel(step, fetch, piece_refs, normed_ref, hidden_ref, first_ref, second_ref):
    width = hidden_ref.shape[2]
    take_piece(step, piece_refs, normed_ref)
    (w_ref,) = fetch()
    for a, b in wide_blocks(width):
        gate = nn(normed_ref[0], w_ref[:, a:b])
        up = nn(normed_ref[0], w_ref[:, width + a : width + b])
        s = sigmoid(gate)
        silu = gate * s
        hidden_ref[0, :, a:b] = (silu * up).astype(BF16)
        first_ref[0, :, a:b] = (up * (s * (1.0 + gate * (1.0 - s)))).astype(BF16)
        second_ref[0, :, a:b] = silu.astype(BF16)


def down_back_kernel(step, fetch, piece_refs, cot_ref, first_ref, second_ref, both_ref, even_ref, odd_ref):
    width = first_ref.shape[2]
    down_ref, w_ref = fetch()
    for a, b in wide_blocks(width):
        d_hidden = nt(cot_ref[0], down_ref[a:b, :])
        both_ref[0, :, a:b] = (d_hidden * first_ref[0, :, a:b].astype(F32)).astype(BF16)
        both_ref[0, :, width + a : width + b] = (d_hidden * second_ref[0, :, a:b].astype(F32)).astype(BF16)
    for a, b in wide_blocks(w_ref.shape[0]):
        put_share(step, even_ref, odd_ref, a, b, nt(both_ref[0], w_ref[a:b, :]))


def out_back_kernel(step, fetch, piece_refs, mixed_ref, o_ref, qd_ref, col_ref, group_ref, *refs):
    branch_ref, d_o_ref, g_ref, toward_ref, sum_ref = refs
    channels = mixed_ref.shape[2]
    take_piece(step, piece_refs, branch_ref)
    alive = (col_ref[0] == 0).astype(F32)
    group = group_ref[...]
    (w_ref,) = fetch()
    d_gated_all = nt(branch_ref[0], w_ref[...])
    for h in range(channels // HEAD):
        cut = slice(h * HEAD, (h + 1) * HEAD)
        d_gated = d_gated_all[:, cut]
        mixed = mixed_ref[0, :, cut]
        scale = lax.rsqrt(jnp.mean(mixed * mixed, axis=-1, keepdims=True) + EPSILON)
        unit = mixed * scale
        o_pre = o_ref[0, :, cut]
        s = sigmoid(o_pre)
        silu = o_pre * s
        both = d_gated * unit
        d_o_ref[0, :, cut] = (both * group * (s * (1.0 + o_pre * (1.0 - s)))).astype(BF16)
        sum_ref[0, :, cut] = jnp.sum(both * silu, axis=0, keepdims=True)
        d_unit = d_gated * group * silu
        d_mixed = scale * (d_unit - unit * jnp.mean(d_unit * unit, axis=-1, keepdims=True))
        g = (d_mixed * SCALE).astype(BF16)
        g_ref[0, :, cut] = g
        reach = (qd_ref[0, :, cut].astype(F32) * alive).astype(BF16)
        toward_ref[0, h] = tn(reach, g)


def mix_back_kernel(
    step, fetch, piece_refs, q_ref, f_ref, v_ref, run_ref, qd_ref, kg_ref, g_ref, state_ref, adjoint_ref, lower_ref,
    row_ref, col_ref, d_o_ref, d_q_ref, d_fv_ref, sum_ref, even_ref, odd_ref,
):
    channels = lower_ref.shape[1]
    length = row_ref.shape[2]
    lower = lower_ref[...]
    row, col = row_ref[0], col_ref[0]
    alive = (col == 0).astype(F32)
    alive_end = alive[length - 1 :]
    tail = (col == col[length - 1 :]).astype(F32)
    mask = jnp.where(triangle(length, True) & (col == row), 1.0, 0.0)
    later = triangle(length, False).astype(BF16)
    eye = lax.broadcasted_iota(jnp.int32, (HEAD, HEAD), 0) == lax.broadcasted_iota(jnp.int32, (HEAD, HEAD), 1)
    for h in range(channels // HEAD):
        cut = slice(h * HEAD, (h + 1) * HEAD)
        q_pre, f_pre = q_ref[0, :, cut], f_ref[0, :, cut]
        values = v_ref[0, :, cut].astype(BF16)
        running = run_ref[0, :, cut]
        qd, kg, g = qd_ref[0, :, cut], kg_ref[0, :, cut], g_ref[0, :, cut]
        state, adjoint = state_ref[0, h], adjoint_ref[0, h]
        low = lower[:, cut]
        opened, closed, decays = gates(f_pre, low)
        keys = (1.0 - low) * closed
        final = running[length - 1 :]
        last_factor = jnp.exp(final - running) * tail
        last = (keys * last_factor).astype(BF16)
        scores = (nt(qd, kg) * mask).astype(BF16)
        d_values = tn(scores, g) + nn(last, adjoint)
        d_scores = (nt(g, values) * mask).astype(BF16)
        d_qd = nn(d_scores, kg) + alive * nt(g, state)
        d_kg = tn(d_scores, qd)
        d_last = nt(values, adjoint)
        part_last = d_last * last.astype(F32)
        moved = d_qd * qd.astype(F32) - d_kg * kg.astype(F32) - part_last
        passed = jnp.sum(adjoint.astype(F32) * state.astype(F32), axis=1, keepdims=True)
        passed = jnp.sum(jnp.where(eye, passed, 0.0), axis=0, keepdims=True)
        d_final = jnp.sum(part_last, axis=0, keepdims=True) + passed * jnp.exp(final) * alive_end
        d_log = add_up(later, moved) + d_final
        d_queries = d_qd * jnp.exp(running)
        d_keys = d_kg * jnp.exp(-running) + d_last * last_factor
        common = d_log / decays - d_keys
        s = sigmoid(q_pre)
        d_q_ref[0, :, cut] = (d_queries * (s * (1.0 + q_pre * (1.0 - s)))).astype(BF16)
        d_fv_ref[0, :, cut] = ((1.0 - low) * opened * closed * common).astype(BF16)
        d_fv_ref[0, :, channels + h * HEAD : channels + (h + 1) * HEAD] = d_values.astype(BF16)
        sum_ref[0, :, cut] = jnp.sum(closed * common, axis=0, keepdims=True)
    (w_ref,) = fetch()
    parts = [(0, d_q_ref), (channels, d_fv_ref), (3 * channels, d_o_ref)]
    for a, b in wide_blocks(w_ref.shape[0]):
        value = sum(nt(ref[0], w_ref[a:b, k : k + ref.shape[2]]) for k, ref in parts)
        put_share(step, even_ref, odd_ref, a, b, value)


def share_kernel(step, fetch, piece_refs, left_ref, even_ref, odd_ref):
    (w_ref,) = fetch()
    for a, b in wide_blocks(w_ref.shape[1]):
        put_share(step, even_ref, odd_ref, a, b, nn(left_ref[0], w_ref[:, a:b]))


def over_sequences(kernel, place, chunk, count, ins, outs, held=(), weights=(), pieces=(), flops=0):
    def spec(shape, kind):
        if kind == "scalars":
            return pl.BlockSpec(memory_space=pltpu.SMEM)
        if kind == "whole":
            return pl.BlockSpec(shape, lambda i: (0,) * len(shape), pipeline_mode=pl.Buffered(1))
        if kind == "pair":
            return pl.BlockSpec((1,) + shape[1:], lambda i: (i // 2,) + (0,) * (len(shape) - 1))
        offset = 0 if kind == "part" else chunk * count
        if isinstance(kind, tuple):
            _, width, at = kind
            return pl.BlockSpec((1, shape[1], width), lambda i: (offset + i, 0, at))
        return pl.BlockSpec((1,) + shape[1:], lambda i: (offset + i,) + (0,) * (len(shape) - 1))

    anywhere = pl.BlockSpec(memory_space=pl.ANY)
    arrays, specs = [place], [pl.BlockSpec(memory_space=pltpu.SMEM)]
    for w in weights:
        arrays += w.blocks
        specs += [anywhere] * len(w.blocks)
    for piece in pieces:
        arrays.append(piece)
        specs.append(spec(piece.shape, "whole"))
    arrays += [a for a, _ in ins]
    specs += [spec(a.shape, kind) for a, kind in ins]
    aliases = {}
    for i, array in enumerate(held):
        if array is not None:
            aliases[len(arrays)] = i
            arrays.append(array)
            specs.append(anywhere)

    def body(*refs):
        refs = list(refs)
        place_ref = refs.pop(0)
        block_refs = [[refs.pop(0) for _ in w.blocks] for w in weights]
        piece_refs = [refs.pop(0) for _ in pieces]
        in_refs = [refs.pop(0) for _ in ins]
        del refs[: len(aliases)]
        out_refs = [refs.pop(0) for _ in outs]
        into, sems = refs[: len(weights)], refs[len(weights) :]
        step = pl.program_id(0)

        @pl.when(step == 0)
        def _():
            for w, blocks, ref, sem in zip(weights, block_refs, into, sems):
                w.load(blocks, place_ref, ref, sem)

        def fetch():
            @pl.when(step == 0)
            def _():
                for w, blocks, ref, sem in zip(weights, block_refs, into, sems):
                    for copy in w.copies_of(blocks, place_ref, ref, sem):
                        copy.wait()

            return into

        kernel(step, fetch, piece_refs, *in_refs, *out_refs)

    size = sum(a.size * a.dtype.itemsize for a in arrays)
    return pl.pallas_call(
        body,
        grid=(count,),
        in_specs=specs,
        out_specs=[spec(shape, kind) for shape, _, kind in outs],
        out_shape=[jax.ShapeDtypeStruct(shape, kind) for shape, kind, _ in outs],
        scratch_shapes=[pltpu.VMEM((w.height, w.n), BF16) for w in weights]
        + [pltpu.SemaphoreType.DMA((w.copies,)) for w in weights],
        input_output_aliases=aliases,
        compiler_params=pltpu.CompilerParams(vmem_limit_bytes=VMEM_LIMIT),
        cost_estimate=pl.CostEstimate(flops=flops, bytes_accessed=size // 4, transcendentals=0),
    )(*arrays)


def after(value, *others):
    return lax.optimization_barrier((value,) + others)[0] if others else value


def build(ny, nz):
    def local(block_in, doc_starts, out_grad, w_mix, w_out, w_gu, w_down, attn_gain, ffn_gain, group_gain, lower_logit):
        at = Places(ny, nz)
        micro, length, features = block_in.shape
        rows = w_mix.shape[0]
        own_channels = ny * nz * rows
        heads = own_channels // HEAD
        strip = own_channels // ny
        ff_rows = w_down.shape[0]
        own_ff = ny * nz * ff_rows
        ff_strip = nz * ff_rows
        total = micro * TEAM
        tokens = total * length
        place = jnp.stack([at.rank, at.y, at.z]).astype(jnp.int32)
        team = ("y", "seq")

        def trade(parts, *held):
            return jnp.stack([parts[0]] + [at.swap(after(parts[j], *held), j) for j in range(1, TEAM)])

        def columns_of(matrix, count, width):
            parts = matrix.reshape(rows, count * ny, TEAM, width)
            return [lax.dynamic_index_in_dim(parts, at.rank ^ j, 2, False).reshape(rows, -1) for j in range(TEAM)]

        group_share = jnp.pad(group_gain, (0, rows - group_gain.shape[0]))
        extra = jnp.stack([attn_gain, ffn_gain, lower_logit, group_share], axis=1).astype(BF16)
        extra = jnp.pad(extra, ((0, 0), (0, HEAD - extra.shape[1])))
        mix_width = 4 * own_channels + HEAD
        mix_parts = pl.pallas_call(
            partial(pick_kernel, strip),
            in_specs=[pl.BlockSpec(memory_space=pltpu.SMEM)] + [pl.BlockSpec(memory_space=pltpu.VMEM)] * 2,
            out_specs=[pl.BlockSpec(memory_space=pltpu.VMEM)] * TEAM,
            out_shape=[jax.ShapeDtypeStruct((rows, mix_width), BF16)] * TEAM,
        )(place, w_mix, extra)
        mix_own, out_own = trade(mix_parts), w_out[None]
        starts = doc_starts.astype(BF16)[:, None]
        starts = jnp.concatenate([starts, at.swap(starts, 1)], axis=1)
        starts = jnp.concatenate([starts, at.swap(starts, 2)], axis=1)
        waits = {}
        if (ny, nz) == (2, 4) and micro == 2:
            z1, z2 = (lambda v: at.swap_z(v, 1)), (lambda v: at.swap_z(v, 2))
            cross = lambda v: at.swap_y(v, 1)
            far = lambda v: at.swap(v, 2)
            m1, m2, my = z1(mix_own), z2(mix_own), cross(mix_own)
            oy = cross(after(out_own, mix_own))
            in0 = far(after(block_in[0], mix_own))
            gu_own = trade(columns_of(after(w_gu, mix_own), 2, ff_strip), mix_own)
            done = (m1, m2, my, oy, in0)
            m12, my1, my2 = z1(after(m2, *done)), cross(after(m1, *done)), cross(after(m2, *done))
            o1, o2 = z1(after(out_own, *done)), z2(after(out_own, *done))
            in1 = far(after(block_in[1], *done, gu_own))
            done = (m12, my1, my2, in1, o1, o2)
            my12 = cross(after(m12, *done))
            o12, oy1, oy2 = z1(after(o2, *done)), cross(after(o1, *done)), cross(after(o2, *done))
            g1, g2 = z1(after(gu_own, *done)), z2(after(gu_own, *done))
            gy = cross(after(gu_own, my12))
            cot0 = far(after(out_grad[0], *done))
            oy12 = cross(o12)
            gy1, gy2 = cross(g1), cross(g2)
            cot1 = far(after(out_grad[1], cot0))
            g12 = z1(g2)
            waits["mix", 0] = (o12, g1)
            waits["mix", 1] = (g2, gy, oy1, oy2, oy12)
            waits["hop", 0] = (g12,)
            waits["hop", 1] = (gy1, cot1)
            waits["out", 0] = (gy2,)

            def later(*held):
                found_gu = found(gu_own, g1, g2, g12, gy, gy1, gy2, cross(g12))
                return Weight(at, found_gu), Weight(at, lax.all_gather(after(w_down, *held), team)[:, None])

            def found(own, a1, a2, a12, y, y1, y2, y12):
                near = {(0, 0): own, (0, 1): a1, (0, 2): a2, (0, 3): a12}
                return {**near, (1, 0): y, (1, 1): y1, (1, 2): y2, (1, 3): y12}

            mix = Weight(at, found(mix_own, m1, m2, m12, my, my1, my2, my12))
            out = Weight(at, found(out_own, o1, o2, o12, oy, oy1, oy2, oy12))
            inputs, cotangent = (
                [[own, at.swap(own, 1), far_own, at.swap(far_own, 1)] for own, far_own in zip(here, there)]
                for here, there in ((block_in, (in0, in1)), (out_grad, (cot0, cot1)))
            )
        else:
            gu_own = trade(columns_of(w_gu, 2, ff_strip))
            mix, out = (Weight(at, at.gather_blocks(v)) for v in (mix_own, out_own))

            def later(*held):
                return Weight(at, at.gather_blocks(gu_own)), Weight(at, lax.all_gather(w_down, team)[:, None])

            inputs = [at.team_gather(block_in[c]) for c in range(micro)]
            cotangent = [at.team_gather(out_grad[c]) for c in range(micro)]

        def turn(name, c, *others):
            return after(place, *waits.get((name, c), ()), *others)

        upto = (jnp.arange(length)[:, None] <= jnp.arange(length)[None, :]).astype(BF16)
        counts = jnp.dot(starts.reshape(total, length), upto, preferred_element_type=F32)
        count_row = counts.reshape(total, 1, length)
        count_col = counts.reshape(total, length, 1)

        def pass_on(leaving, fade, sign, *held):
            factor = fade.reshape(TEAM, heads, HEAD)[..., None]
            entering = jnp.zeros(leaving.shape, F32)
            hops = []
            for k in range(nz - 1):
                pair = (k, k + 1) if sign == 1 else (nz - 1 - k, nz - 2 - k)
                moved = (factor * entering + leaving).astype(BF16)
                moved = lax.ppermute(after(moved, *held) if k == 1 else moved, "seq", [pair])
                hops.append(moved)
                entering = entering + moved.astype(F32)
            return entering.astype(BF16), hops

        span, part, pair = (total, length), (TEAM, length), (TEAM // 2, length, features)
        states = (TEAM, heads, HEAD, HEAD)
        wide = 4 * own_channels
        per_matmul = 2 * TEAM * length * features

        normed = proj = running = qd = kg = mixed = gated = None
        normed2 = hidden = first = second = None
        entering, residual, fades, team_normed2 = [], [], [], []
        insides, leavings = [], []
        for c in range(micro):
            rows_c, cols_c = (a[c * TEAM : (c + 1) * TEAM] for a in (count_row, count_col))
            normed, proj, running, qd, kg, inside, leaving, fade, scales, bound = over_sequences(
                partial(mix_kernel, strip), turn("mix", c), c, TEAM,
                [(place, "scalars"), (rows_c, "part"), (cols_c, "part")],
                [
                    (span + (features,), BF16, "all"),
                    (span + (wide,), F32, "all"),
                    (span + (own_channels,), F32, "all"),
                    (span + (own_channels,), BF16, "all"),
                    (span + (own_channels,), BF16, "all"),
                    (part + (own_channels,), F32, "part"),
                    (states, F32, "part"),
                    ((TEAM, 1, own_channels), F32, "part"),
                    ((8, features), F32, "whole"),
                    ((1, own_channels), F32, "whole"),
                ],
                [normed, proj, running, qd, kg], [mix], inputs[c], per_matmul * wide,
            )
            if c == 0:
                attn_scale, ffn_scale = scales[0:1], scales[1:2]
                group_scale = scales[3].reshape(-1, rows)[:, : group_gain.shape[0]].reshape(1, HEAD)
            fades.append(fade)
            insides.append(inside)
            leavings.append(leaving)
            entering.append(pass_on(leaving, fade, 1, *waits.get(("hop", c), ()))[0])
        gu, down = later(*entering)
        for c in range(micro):
            cols_c = count_col[c * TEAM : (c + 1) * TEAM]
            mixed, gated, even, odd = over_sequences(
                out_kernel, turn("out", c, *leavings), c, TEAM,
                [
                    (insides[c], "part"), (qd, "all"), (proj, ("all", own_channels, 3)), (entering[c], "part"), (cols_c, "part"),
                    (group_scale, "whole"),
                ],
                [
                    (span + (own_channels,), F32, "all"), (span + (own_channels,), BF16, "all"),
                    (pair, BF16, "pair"), (pair, BF16, "pair"),
                ],
                [mixed, gated], [out], (), per_matmul * own_channels,
            )
            residual.append(block_in[c].astype(F32) + at.team_sum(even[None], odd[None], ())[0][0])
            rms_two = lax.rsqrt(jnp.mean(residual[c] * residual[c], axis=-1, keepdims=True) + EPSILON)
            team_normed2.append(at.team_gather((residual[c] * rms_two * ffn_scale).astype(BF16)))

        def flat(a):
            return a.reshape(tokens, a.shape[-1])

        def team_share(left, right, s):
            product = tn(left, right).astype(BF16).reshape(ny, s, nz, -1, right.shape[1])
            product = jnp.swapaxes(product, 1, 2).reshape(ny * nz, -1, right.shape[1])
            return lax.psum_scatter(product, team, scatter_dimension=0, tiled=False).reshape(s, -1, right.shape[1]), product

        def weight_half(left, right, k):
            size = left.shape[1] // ny
            if ny == 2:
                y = 1 - at.y if k == 0 else at.y
                return tn(lax.dynamic_slice_in_dim(left, y * size, size, 1), right).astype(BF16)
            return tn(left, right).astype(BF16).reshape(ny, size, right.shape[1])

        def weight_halves(left, right):
            return [weight_half(left, right, k) for k in range(2 if ny == 2 else 1)]

        def weight_sum(parts, s, held=(), first_held=()):
            width = parts[0].shape[-1]
            if ny == 2:
                send, keep = parts
                terms = [keep, after(at.swap_y(after(send, *first_held), 1), *held)]
            else:
                terms = parts
                for step in [1 << i for i in reversed(range(ny.bit_length() - 1))]:
                    halves = [t.reshape((t.shape[0] // 2 // step, 2, step) + t.shape[1:])[0] for t in terms]
                    bit = (at.y // step) % 2
                    pick = lambda k: [lax.dynamic_index_in_dim(t, k, 0, False) for t in halves]
                    send = sum(t.astype(F32) for t in pick(1 - bit)).astype(BF16)
                    terms = pick(bit) + [at.swap_y(send, step)]
                terms = [t[0] for t in terms]
            terms = [t.reshape(s, nz, -1, width) for t in terms]
            count = nz
            for i in range(nz.bit_length() - 1):
                count //= 2
                halves = [t.reshape((s, count, 2) + t.shape[2:]) for t in terms]
                bit = (at.z // (1 << i)) % 2
                pick = lambda k: [lax.dynamic_index_in_dim(t, k, 2, False) for t in halves]
                send = sum(t.astype(F32) for t in pick(1 - bit)).astype(BF16)
                terms = pick(bit) + [at.swap_z(send, 1 << i)]
            return (lambda i: sum(lax.dynamic_index_in_dim(t[:, 0], i, 0, False).astype(F32) for t in terms)), send

        def out_of_team(summed, count, *held):
            got = at.by_rank(trade([summed(at.rank ^ j).astype(BF16) for j in range(TEAM)], *held)).astype(F32)
            width = got.shape[2] // (count * ny)
            got = got.reshape(TEAM, rows, count, ny, width)
            return jnp.transpose(got, (1, 2, 3, 0, 4)).reshape(rows, -1)

        both = whole_branch = None
        all_cot = jnp.concatenate([jnp.stack(pieces) for pieces in cotangent])
        for c in range(micro):
            normed2, hidden, first, second = over_sequences(
                up_kernel, turn("up", c), c, TEAM,
                [],
                [(span + (features,), BF16, "all")] + [(span + (own_ff,), BF16, "all")] * 3,
                [normed2, hidden, first, second], [gu], team_normed2[c], per_matmul * 2 * own_ff,
            )
        d_residual, d_branch, branch_own, gain_sums, sents = [], [], [], [], []
        held, branch_sum = (), ()
        for c in range(micro):
            both, even, odd = over_sequences(
                down_back_kernel, turn("down_back", c, *held), c, TEAM,
                [(all_cot, "all"), (first, "all"), (second, "all")],
                [(span + (2 * own_ff,), BF16, "all"), (pair, BF16, "pair"), (pair, BF16, "pair")],
                [both], [down, gu], (), per_matmul * 3 * own_ff,
            )
            if c == 0:
                grad_down, down_product = team_share(after(flat(hidden), even), flat(all_cot), 1)
                grad_down = grad_down[0].astype(F32)
            d_normed2, sent = at.team_sum(even[None], odd[None], branch_sum, *((down_product,) if c == 0 else branch_own))
            held = (down_product, sent)
            d_normed2 = d_normed2[0]
            branch_sum = (d_normed2,)
            sents.append(sent)
            res = residual[c]
            rms_two = lax.rsqrt(jnp.mean(res * res, axis=-1, keepdims=True) + EPSILON)
            gain_sums.append(jnp.sum(d_normed2 * res * rms_two, axis=0))
            scaled = d_normed2 * ffn_scale
            d_residual.append(
                out_grad[c].astype(F32)
                + rms_two * (scaled - res * rms_two * rms_two * jnp.mean(scaled * res, axis=-1, keepdims=True))
            )
            branch_own.append(d_residual[c].astype(BF16))
            d_branch.append(at.team_gather(branch_own[c]))

        d_q = d_fv = d_o = None
        gs, group_sums, logit_sums, adjoints = [], [], [], []

        def enter_back(c, whole_branch, d_o, *held):
            cols_c = count_col[c * TEAM : (c + 1) * TEAM]
            whole_branch, d_o, g, toward, group_sum = over_sequences(
                out_back_kernel, turn("out_back", c, *held), c, TEAM,
                [
                    (mixed, "all"), (proj, ("all", own_channels, 3)), (qd, "all"), (cols_c, "part"), (group_scale, "whole"),
                ],
                [
                    (span + (features,), BF16, "all"), (span + (own_channels,), BF16, "all"),
                    (part + (own_channels,), BF16, "part"), (states, F32, "part"), ((TEAM, 1, own_channels), F32, "part"),
                ],
                [whole_branch, d_o], [out], d_branch[c], per_matmul * own_channels,
            )
            gs.append(g)
            group_sums.append(group_sum)
            adjoint, hops = pass_on(toward, fades[c], -1)
            adjoints.append(adjoint)
            return whole_branch, d_o, toward, hops

        toward = place
        gu_send = weight_half(after(flat(normed2), branch_own[0]), flat(both), 0)
        hops = []
        for c in range(micro - 1):
            whole_branch, d_o, toward, hops = enter_back(c, whole_branch, d_o, gu_send, sents[c + 1])
        gu_halves = [gu_send] + ([weight_half(after(flat(normed2), toward), flat(both), 1)] if ny == 2 else [])
        even, odd = over_sequences(
            share_kernel, after(place, gu_halves[-1], branch_own[-1], *hops[:1]), 0, total, [(hidden, "part")],
            [((micro * TEAM // 2, length, features), BF16, "pair")] * 2, (), [down], (), 2 * tokens * own_ff * features,
        )
        whole_branch, d_o, toward, last_hops = enter_back(micro - 1, whole_branch, d_o, even, *hops[1:2])
        paired = (micro, TEAM // 2, length, features)
        ffn_near = after(at.swap(odd, 1), toward).reshape(paired)
        even = even.reshape(paired)
        ffn_sent = [(even[c, 1].astype(F32) + ffn_near[c, 1].astype(F32)).astype(BF16) for c in range(micro)]
        block_out = [
            (residual[c] + (even[c, 0].astype(F32) + ffn_near[c, 0].astype(F32) + at.swap(ffn_sent[c], 2).astype(F32))).astype(BF16)
            for c in range(micro)
        ]
        out_halves = weight_halves(flat(gated), flat(whole_branch))
        mix_halves = {"o": weight_halves(after(flat(normed), *last_hops[:1]), flat(d_o))}
        gu_sum, gu_sent = weight_sum(gu_halves, TEAM, adjoints)

        d_normed, dn_sent = [], []
        for c in range(micro):
            rows_c, cols_c = (a[c * TEAM : (c + 1) * TEAM] for a in (count_row, count_col))
            held = (*ffn_sent, *last_hops[1:2], *out_halves, *mix_halves["o"]) if c == 0 else (gu_sent, block_out[0])
            d_q, d_fv, logit_sum, even, odd = over_sequences(
                mix_back_kernel, turn("mix_back", c, *held), c, TEAM,
                [
                    (proj, ("all", own_channels, 0)), (proj, ("all", own_channels, 1)), (proj, ("all", own_channels, 2)),
                    (running, "all"), (qd, "all"), (kg, "all"), (gs[c], "part"), (entering[c], "part"), (adjoints[c], "part"),
                    (bound, "whole"), (rows_c, "part"), (cols_c, "part"), (d_o, "all"),
                ],
                [
                    (span + (own_channels,), BF16, "all"), (span + (2 * own_channels,), BF16, "all"),
                    ((TEAM, 1, own_channels), F32, "part"), (pair, BF16, "pair"), (pair, BF16, "pair"),
                ],
                [d_q, d_fv], [mix], (), per_matmul * wide,
            )
            logit_sums.append(logit_sum)
            summed, sent = at.team_sum(even[None], odd[None], ())
            d_normed.append(summed[0])
            dn_sent.append(sent)
        last, d_q = d_fv, after(d_q, d_fv)
        fv_sum, fv_product = team_share(flat(normed), flat(d_fv), TEAM)
        mix_halves["q"] = [weight_half(after(flat(normed), fv_product), flat(d_q), 0)]
        if ny == 2:
            q_left = after(flat(normed), *dn_sent, *mix_halves["q"])
            mix_halves["q"].append(weight_half(q_left, flat(d_q), 1))
        d_normed, block_out = jnp.stack(d_normed), jnp.stack(block_out)
        x = block_in.astype(F32)
        rms_one = lax.rsqrt(jnp.mean(x * x, axis=-1, keepdims=True) + EPSILON)
        attn_sum = jnp.sum(d_normed * x * rms_one, axis=(0, 1))
        scaled = d_normed * attn_scale
        in_grad = jnp.stack(d_residual) + rms_one * (
            scaled - x * rms_one * rms_one * jnp.mean(scaled * x, axis=-1, keepdims=True)
        )

        logit_sum = bound[0] * (1.0 - bound[0]) * sum(jnp.sum(a, axis=(0, 1)) for a in logit_sums)
        logit_all = jnp.where(
            jnp.arange(TEAM)[None, :, None] == at.rank, logit_sum.reshape(ny, 1, strip), 0.0
        ).reshape(features)
        group_all = jnp.sum(sum(jnp.sum(a, axis=(0, 1)) for a in group_sums).reshape(heads, HEAD), axis=0)
        sums = at.everyone_sum(jnp.concatenate([attn_sum, sum(gain_sums), logit_all, group_all]))

        grad_gu = out_of_team(gu_sum, 2)
        grad_out = weight_sum(out_halves, 1, (last,), adjoints)[0](0)
        grads = [
            out_of_team(weight_sum(mix_halves[name], TEAM, (last, fv_product), adjoints)[0], 1) for name in ("q", "o")
        ]
        grad_fv = out_of_team(
            lambda i: lax.dynamic_index_in_dim(fv_sum, i, 0, False), 2, sums, grad_gu, grad_out, *grads
        )
        grad_mix = jnp.concatenate([grads[0], grad_fv, grads[1]], axis=1)
        here = (at.y * TEAM + at.rank) * nz + at.z

        def mine(start, size):
            return lax.dynamic_slice_in_dim(sums, start + here * size, size)

        return (
            block_out,
            in_grad,
            grad_mix,
            grad_out,
            grad_gu,
            grad_down,
            mine(0, rows),
            mine(features, rows),
            mine(3 * features, group_gain.shape[0]),
            mine(2 * features, rows),
        )

    return local


def solution(mesh):
    devices = mesh.devices.reshape(-1, TEAM, mesh.shape["seq"])
    tokens = P(("y", "team"), "seq", None)
    matrix = P(("y", "team", "seq"), None)
    vector = P(("y", "team", "seq"))
    return jax.shard_map(
        build(devices.shape[0], devices.shape[2]),
        mesh=Mesh(devices, ("y", "team", "seq")),
        in_specs=(tokens, P(("y", "team"), "seq"), tokens) + (matrix,) * 4 + (vector,) * 4,
        out_specs=(tokens, tokens) + (matrix,) * 4 + (vector,) * 4,
        check_vma=False,
    )
```

```python
from functools import partial

import jax
import jax.numpy as jnp
from jax import lax
from jax.experimental import pallas as pl
from jax.experimental.pallas import tpu as pltpu
from jax.sharding import Mesh, PartitionSpec as P

HEAD = 128
TEAM = 4
EPSILON = 1e-06
SCALE = HEAD**-0.5
F32 = jnp.float32
BF16 = jnp.bfloat16
VMEM_LIMIT = 60 * 1024 * 1024


class Places:
    def __init__(self, ny, nz):
        self.ny, self.nz = ny, nz
        self.rank, self.y, self.z = lax.axis_index("team"), lax.axis_index("y"), lax.axis_index("seq")

    def swap(self, value, bits):
        return lax.ppermute(value, "team", [(i, i ^ bits) for i in range(TEAM)])

    def swap_y(self, value, bits):
        return lax.ppermute(value, "y", [(i, i ^ bits) for i in range(self.ny)])

    def swap_z(self, value, bits):
        return lax.ppermute(value, "seq", [(i, i ^ bits) for i in range(self.nz)])

    def by_rank(self, stack):
        odd, high = (self.rank & 1) == 1, (self.rank & 2) == 2
        stack = jnp.where(odd, jnp.concatenate([stack[1:2], stack[0:1], stack[3:4], stack[2:3]]), stack)
        return jnp.where(high, jnp.concatenate([stack[2:], stack[:2]]), stack)

    def team_gather(self, own, *held):
        one, two = self.swap(own, 1), self.swap(own, 2)
        return [own, one, two, self.swap(after(two, *held), 1)]

    def team_sum(self, even, odd, first_held, *held):
        near = self.swap(after(odd, *first_held), 1)
        sent = (even[:, 1].astype(F32) + after(near, *held)[:, 1].astype(F32)).astype(BF16)
        far = self.swap(sent, 2)
        return lambda *held: even[:, 0].astype(F32) + near[:, 0].astype(F32) + after(far, *held).astype(F32), sent, far


    def gather_blocks(self, own):
        found = {(0, 0): own}
        for step in [1 << i for i in reversed(range(self.nz.bit_length() - 1))]:
            found.update({(0, dz ^ step): self.swap_z(v, step) for (_, dz), v in list(found.items())})
        for step in [1 << i for i in range(self.ny.bit_length() - 1)]:
            found.update({(dy ^ step, dz): self.swap_y(v, step) for (dy, dz), v in list(found.items())})
        return found

    def everyone_sum(self, value):
        for step in (2, 1):
            value = value + self.swap(value, step)
        for step in [1 << i for i in reversed(range(self.ny.bit_length() - 1))]:
            value = value + self.swap_y(value, step)
        for step in [1 << i for i in reversed(range(self.nz.bit_length() - 1))]:
            value = value + self.swap_z(value, step)
        return value


class Weight:
    def __init__(self, at, found):
        self.ny, self.nz = at.ny, at.nz
        if isinstance(found, dict):
            self.s, self.rows, self.n = found[0, 0].shape
            self.keys, self.blocks = list(found), list(found.values())
        else:
            self.s, self.rows, self.n = found.shape[1:]
            self.keys, self.blocks = None, [found]
        self.height = self.ny * self.nz * self.s * self.rows
        self.split = self.rows % 16 == 0
        if not self.split:
            if self.keys:
                found = jnp.zeros((self.ny, self.nz) + self.blocks[0].shape, BF16)
                for (dy, dz), block in zip(self.keys, self.blocks):
                    found = lax.dynamic_update_slice(found, block[None, None], (at.y ^ dy, at.z ^ dz, 0, 0, 0))
            found = found.reshape(self.ny, self.nz, self.s, self.rows, self.n)
            self.blocks = [jnp.swapaxes(found, 1, 2).reshape(self.height, self.n)]

    @property
    def copies(self):
        return self.ny * self.nz * self.s if self.split else 1

    def load(self, refs, place_ref, into, sems):
        for copy in self.copies_of(refs, place_ref, into, sems):
            copy.start()

    def copies_of(self, refs, place_ref, into, sems):
        if not self.split:
            return [pltpu.make_async_copy(refs[0], into, sems.at[0])]
        rank, y, z = place_ref[0], place_ref[1], place_ref[2]
        if self.keys:
            blocks = [(y ^ dy, z ^ dz, ref) for (dy, dz), ref in zip(self.keys, refs)]
        else:
            blocks = [(i // self.nz, i % self.nz, refs[0].at[i]) for i in range(self.ny * self.nz)]
        copies = []
        for there_y, there_z, ref in blocks:
            for j in range(self.s):
                s = rank ^ j if self.s > 1 else 0
                row = ((there_y * self.s + s) * self.nz + there_z) * self.rows
                if not isinstance(row, int):
                    row = pl.multiple_of(row, self.rows)
                copies.append(pltpu.make_async_copy(ref.at[j], into.at[pl.ds(row, self.rows)], sems.at[len(copies)]))
        return copies


def nn(a, b):
    return jnp.dot(a, b, preferred_element_type=F32)


def nt(a, b):
    return lax.dot_general(a, b, (((1,), (1,)), ((), ())), preferred_element_type=F32)


def tn(a, b):
    return lax.dot_general(a, b, (((0,), (0,)), ((), ())), preferred_element_type=F32)


def add_up(matrix, value):
    high = value.astype(BF16)
    rest = value - high.astype(F32)
    mid = rest.astype(BF16)
    low = (rest - mid.astype(F32)).astype(BF16)
    return nn(matrix, high) + nn(matrix, mid) + nn(matrix, low)


def triangle(n, lower):
    row = lax.broadcasted_iota(jnp.int32, (n, n), 0)
    col = lax.broadcasted_iota(jnp.int32, (n, n), 1)
    return row >= col if lower else row <= col


def sigmoid(z):
    return 1.0 / (1.0 + jnp.exp(-z))


def gates(f_pre, lower):
    small = jnp.exp(-jnp.abs(f_pre))
    big_part = 1.0 / (1.0 + small)
    small_part = small * big_part
    positive = f_pre >= 0
    opened = jnp.where(positive, big_part, small_part)
    closed = jnp.where(positive, small_part, big_part)
    return opened, closed, lower + (1.0 - lower) * opened


def wide_blocks(width):
    step = 512
    return [(a, min(a + step, width)) for a in range(0, width, step)]


def take_piece(step, piece_refs, into_ref):
    for j, ref in enumerate(piece_refs):

        @pl.when(step == j)
        def _(ref=ref):
            into_ref[0] = ref[...]


def put_share(step, even_ref, odd_ref, a, b, value):
    value = value.astype(BF16)

    @pl.when(step % 2 == 0)
    def _():
        even_ref[0, :, a:b] = value

    @pl.when(step % 2 == 1)
    def _():
        odd_ref[0, :, a:b] = value


def pick_kernel(strip, place_ref, w_ref, extra_ref, *out_refs):
    rank = place_ref[0]
    count = w_ref.shape[1] // (TEAM * strip)
    for j, out_ref in enumerate(out_refs):
        for k in range(count):
            at = pl.multiple_of((k * TEAM + (rank ^ j)) * strip, strip)
            out_ref[:, k * strip : (k + 1) * strip] = w_ref[:, pl.ds(at, strip)]
        out_ref[:, count * strip :] = extra_ref[...]


def place_kernel(strip, place_ref, *refs):
    out_ref = refs[-1]
    for j, ref in enumerate(refs[:-1]):
        for k in range(ref.shape[1] // strip):
            at = pl.multiple_of((k * TEAM + (place_ref[0] ^ j)) * strip, strip)
            out_ref[:, pl.ds(at, strip)] = ref[:, k * strip : (k + 1) * strip].astype(F32)


def mix_kernel(strip, step, fetch, piece_refs, place_ref, row_ref, col_ref, *refs):
    normed_ref, proj_ref, run_ref, qd_ref, kg_ref, ins_ref, leave_ref, fade_ref, scales_ref, lower_ref = refs
    channels = lower_ref.shape[1]
    (w_ref,) = fetch()

    @pl.when(step == 0)
    def _():
        row = lax.broadcasted_iota(jnp.int32, (8, HEAD), 0)
        col = lax.broadcasted_iota(jnp.int32, (8, HEAD), 1)
        pick = jnp.where(row == col, 1.0, 0.0).astype(BF16)
        scales_ref[...] = nt(pick, w_ref[:, 4 * channels :])
        for k in range(channels // strip):
            at = pl.multiple_of((k * TEAM + place_ref[0]) * strip, strip)
            lower_ref[:, k * strip : (k + 1) * strip] = sigmoid(scales_ref[2:3, pl.ds(at, strip)])

    gain = scales_ref[0:1]
    take_piece(step, piece_refs, normed_ref)
    x = normed_ref[0].astype(F32)
    scale = lax.rsqrt(jnp.mean(x * x, axis=-1, keepdims=True) + EPSILON)
    normed_ref[0] = (x * scale * gain).astype(BF16)
    for a, b in wide_blocks(4 * channels):
        proj_ref[0, :, a:b] = nn(normed_ref[0], w_ref[:, a:b])
    lower = lower_ref[...]
    q_pre = proj_ref[0, :, 0:channels]
    f_pre = proj_ref[0, :, channels : 2 * channels]
    _, closed, decays = gates(f_pre, lower)
    keys = (1.0 - lower) * closed
    length = x.shape[0]
    causal = triangle(length, True)
    running = add_up(causal.astype(BF16), jnp.log(decays))
    run_ref[0] = running
    row, col = row_ref[0], col_ref[0]
    alive = (col[length - 1 :] == 0).astype(F32)
    tail = (col == col[length - 1 :]).astype(F32)
    final = running[length - 1 :]
    fade_ref[0] = jnp.exp(final) * alive
    qd_ref[0] = (q_pre * sigmoid(q_pre) * jnp.exp(running)).astype(BF16)
    kg_ref[0] = (keys * jnp.exp(-running)).astype(BF16)
    last = (keys * jnp.exp(final - running) * tail).astype(BF16)
    mask = jnp.where(causal & (col == row), 1.0, 0.0)
    for h in range(channels // HEAD):
        cut = slice(h * HEAD, (h + 1) * HEAD)
        values = proj_ref[0, :, 2 * channels + h * HEAD : 2 * channels + (h + 1) * HEAD].astype(BF16)
        scores = (nt(qd_ref[0, :, cut], kg_ref[0, :, cut]) * mask).astype(BF16)
        ins_ref[0, :, cut] = nn(scores, values) * SCALE
        leave_ref[0, h] = tn(last[:, cut], values)


def out_kernel(step, fetch, piece_refs, ins_ref, qd_ref, o_ref, state_ref, col_ref, group_ref, *refs):
    mixed_ref, gated_ref, even_ref, odd_ref = refs
    channels = ins_ref.shape[2]
    alive = (col_ref[0] == 0).astype(F32) * SCALE
    for h in range(channels // HEAD):
        cut = slice(h * HEAD, (h + 1) * HEAD)
        mixed = ins_ref[0, :, cut] + alive * nn(qd_ref[0, :, cut], state_ref[0, h])
        mixed_ref[0, :, cut] = mixed
        scale = lax.rsqrt(jnp.mean(mixed * mixed, axis=-1, keepdims=True) + EPSILON)
        o_pre = o_ref[0, :, cut]
        gated_ref[0, :, cut] = (mixed * scale * group_ref[...] * (o_pre * sigmoid(o_pre))).astype(BF16)
    (w_ref,) = fetch()
    for a, b in wide_blocks(w_ref.shape[1]):
        put_share(step, even_ref, odd_ref, a, b, nn(gated_ref[0], w_ref[:, a:b]))


def up_kernel(step, fetch, piece_refs, normed_ref, hidden_ref, first_ref, second_ref):
    width = hidden_ref.shape[2]
    take_piece(step, piece_refs, normed_ref)
    (w_ref,) = fetch()
    for a, b in wide_blocks(width):
        gate = nn(normed_ref[0], w_ref[:, a:b])
        up = nn(normed_ref[0], w_ref[:, width + a : width + b])
        s = sigmoid(gate)
        silu = gate * s
        hidden_ref[0, :, a:b] = (silu * up).astype(BF16)
        first_ref[0, :, a:b] = (up * (s * (1.0 + gate * (1.0 - s)))).astype(BF16)
        second_ref[0, :, a:b] = silu.astype(BF16)


def down_back_kernel(step, fetch, piece_refs, cot_ref, first_ref, second_ref, both_ref, even_ref, odd_ref):
    width = first_ref.shape[2]
    down_ref, w_ref = fetch()
    for a, b in wide_blocks(width):
        d_hidden = nt(cot_ref[0], down_ref[a:b, :])
        both_ref[0, :, a:b] = (d_hidden * first_ref[0, :, a:b].astype(F32)).astype(BF16)
        both_ref[0, :, width + a : width + b] = (d_hidden * second_ref[0, :, a:b].astype(F32)).astype(BF16)
    for a, b in wide_blocks(w_ref.shape[0]):
        put_share(step, even_ref, odd_ref, a, b, nt(both_ref[0], w_ref[a:b, :]))


def out_back_kernel(step, fetch, piece_refs, mixed_ref, o_ref, qd_ref, col_ref, group_ref, *refs):
    branch_ref, d_o_ref, g_ref, toward_ref, sum_ref = refs
    channels = mixed_ref.shape[2]
    take_piece(step, piece_refs, branch_ref)
    alive = (col_ref[0] == 0).astype(F32)
    group = group_ref[...]
    (w_ref,) = fetch()
    d_gated_all = nt(branch_ref[0], w_ref[...])
    for h in range(channels // HEAD):
        cut = slice(h * HEAD, (h + 1) * HEAD)
        d_gated = d_gated_all[:, cut]
        mixed = mixed_ref[0, :, cut]
        scale = lax.rsqrt(jnp.mean(mixed * mixed, axis=-1, keepdims=True) + EPSILON)
        unit = mixed * scale
        o_pre = o_ref[0, :, cut]
        s = sigmoid(o_pre)
        silu = o_pre * s
        both = d_gated * unit
        d_o_ref[0, :, cut] = (both * group * (s * (1.0 + o_pre * (1.0 - s)))).astype(BF16)
        sum_ref[0, :, cut] = jnp.sum(both * silu, axis=0, keepdims=True)
        d_unit = d_gated * group * silu
        d_mixed = scale * (d_unit - unit * jnp.mean(d_unit * unit, axis=-1, keepdims=True))
        g = (d_mixed * SCALE).astype(BF16)
        g_ref[0, :, cut] = g
        reach = (qd_ref[0, :, cut].astype(F32) * alive).astype(BF16)
        toward_ref[0, h] = tn(reach, g)


def mix_back_kernel(
    step, fetch, piece_refs, q_ref, f_ref, v_ref, run_ref, qd_ref, kg_ref, g_ref, state_ref, adjoint_ref, lower_ref,
    row_ref, col_ref, d_o_ref, d_q_ref, d_fv_ref, sum_ref, even_ref, odd_ref,
):
    channels = lower_ref.shape[1]
    length = row_ref.shape[2]
    lower = lower_ref[...]
    row, col = row_ref[0], col_ref[0]
    alive = (col == 0).astype(F32)
    alive_end = alive[length - 1 :]
    tail = (col == col[length - 1 :]).astype(F32)
    mask = jnp.where(triangle(length, True) & (col == row), 1.0, 0.0)
    later = triangle(length, False).astype(BF16)
    eye = lax.broadcasted_iota(jnp.int32, (HEAD, HEAD), 0) == lax.broadcasted_iota(jnp.int32, (HEAD, HEAD), 1)
    for h in range(channels // HEAD):
        cut = slice(h * HEAD, (h + 1) * HEAD)
        q_pre, f_pre = q_ref[0, :, cut], f_ref[0, :, cut]
        values = v_ref[0, :, cut].astype(BF16)
        running = run_ref[0, :, cut]
        qd, kg, g = qd_ref[0, :, cut], kg_ref[0, :, cut], g_ref[0, :, cut]
        state, adjoint = state_ref[0, h], adjoint_ref[0, h]
        low = lower[:, cut]
        opened, closed, decays = gates(f_pre, low)
        keys = (1.0 - low) * closed
        final = running[length - 1 :]
        last_factor = jnp.exp(final - running) * tail
        last = (keys * last_factor).astype(BF16)
        scores = (nt(qd, kg) * mask).astype(BF16)
        d_values = tn(scores, g) + nn(last, adjoint)
        d_scores = (nt(g, values) * mask).astype(BF16)
        d_qd = nn(d_scores, kg) + alive * nt(g, state)
        d_kg = tn(d_scores, qd)
        d_last = nt(values, adjoint)
        part_last = d_last * last.astype(F32)
        moved = d_qd * qd.astype(F32) - d_kg * kg.astype(F32) - part_last
        passed = jnp.sum(adjoint.astype(F32) * state.astype(F32), axis=1, keepdims=True)
        passed = jnp.sum(jnp.where(eye, passed, 0.0), axis=0, keepdims=True)
        d_final = jnp.sum(part_last, axis=0, keepdims=True) + passed * jnp.exp(final) * alive_end
        d_log = add_up(later, moved) + d_final
        d_queries = d_qd * jnp.exp(running)
        d_keys = d_kg * jnp.exp(-running) + d_last * last_factor
        common = d_log / decays - d_keys
        s = sigmoid(q_pre)
        d_q_ref[0, :, cut] = (d_queries * (s * (1.0 + q_pre * (1.0 - s)))).astype(BF16)
        d_fv_ref[0, :, cut] = ((1.0 - low) * opened * closed * common).astype(BF16)
        d_fv_ref[0, :, channels + h * HEAD : channels + (h + 1) * HEAD] = d_values.astype(BF16)
        sum_ref[0, :, cut] = jnp.sum(closed * common, axis=0, keepdims=True)
    (w_ref,) = fetch()
    parts = [(0, d_q_ref), (channels, d_fv_ref), (3 * channels, d_o_ref)]
    for a, b in wide_blocks(w_ref.shape[0]):
        value = sum(nt(ref[0], w_ref[a:b, k : k + ref.shape[2]]) for k, ref in parts)
        put_share(step, even_ref, odd_ref, a, b, value)


def share_kernel(step, fetch, piece_refs, left_ref, even_ref, odd_ref):
    (w_ref,) = fetch()
    for a, b in wide_blocks(w_ref.shape[1]):
        put_share(step, even_ref, odd_ref, a, b, nn(left_ref[0], w_ref[:, a:b]))


def over_sequences(kernel, place, chunk, count, ins, outs, held=(), weights=(), pieces=(), flops=0):
    def spec(shape, kind):
        if kind == "scalars":
            return pl.BlockSpec(memory_space=pltpu.SMEM)
        if kind == "whole":
            return pl.BlockSpec(shape, lambda i: (0,) * len(shape), pipeline_mode=pl.Buffered(1))
        if kind == "pair":
            return pl.BlockSpec((1,) + shape[1:], lambda i: (i // 2,) + (0,) * (len(shape) - 1))
        offset = 0 if kind == "part" else chunk * count
        if isinstance(kind, tuple):
            _, width, at = kind
            return pl.BlockSpec((1, shape[1], width), lambda i: (offset + i, 0, at))
        return pl.BlockSpec((1,) + shape[1:], lambda i: (offset + i,) + (0,) * (len(shape) - 1))

    anywhere = pl.BlockSpec(memory_space=pl.ANY)
    arrays, specs = [place], [pl.BlockSpec(memory_space=pltpu.SMEM)]
    for w in weights:
        arrays += w.blocks
        specs += [anywhere] * len(w.blocks)
    for piece in pieces:
        arrays.append(piece)
        specs.append(spec(piece.shape, "whole"))
    arrays += [a for a, _ in ins]
    specs += [spec(a.shape, kind) for a, kind in ins]
    aliases = {}
    for i, array in enumerate(held):
        if array is not None:
            aliases[len(arrays)] = i
            arrays.append(array)
            specs.append(anywhere)

    def body(*refs):
        refs = list(refs)
        place_ref = refs.pop(0)
        block_refs = [[refs.pop(0) for _ in w.blocks] for w in weights]
        piece_refs = [refs.pop(0) for _ in pieces]
        in_refs = [refs.pop(0) for _ in ins]
        del refs[: len(aliases)]
        out_refs = [refs.pop(0) for _ in outs]
        into, sems = refs[: len(weights)], refs[len(weights) :]
        step = pl.program_id(0)

        @pl.when(step == 0)
        def _():
            for w, blocks, ref, sem in zip(weights, block_refs, into, sems):
                w.load(blocks, place_ref, ref, sem)

        def fetch():
            @pl.when(step == 0)
            def _():
                for w, blocks, ref, sem in zip(weights, block_refs, into, sems):
                    for copy in w.copies_of(blocks, place_ref, ref, sem):
                        copy.wait()

            return into

        kernel(step, fetch, piece_refs, *in_refs, *out_refs)

    size = sum(a.size * a.dtype.itemsize for a in arrays)
    return pl.pallas_call(
        body,
        grid=(count,),
        in_specs=specs,
        out_specs=[spec(shape, kind) for shape, _, kind in outs],
        out_shape=[jax.ShapeDtypeStruct(shape, kind) for shape, kind, _ in outs],
        scratch_shapes=[pltpu.VMEM((w.height, w.n), BF16) for w in weights]
        + [pltpu.SemaphoreType.DMA((w.copies,)) for w in weights],
        input_output_aliases=aliases,
        compiler_params=pltpu.CompilerParams(vmem_limit_bytes=VMEM_LIMIT),
        cost_estimate=pl.CostEstimate(flops=flops, bytes_accessed=size // 4, transcendentals=0),
    )(*arrays)


def after(value, *others):
    return lax.optimization_barrier((value,) + others)[0] if others else value


def build(ny, nz):
    def local(block_in, doc_starts, out_grad, w_mix, w_out, w_gu, w_down, attn_gain, ffn_gain, group_gain, lower_logit):
        at = Places(ny, nz)
        micro, length, features = block_in.shape
        rows = w_mix.shape[0]
        own_channels = ny * nz * rows
        heads = own_channels // HEAD
        strip = own_channels // ny
        ff_rows = w_down.shape[0]
        own_ff = ny * nz * ff_rows
        ff_strip = nz * ff_rows
        total = micro * TEAM
        tokens = total * length
        place = jnp.stack([at.rank, at.y, at.z]).astype(jnp.int32)
        team = ("y", "seq")

        def trade(parts, *held):
            return jnp.stack([parts[0]] + [at.swap(after(parts[j], *held), j) for j in range(1, TEAM)])

        def columns_of(matrix, count, width):
            parts = matrix.reshape(rows, count * ny, TEAM, width)
            return [lax.dynamic_index_in_dim(parts, at.rank ^ j, 2, False).reshape(rows, -1) for j in range(TEAM)]

        group_share = jnp.pad(group_gain, (0, rows - group_gain.shape[0]))
        extra = jnp.stack([attn_gain, ffn_gain, lower_logit, group_share], axis=1).astype(BF16)
        extra = jnp.pad(extra, ((0, 0), (0, HEAD - extra.shape[1])))
        mix_width = 4 * own_channels + HEAD
        mix_parts = pl.pallas_call(
            partial(pick_kernel, strip),
            in_specs=[pl.BlockSpec(memory_space=pltpu.SMEM)] + [pl.BlockSpec(memory_space=pltpu.VMEM)] * 2,
            out_specs=[pl.BlockSpec(memory_space=pltpu.VMEM)] * TEAM,
            out_shape=[jax.ShapeDtypeStruct((rows, mix_width), BF16)] * TEAM,
        )(place, w_mix, extra)
        mix_own, out_own = trade(mix_parts), w_out[None]
        starts = doc_starts.astype(BF16)[:, None]
        starts = jnp.concatenate([starts, at.swap(starts, 1)], axis=1)
        starts = jnp.concatenate([starts, at.swap(starts, 2)], axis=1)
        waits = {}
        if (ny, nz) == (2, 4) and micro == 2:
            z1, z2 = (lambda v: at.swap_z(v, 1)), (lambda v: at.swap_z(v, 2))
            cross = lambda v: at.swap_y(v, 1)
            far = lambda v: at.swap(v, 2)
            m1, m2, my = z1(mix_own), z2(mix_own), cross(mix_own)
            oy = cross(after(out_own, mix_own))
            in0 = far(after(block_in[0], mix_own))
            gu_own = trade(columns_of(after(w_gu, mix_own), 2, ff_strip), mix_own)
            done = (m1, m2, my, oy, in0)
            m12, my1, my2 = z1(after(m2, *done)), cross(after(m1, *done)), cross(after(m2, *done))
            o1, o2 = z1(after(out_own, *done)), z2(after(out_own, *done))
            in1 = far(after(block_in[1], *done, gu_own))
            done = (m12, my1, my2, in1, o1, o2)
            my12 = cross(after(m12, *done))
            o12, oy1, oy2 = z1(after(o2, *done)), cross(after(o1, *done)), cross(after(o2, *done))
            g1, g2 = z1(after(gu_own, *done)), z2(after(gu_own, *done))
            gy = cross(after(gu_own, my12))
            cot0 = far(after(out_grad[0], *done))
            oy12 = cross(o12)
            gy1, gy2 = cross(g1), cross(g2)
            cot1 = far(after(out_grad[1], cot0))
            g12 = z1(g2)
            waits["mix", 0] = (o12, g1)
            waits["mix", 1] = (g2, gy, oy1, oy2, oy12)
            waits["hop", 0] = (g12,)
            waits["hop", 1] = (gy1, cot1)
            waits["out", 0] = (gy2,)

            def later(*held):
                gy12 = cross(g12)
                waits["norm", 0] = (gy12,)
                found_gu = found(gu_own, g1, g2, g12, gy, gy1, gy2, gy12)
                return Weight(at, found_gu), Weight(at, lax.all_gather(after(w_down, *held), team)[:, None])

            def found(own, a1, a2, a12, y, y1, y2, y12):
                near = {(0, 0): own, (0, 1): a1, (0, 2): a2, (0, 3): a12}
                return {**near, (1, 0): y, (1, 1): y1, (1, 2): y2, (1, 3): y12}

            mix = Weight(at, found(mix_own, m1, m2, m12, my, my1, my2, my12))
            out = Weight(at, found(out_own, o1, o2, o12, oy, oy1, oy2, oy12))
            inputs, cotangent = (
                [[own, at.swap(own, 1), far_own, at.swap(far_own, 1)] for own, far_own in zip(here, there)]
                for here, there in ((block_in, (in0, in1)), (out_grad, (cot0, cot1)))
            )
        else:
            gu_own = trade(columns_of(w_gu, 2, ff_strip))
            mix, out = (Weight(at, at.gather_blocks(v)) for v in (mix_own, out_own))

            def later(*held):
                return Weight(at, at.gather_blocks(gu_own)), Weight(at, lax.all_gather(w_down, team)[:, None])

            inputs = [at.team_gather(block_in[c]) for c in range(micro)]
            cotangent = [at.team_gather(out_grad[c]) for c in range(micro)]

        def turn(name, c, *others):
            return after(place, *waits.get((name, c), ()), *others)

        upto = (jnp.arange(length)[:, None] <= jnp.arange(length)[None, :]).astype(BF16)
        counts = jnp.dot(starts.reshape(total, length), upto, preferred_element_type=F32)
        count_row = counts.reshape(total, 1, length)
        count_col = counts.reshape(total, length, 1)

        def pass_on(leaving, fade, sign, *held):
            factor = fade.reshape(TEAM, heads, HEAD)[..., None]
            entering = jnp.zeros(leaving.shape, F32)
            hops, moved = [], None
            for k in range(nz - 1):
                if moved is not None:
                    entering = entering + moved.astype(F32)
                pair = (k, k + 1) if sign == 1 else (nz - 1 - k, nz - 2 - k)
                moved = (factor * entering + leaving).astype(BF16)
                moved = lax.ppermute(after(moved, *held) if k == 1 else moved, "seq", [pair])
                hops.append(moved)
            return lambda *held: (entering + after(moved, *held).astype(F32)).astype(BF16), hops

        span, part, pair = (total, length), (TEAM, length), (TEAM // 2, length, features)
        states = (TEAM, heads, HEAD, HEAD)
        wide = 4 * own_channels
        per_matmul = 2 * TEAM * length * features

        normed = proj = running = qd = kg = mixed = gated = None
        normed2 = hidden = first = second = None
        entering, residual, fades, own_normed2 = [], [], [], []
        insides, leavings = [], []
        for c in range(micro):
            rows_c, cols_c = (a[c * TEAM : (c + 1) * TEAM] for a in (count_row, count_col))
            normed, proj, running, qd, kg, inside, leaving, fade, scales, bound = over_sequences(
                partial(mix_kernel, strip), turn("mix", c), c, TEAM,
                [(place, "scalars"), (rows_c, "part"), (cols_c, "part")],
                [
                    (span + (features,), BF16, "all"),
                    (span + (wide,), F32, "all"),
                    (span + (own_channels,), F32, "all"),
                    (span + (own_channels,), BF16, "all"),
                    (span + (own_channels,), BF16, "all"),
                    (part + (own_channels,), F32, "part"),
                    (states, F32, "part"),
                    ((TEAM, 1, own_channels), F32, "part"),
                    ((8, features), F32, "whole"),
                    ((1, own_channels), F32, "whole"),
                ],
                [normed, proj, running, qd, kg], [mix], inputs[c], per_matmul * wide,
            )
            if c == 0:
                attn_scale, ffn_scale = scales[0:1], scales[1:2]
                group_scale = scales[3].reshape(-1, rows)[:, : group_gain.shape[0]].reshape(1, HEAD)
            fades.append(fade)
            insides.append(inside)
            leavings.append(leaving)
            entering.append(pass_on(leaving, fade, 1, *waits.get(("hop", c), ()))[0]())
        gu, down = later(*entering)
        for c in range(micro):
            cols_c = count_col[c * TEAM : (c + 1) * TEAM]
            mixed, gated, even, odd = over_sequences(
                out_kernel, turn("out", c, *leavings), c, TEAM,
                [
                    (insides[c], "part"), (qd, "all"), (proj, ("all", own_channels, 3)), (entering[c], "part"), (cols_c, "part"),
                    (group_scale, "whole"),
                ],
                [
                    (span + (own_channels,), F32, "all"), (span + (own_channels,), BF16, "all"),
                    (pair, BF16, "pair"), (pair, BF16, "pair"),
                ],
                [mixed, gated], [out], (), per_matmul * own_channels,
            )
            summed = at.team_sum(even[None], odd[None], ())[0](*own_normed2)
            residual.append(block_in[c].astype(F32) + summed[0])
            rms_two = lax.rsqrt(jnp.mean(residual[c] * residual[c], axis=-1, keepdims=True) + EPSILON)
            own_normed2.append(after(residual[c] * rms_two * ffn_scale, *waits.get(("norm", c), ())).astype(BF16))

        def flat(a):
            return a.reshape(tokens, a.shape[-1])

        def team_share(left, right, s, *held):
            product = tn(left, right).astype(BF16).reshape(ny, s, nz, -1, right.shape[1])
            product = jnp.swapaxes(product, 1, 2).reshape(ny * nz, -1, right.shape[1])
            summed = lax.psum_scatter(after(product, *held), team, scatter_dimension=0, tiled=False)
            return summed.reshape(s, -1, right.shape[1]), product

        def weight_half(left, right, k):
            size = left.shape[1] // ny
            if ny == 2:
                y = 1 - at.y if k == 0 else at.y
                return tn(lax.dynamic_slice_in_dim(left, y * size, size, 1), right).astype(BF16)
            return tn(left, right).astype(BF16).reshape(ny, size, right.shape[1])

        def weight_halves(left, right):
            return [weight_half(left, right, k) for k in range(2 if ny == 2 else 1)]

        class WeightSum:
            def __init__(self, parts, s, moved=None, hold=()):
                self.s, width = s, parts[0].shape[-1]
                if ny == 2:
                    send, keep = parts
                    terms = [keep, at.swap_y(send, 1) if moved is None else moved]
                else:
                    terms = parts
                    for step in [1 << i for i in reversed(range(ny.bit_length() - 1))]:
                        halves = [t.reshape((t.shape[0] // 2 // step, 2, step) + t.shape[1:])[0] for t in terms]
                        bit = (at.y // step) % 2
                        pick = lambda k: [lax.dynamic_index_in_dim(t, k, 0, False) for t in halves]
                        send = sum(t.astype(F32) for t in pick(1 - bit)).astype(BF16)
                        terms = pick(bit) + [at.swap_y(send, step)]
                    terms = [t[0] for t in terms]
                self.terms = [t.reshape(s, nz, -1, width) for t in terms]
                self.terms[-1] = after(self.terms[-1], *hold)
                self.left, self.bit = nz, 0

            def step(self, *held):
                self.left //= 2
                terms = self.terms[:-1] + [after(self.terms[-1], *held)]
                halves = [t.reshape((self.s, self.left, 2) + t.shape[2:]) for t in terms]
                bit = (at.z // (1 << self.bit)) % 2
                pick = lambda k: [lax.dynamic_index_in_dim(t, k, 2, False) for t in halves]
                send = sum(t.astype(F32) for t in pick(1 - bit)).astype(BF16)
                self.terms = pick(bit) + [at.swap_z(send, 1 << self.bit)]
                self.bit += 1
                return send

            def finish(self, *held):
                while self.left > 1:
                    self.step()
                terms = self.terms[:-1] + [after(self.terms[-1], *held)]
                return lambda i: sum(lax.dynamic_index_in_dim(t[:, 0], i, 0, False).astype(F32) for t in terms)

        def out_of_team(summed, count, *held):
            got = at.by_rank(trade([summed(at.rank ^ j).astype(BF16) for j in range(TEAM)], *held)).astype(F32)
            width = got.shape[2] // (count * ny)
            got = got.reshape(TEAM, rows, count, ny, width)
            return jnp.transpose(got, (1, 2, 3, 0, 4)).reshape(rows, -1)

        both = whole_branch = None
        all_cot = jnp.concatenate([jnp.stack(pieces) for pieces in cotangent])
        for c in range(micro):
            normed2, hidden, first, second = over_sequences(
                up_kernel, turn("up", c), c, TEAM,
                [],
                [(span + (features,), BF16, "all")] + [(span + (own_ff,), BF16, "all")] * 3,
                [normed2, hidden, first, second], [gu],
                at.team_gather(own_normed2[c], *(() if hidden is None else (hidden,))), per_matmul * 2 * own_ff,
            )
        d_residual, d_branch, branch_own, gain_sums, sents = [], [], [], [], []
        held, moved, sums_of = (), (), []
        for c in range(micro):
            both, even, odd = over_sequences(
                down_back_kernel, turn("down_back", c, *held), c, TEAM,
                [(all_cot, "all"), (first, "all"), (second, "all")],
                [(span + (2 * own_ff,), BF16, "all"), (pair, BF16, "pair"), (pair, BF16, "pair")],
                [both], [down, gu], (), per_matmul * 3 * own_ff,
            )
            if c == 0:
                grad_down, down_product = team_share(after(flat(hidden), even), flat(all_cot), 1)
                grad_down = grad_down[0].astype(F32)
            else:
                finish(c - 1, even)
            d_normed2_of, sent, far = at.team_sum(even[None], odd[None], moved, *((down_product,) if c == 0 else branch_own))
            held, moved = (down_product, sent), (far,)
            sents.append(sent)
            sums_of.append(d_normed2_of)

            def finish(c, *held):
                d_normed2 = sums_of[c](*held)[0]
                res = residual[c]
                rms_two = lax.rsqrt(jnp.mean(res * res, axis=-1, keepdims=True) + EPSILON)
                gain_sums.append(jnp.sum(d_normed2 * res * rms_two, axis=0))
                scaled = d_normed2 * ffn_scale
                d_residual.append(
                    out_grad[c].astype(F32)
                    + rms_two * (scaled - res * rms_two * rms_two * jnp.mean(scaled * res, axis=-1, keepdims=True))
                )
                branch_own.append(d_residual[c].astype(BF16))
                return branch_own[c]

        finish(micro - 1)

        d_q = d_fv = d_o = None
        gs, group_sums, logit_sums, adjoints = [], [], [], []

        def enter_back(c, whole_branch, d_o, *held):
            cols_c = count_col[c * TEAM : (c + 1) * TEAM]
            whole_branch, d_o, g, toward, group_sum = over_sequences(
                out_back_kernel, turn("out_back", c, *held), c, TEAM,
                [
                    (mixed, "all"), (proj, ("all", own_channels, 3)), (qd, "all"), (cols_c, "part"), (group_scale, "whole"),
                ],
                [
                    (span + (features,), BF16, "all"), (span + (own_channels,), BF16, "all"),
                    (part + (own_channels,), BF16, "part"), (states, F32, "part"), ((TEAM, 1, own_channels), F32, "part"),
                ],
                [whole_branch, d_o], [out], d_branch[c], per_matmul * own_channels,
            )
            gs.append(g)
            group_sums.append(group_sum)
            adjoint, hops = pass_on(toward, fades[c], -1)
            adjoints.append(adjoint)
            return whole_branch, d_o, toward, hops

        toward = place
        gu_send = weight_half(after(flat(normed2), branch_own[0]), flat(both), 0)
        d_branch = [at.team_gather(branch_own[0], gu_send)]
        hops = []
        whole_branch, d_o, toward, hops = enter_back(0, whole_branch, d_o, gu_send, *sents[1:])
        gu_halves = [gu_send] + ([weight_half(after(flat(normed2), toward), flat(both), 1)] if ny == 2 else [])
        last_hops = hops
        for c in range(1, micro):
            d_branch.append(at.team_gather(branch_own[c], gu_halves[-1]))
            whole_branch, d_o, toward, last_hops = enter_back(c, whole_branch, d_o, gu_halves[-1], grad_down, *hops[:1])
        adjoints = [adjoint(toward) if c == 0 else adjoint() for c, adjoint in enumerate(adjoints)]
        gu_rows = sum(t.astype(F32) for t in WeightSum(gu_halves, TEAM, hold=adjoints).terms).astype(BF16)
        gu_rows = jnp.swapaxes(gu_rows, 0, 1).reshape(nz, TEAM * rows, 2 * own_ff)
        gu_sum = lax.psum_scatter(gu_rows, "seq", scatter_dimension=0, tiled=False).reshape(TEAM, rows, 2 * own_ff)
        paired = (micro, TEAM // 2, length, features)

        d_normed, dn_sent = [], []
        for c in range(micro):
            rows_c, cols_c = (a[c * TEAM : (c + 1) * TEAM] for a in (count_row, count_col))
            held = (toward,) if c == 0 else (*ffn_sent, *o_halves, *out_halves)
            d_q, d_fv, logit_sum, even, odd = over_sequences(
                mix_back_kernel, turn("mix_back", c, *held), c, TEAM,
                [
                    (proj, ("all", own_channels, 0)), (proj, ("all", own_channels, 1)), (proj, ("all", own_channels, 2)),
                    (running, "all"), (qd, "all"), (kg, "all"), (gs[c], "part"), (entering[c], "part"), (adjoints[c], "part"),
                    (bound, "whole"), (rows_c, "part"), (cols_c, "part"), (d_o, "all"),
                ],
                [
                    (span + (own_channels,), BF16, "all"), (span + (2 * own_channels,), BF16, "all"),
                    ((TEAM, 1, own_channels), F32, "part"), (pair, BF16, "pair"), (pair, BF16, "pair"),
                ],
                [d_q, d_fv], [mix], (), per_matmul * wide,
            )
            logit_sums.append(logit_sum)
            summed, sent, _ = at.team_sum(even[None], odd[None], ())
            d_normed.append(summed)
            dn_sent.append(sent)
            if c == 0:
                even, odd = over_sequences(
                    share_kernel, after(place, d_q, *last_hops[:1]), 0, total, [(hidden, "part")],
                    [((micro * TEAM // 2, length, features), BF16, "pair")] * 2, (), [down], (), 2 * tokens * own_ff * features,
                )
                o_halves = weight_halves(after(flat(normed), even, *last_hops[1:2], *dn_sent), flat(d_o))
                out_halves = weight_halves(after(flat(gated), *o_halves), flat(whole_branch))
                even, ffn_near = even.reshape(paired), after(at.swap(odd, 1), *o_halves).reshape(paired)
                ffn_sent = [(even[k, 1].astype(F32) + ffn_near[k, 1].astype(F32)).astype(BF16) for k in range(micro)]
                block_out = [
                    residual[k] + (even[k, 0].astype(F32) + ffn_near[k, 0].astype(F32) + at.swap(ffn_sent[k], 2).astype(F32))
                    for k in range(micro)
                ]
                block_out = [a.astype(BF16) for a in block_out]
        last, d_q = d_fv, after(d_q, d_fv)
        d_normed = [summed(last)[0] for summed in d_normed]
        if ny == 2:
            fv_halves = [weight_half(flat(normed), flat(d_fv), 0)]
            q_halves = [weight_half(after(flat(normed), *fv_halves), flat(d_q), 0)]
            fv_moved = at.swap_y(fv_halves[0], 1)
            q_moved = at.swap_y(after(q_halves[0], fv_moved), 1)
            out_halves[0] = after(out_halves[0], q_moved)
            left = after(flat(normed), *q_halves, *dn_sent)
            fv_halves.append(weight_half(left, flat(d_fv), 1))
            q_halves.append(weight_half(left, flat(d_q), 1))
        else:
            fv_halves, q_halves = weight_halves(flat(normed), flat(d_fv)), weight_halves(flat(normed), flat(d_q))
            fv_moved, q_moved = None, None
        o_part, out_part = WeightSum(o_halves, TEAM), WeightSum(out_halves, 1)
        fv_part, q_part = WeightSum(fv_halves, TEAM, fv_moved), WeightSum(q_halves, TEAM, q_moved)
        sent = o_part.step(fv_halves[-1], q_halves[-1])
        sent = fv_part.step(sent, *d_normed)
        q_sent = q_part.step(sent)
        sent = o_part.step(q_sent)
        sent = out_part.step(sent)
        gu_final = lambda i: lax.dynamic_index_in_dim(after(gu_sum, q_sent), i, 0, False)
        sent = fv_part.step(sent)
        sent = q_part.step(sent)
        sent = out_part.step(sent)
        d_normed, block_out = jnp.stack(d_normed), jnp.stack(block_out)
        x = block_in.astype(F32)
        rms_one = lax.rsqrt(jnp.mean(x * x, axis=-1, keepdims=True) + EPSILON)
        attn_sum = jnp.sum(d_normed * x * rms_one, axis=(0, 1))
        scaled = d_normed * attn_scale
        in_grad = jnp.stack(d_residual) + rms_one * (
            scaled - x * rms_one * rms_one * jnp.mean(scaled * x, axis=-1, keepdims=True)
        )

        logit_sum = bound[0] * (1.0 - bound[0]) * sum(jnp.sum(a, axis=(0, 1)) for a in logit_sums)
        logit_all = jnp.where(
            jnp.arange(TEAM)[None, :, None] == at.rank, logit_sum.reshape(ny, 1, strip), 0.0
        ).reshape(features)
        group_all = jnp.sum(sum(jnp.sum(a, axis=(0, 1)) for a in group_sums).reshape(heads, HEAD), axis=0)
        sums = at.everyone_sum(after(jnp.concatenate([attn_sum, sum(gain_sums), logit_all, group_all]), q_sent))

        grad_gu = out_of_team(gu_final, 2)
        parts = [part.finish(sums, grad_gu) for part in (q_part, fv_part, o_part)]
        parts = [
            jnp.concatenate([part(at.rank ^ j) for part in parts], axis=1).astype(BF16) for j in range(TEAM)
        ]
        grad_mix = pl.pallas_call(
            partial(place_kernel, strip),
            in_specs=[pl.BlockSpec(memory_space=pltpu.SMEM)] + [pl.BlockSpec(memory_space=pltpu.VMEM)] * TEAM,
            out_specs=pl.BlockSpec(memory_space=pltpu.VMEM),
            out_shape=jax.ShapeDtypeStruct((rows, TEAM * 4 * own_channels), F32),
        )(place, parts[0], *(at.swap(parts[j], j) for j in range(1, TEAM)))
        grad_out = out_part.finish(sums)(0)
        here = (at.y * TEAM + at.rank) * nz + at.z

        def mine(start, size):
            return lax.dynamic_slice_in_dim(sums, start + here * size, size)

        return (
            block_out,
            in_grad,
            grad_mix,
            grad_out,
            grad_gu,
            grad_down,
            mine(0, rows),
            mine(features, rows),
            mine(3 * features, group_gain.shape[0]),
            mine(2 * features, rows),
        )

    return local


def solution(mesh):
    devices = mesh.devices.reshape(-1, TEAM, mesh.shape["seq"])
    tokens = P(("y", "team"), "seq", None)
    matrix = P(("y", "team", "seq"), None)
    vector = P(("y", "team", "seq"))
    return jax.shard_map(
        build(devices.shape[0], devices.shape[2]),
        mesh=Mesh(devices, ("y", "team", "seq")),
        in_specs=(tokens, P(("y", "team"), "seq"), tokens) + (matrix,) * 4 + (vector,) * 4,
        out_specs=(tokens, tokens) + (matrix,) * 4 + (vector,) * 4,
        check_vma=False,
    )
```

```python
from functools import partial

import jax
import jax.numpy as jnp
from jax import lax
from jax.experimental import pallas as pl
from jax.experimental.pallas import tpu as pltpu
from jax.sharding import Mesh, PartitionSpec as P

HEAD = 128
TEAM = 4
EPSILON = 1e-06
SCALE = HEAD**-0.5
F32 = jnp.float32
BF16 = jnp.bfloat16
VMEM_LIMIT = 60 * 1024 * 1024


class Places:
    def __init__(self, ny, nz):
        self.ny, self.nz = ny, nz
        self.rank, self.y, self.z = lax.axis_index("team"), lax.axis_index("y"), lax.axis_index("seq")

    def swap(self, value, bits):
        return lax.ppermute(value, "team", [(i, i ^ bits) for i in range(TEAM)])

    def swap_y(self, value, bits):
        return lax.ppermute(value, "y", [(i, i ^ bits) for i in range(self.ny)])

    def swap_z(self, value, bits):
        return lax.ppermute(value, "seq", [(i, i ^ bits) for i in range(self.nz)])

    def by_rank(self, stack):
        odd, high = (self.rank & 1) == 1, (self.rank & 2) == 2
        stack = jnp.where(odd, jnp.concatenate([stack[1:2], stack[0:1], stack[3:4], stack[2:3]]), stack)
        return jnp.where(high, jnp.concatenate([stack[2:], stack[:2]]), stack)

    def team_gather(self, own, *held):
        one, two = self.swap(own, 1), self.swap(own, 2)
        return [own, one, two, self.swap(after(two, *held), 1)]

    def team_sum(self, even, odd, first_held, *held):
        near = self.swap(after(odd, *first_held), 1)
        sent = (even[:, 1].astype(F32) + after(near, *held)[:, 1].astype(F32)).astype(BF16)
        far = self.swap(sent, 2)
        return lambda *held: even[:, 0].astype(F32) + near[:, 0].astype(F32) + after(far, *held).astype(F32), sent, far


    def gather_blocks(self, own):
        found = {(0, 0): own}
        for step in [1 << i for i in reversed(range(self.nz.bit_length() - 1))]:
            found.update({(0, dz ^ step): self.swap_z(v, step) for (_, dz), v in list(found.items())})
        for step in [1 << i for i in range(self.ny.bit_length() - 1)]:
            found.update({(dy ^ step, dz): self.swap_y(v, step) for (dy, dz), v in list(found.items())})
        return found

    def everyone_sum(self, value):
        for step in (2, 1):
            value = value + self.swap(value, step)
        for step in [1 << i for i in reversed(range(self.ny.bit_length() - 1))]:
            value = value + self.swap_y(value, step)
        for step in [1 << i for i in reversed(range(self.nz.bit_length() - 1))]:
            value = value + self.swap_z(value, step)
        return value


class Weight:
    def __init__(self, at, found):
        self.ny, self.nz = at.ny, at.nz
        if isinstance(found, dict):
            self.s, self.rows, self.n = found[0, 0].shape
            self.keys, self.blocks = list(found), list(found.values())
        else:
            self.s, self.rows, self.n = found.shape[1:]
            self.keys, self.blocks = None, [found]
        self.height = self.ny * self.nz * self.s * self.rows
        self.split = self.rows % 16 == 0
        if not self.split:
            if self.keys:
                found = jnp.zeros((self.ny, self.nz) + self.blocks[0].shape, BF16)
                for (dy, dz), block in zip(self.keys, self.blocks):
                    found = lax.dynamic_update_slice(found, block[None, None], (at.y ^ dy, at.z ^ dz, 0, 0, 0))
            found = found.reshape(self.ny, self.nz, self.s, self.rows, self.n)
            self.blocks = [jnp.swapaxes(found, 1, 2).reshape(self.height, self.n)]

    @property
    def copies(self):
        return self.ny * self.nz * self.s if self.split else 1

    def load(self, refs, place_ref, into, sems):
        for copy in self.copies_of(refs, place_ref, into, sems):
            copy.start()

    def copies_of(self, refs, place_ref, into, sems):
        if not self.split:
            return [pltpu.make_async_copy(refs[0], into, sems.at[0])]
        rank, y, z = place_ref[0], place_ref[1], place_ref[2]
        if self.keys:
            blocks = [(y ^ dy, z ^ dz, ref) for (dy, dz), ref in zip(self.keys, refs)]
        else:
            blocks = [(i // self.nz, i % self.nz, refs[0].at[i]) for i in range(self.ny * self.nz)]
        copies = []
        for there_y, there_z, ref in blocks:
            for j in range(self.s):
                s = rank ^ j if self.s > 1 else 0
                row = ((there_y * self.s + s) * self.nz + there_z) * self.rows
                if not isinstance(row, int):
                    row = pl.multiple_of(row, self.rows)
                copies.append(pltpu.make_async_copy(ref.at[j], into.at[pl.ds(row, self.rows)], sems.at[len(copies)]))
        return copies


def nn(a, b):
    return jnp.dot(a, b, preferred_element_type=F32)


def nt(a, b):
    return lax.dot_general(a, b, (((1,), (1,)), ((), ())), preferred_element_type=F32)


def tn(a, b):
    return lax.dot_general(a, b, (((0,), (0,)), ((), ())), preferred_element_type=F32)


def add_up(matrix, value):
    high = value.astype(BF16)
    rest = value - high.astype(F32)
    mid = rest.astype(BF16)
    low = (rest - mid.astype(F32)).astype(BF16)
    return nn(matrix, high) + nn(matrix, mid) + nn(matrix, low)


def triangle(n, lower):
    row = lax.broadcasted_iota(jnp.int32, (n, n), 0)
    col = lax.broadcasted_iota(jnp.int32, (n, n), 1)
    return row >= col if lower else row <= col


def sigmoid(z):
    return 1.0 / (1.0 + jnp.exp(-z))


def gates(f_pre, lower):
    small = jnp.exp(-jnp.abs(f_pre))
    big_part = 1.0 / (1.0 + small)
    small_part = small * big_part
    positive = f_pre >= 0
    opened = jnp.where(positive, big_part, small_part)
    closed = jnp.where(positive, small_part, big_part)
    return opened, closed, lower + (1.0 - lower) * opened


def wide_blocks(width):
    step = 512
    return [(a, min(a + step, width)) for a in range(0, width, step)]


def take_piece(step, piece_refs, into_ref):
    for j, ref in enumerate(piece_refs):

        @pl.when(step == j)
        def _(ref=ref):
            into_ref[0] = ref[...]


def put_share(step, even_ref, odd_ref, a, b, value):
    value = value.astype(BF16)

    @pl.when(step % 2 == 0)
    def _():
        even_ref[0, :, a:b] = value

    @pl.when(step % 2 == 1)
    def _():
        odd_ref[0, :, a:b] = value


def pick_kernel(strip, place_ref, w_ref, extra_ref, *out_refs):
    rank = place_ref[0]
    count = w_ref.shape[1] // (TEAM * strip)
    for j, out_ref in enumerate(out_refs):
        for k in range(count):
            at = pl.multiple_of((k * TEAM + (rank ^ j)) * strip, strip)
            out_ref[:, k * strip : (k + 1) * strip] = w_ref[:, pl.ds(at, strip)]
        out_ref[:, count * strip :] = extra_ref[...]


def place_kernel(strip, place_ref, *refs):
    out_ref = refs[-1]
    for j, ref in enumerate(refs[:-1]):
        for k in range(ref.shape[1] // strip):
            at = pl.multiple_of((k * TEAM + (place_ref[0] ^ j)) * strip, strip)
            out_ref[:, pl.ds(at, strip)] = ref[:, k * strip : (k + 1) * strip].astype(F32)


def place_cases_kernel(strip, place_ref, *refs):
    out_ref = refs[-1]
    for rank in range(TEAM):

        @pl.when(place_ref[0] == rank)
        def _(rank=rank):
            for j, ref in enumerate(refs[:-1]):
                for k in range(ref.shape[1] // strip):
                    at = (k * TEAM + (rank ^ j)) * strip
                    out_ref[:, at : at + strip] = ref[:, k * strip : (k + 1) * strip].astype(F32)


def mix_kernel(strip, step, fetch, piece_refs, place_ref, row_ref, col_ref, *refs):
    normed_ref, proj_ref, run_ref, qd_ref, kg_ref, ins_ref, leave_ref, fade_ref, scales_ref, lower_ref = refs
    channels = lower_ref.shape[1]
    (w_ref,) = fetch()

    @pl.when(step == 0)
    def _():
        row = lax.broadcasted_iota(jnp.int32, (8, HEAD), 0)
        col = lax.broadcasted_iota(jnp.int32, (8, HEAD), 1)
        pick = jnp.where(row == col, 1.0, 0.0).astype(BF16)
        scales_ref[...] = nt(pick, w_ref[:, 4 * channels :])
        for k in range(channels // strip):
            at = pl.multiple_of((k * TEAM + place_ref[0]) * strip, strip)
            lower_ref[:, k * strip : (k + 1) * strip] = sigmoid(scales_ref[2:3, pl.ds(at, strip)])

    gain = scales_ref[0:1]
    take_piece(step, piece_refs, normed_ref)
    x = normed_ref[0].astype(F32)
    scale = lax.rsqrt(jnp.mean(x * x, axis=-1, keepdims=True) + EPSILON)
    normed_ref[0] = (x * scale * gain).astype(BF16)
    for a, b in wide_blocks(4 * channels):
        proj_ref[0, :, a:b] = nn(normed_ref[0], w_ref[:, a:b])
    lower = lower_ref[...]
    q_pre = proj_ref[0, :, 0:channels]
    f_pre = proj_ref[0, :, channels : 2 * channels]
    _, closed, decays = gates(f_pre, lower)
    keys = (1.0 - lower) * closed
    length = x.shape[0]
    causal = triangle(length, True)
    running = add_up(causal.astype(BF16), jnp.log(decays))
    run_ref[0] = running
    row, col = row_ref[0], col_ref[0]
    alive = (col[length - 1 :] == 0).astype(F32)
    tail = (col == col[length - 1 :]).astype(F32)
    final = running[length - 1 :]
    fade_ref[0] = jnp.exp(final) * alive
    qd_ref[0] = (q_pre * sigmoid(q_pre) * jnp.exp(running)).astype(BF16)
    kg_ref[0] = (keys * jnp.exp(-running)).astype(BF16)
    last = (keys * jnp.exp(final - running) * tail).astype(BF16)
    mask = jnp.where(causal & (col == row), 1.0, 0.0)
    for h in range(channels // HEAD):
        cut = slice(h * HEAD, (h + 1) * HEAD)
        values = proj_ref[0, :, 2 * channels + h * HEAD : 2 * channels + (h + 1) * HEAD].astype(BF16)
        scores = (nt(qd_ref[0, :, cut], kg_ref[0, :, cut]) * mask).astype(BF16)
        ins_ref[0, :, cut] = nn(scores, values) * SCALE
        leave_ref[0, h] = tn(last[:, cut], values)


def out_kernel(step, fetch, piece_refs, ins_ref, qd_ref, o_ref, state_ref, col_ref, group_ref, *refs):
    mixed_ref, gated_ref, even_ref, odd_ref = refs
    channels = ins_ref.shape[2]
    alive = (col_ref[0] == 0).astype(F32) * SCALE
    for h in range(channels // HEAD):
        cut = slice(h * HEAD, (h + 1) * HEAD)
        mixed = ins_ref[0, :, cut] + alive * nn(qd_ref[0, :, cut], state_ref[0, h])
        mixed_ref[0, :, cut] = mixed
        scale = lax.rsqrt(jnp.mean(mixed * mixed, axis=-1, keepdims=True) + EPSILON)
        o_pre = o_ref[0, :, cut]
        gated_ref[0, :, cut] = (mixed * scale * group_ref[...] * (o_pre * sigmoid(o_pre))).astype(BF16)
    (w_ref,) = fetch()
    for a, b in wide_blocks(w_ref.shape[1]):
        put_share(step, even_ref, odd_ref, a, b, nn(gated_ref[0], w_ref[:, a:b]))


def up_kernel(step, fetch, piece_refs, normed_ref, hidden_ref, first_ref, second_ref):
    width = hidden_ref.shape[2]
    take_piece(step, piece_refs, normed_ref)
    (w_ref,) = fetch()
    for a, b in wide_blocks(width):
        gate = nn(normed_ref[0], w_ref[:, a:b])
        up = nn(normed_ref[0], w_ref[:, width + a : width + b])
        s = sigmoid(gate)
        silu = gate * s
        hidden_ref[0, :, a:b] = (silu * up).astype(BF16)
        first_ref[0, :, a:b] = (up * (s * (1.0 + gate * (1.0 - s)))).astype(BF16)
        second_ref[0, :, a:b] = silu.astype(BF16)


def down_back_kernel(step, fetch, piece_refs, cot_ref, first_ref, second_ref, both_ref, even_ref, odd_ref):
    width = first_ref.shape[2]
    down_ref, w_ref = fetch()
    for a, b in wide_blocks(width):
        d_hidden = nt(cot_ref[0], down_ref[a:b, :])
        both_ref[0, :, a:b] = (d_hidden * first_ref[0, :, a:b].astype(F32)).astype(BF16)
        both_ref[0, :, width + a : width + b] = (d_hidden * second_ref[0, :, a:b].astype(F32)).astype(BF16)
    for a, b in wide_blocks(w_ref.shape[0]):
        put_share(step, even_ref, odd_ref, a, b, nt(both_ref[0], w_ref[a:b, :]))


def out_back_kernel(step, fetch, piece_refs, mixed_ref, o_ref, qd_ref, col_ref, group_ref, *refs):
    branch_ref, d_o_ref, g_ref, toward_ref, sum_ref = refs
    channels = mixed_ref.shape[2]
    take_piece(step, piece_refs, branch_ref)
    alive = (col_ref[0] == 0).astype(F32)
    group = group_ref[...]
    (w_ref,) = fetch()
    d_gated_all = nt(branch_ref[0], w_ref[...])
    for h in range(channels // HEAD):
        cut = slice(h * HEAD, (h + 1) * HEAD)
        d_gated = d_gated_all[:, cut]
        mixed = mixed_ref[0, :, cut]
        scale = lax.rsqrt(jnp.mean(mixed * mixed, axis=-1, keepdims=True) + EPSILON)
        unit = mixed * scale
        o_pre = o_ref[0, :, cut]
        s = sigmoid(o_pre)
        silu = o_pre * s
        both = d_gated * unit
        d_o_ref[0, :, cut] = (both * group * (s * (1.0 + o_pre * (1.0 - s)))).astype(BF16)
        sum_ref[0, :, cut] = jnp.sum(both * silu, axis=0, keepdims=True)
        d_unit = d_gated * group * silu
        d_mixed = scale * (d_unit - unit * jnp.mean(d_unit * unit, axis=-1, keepdims=True))
        g = (d_mixed * SCALE).astype(BF16)
        g_ref[0, :, cut] = g
        reach = (qd_ref[0, :, cut].astype(F32) * alive).astype(BF16)
        toward_ref[0, h] = tn(reach, g)


def mix_back_kernel(
    step, fetch, piece_refs, q_ref, f_ref, v_ref, run_ref, qd_ref, kg_ref, g_ref, state_ref, adjoint_ref, lower_ref,
    row_ref, col_ref, d_o_ref, d_q_ref, d_fv_ref, sum_ref, even_ref, odd_ref,
):
    channels = lower_ref.shape[1]
    length = row_ref.shape[2]
    lower = lower_ref[...]
    row, col = row_ref[0], col_ref[0]
    alive = (col == 0).astype(F32)
    alive_end = alive[length - 1 :]
    tail = (col == col[length - 1 :]).astype(F32)
    mask = jnp.where(triangle(length, True) & (col == row), 1.0, 0.0)
    later = triangle(length, False).astype(BF16)
    eye = lax.broadcasted_iota(jnp.int32, (HEAD, HEAD), 0) == lax.broadcasted_iota(jnp.int32, (HEAD, HEAD), 1)
    for h in range(channels // HEAD):
        cut = slice(h * HEAD, (h + 1) * HEAD)
        q_pre, f_pre = q_ref[0, :, cut], f_ref[0, :, cut]
        values = v_ref[0, :, cut].astype(BF16)
        running = run_ref[0, :, cut]
        qd, kg, g = qd_ref[0, :, cut], kg_ref[0, :, cut], g_ref[0, :, cut]
        state, adjoint = state_ref[0, h], adjoint_ref[0, h]
        low = lower[:, cut]
        opened, closed, decays = gates(f_pre, low)
        keys = (1.0 - low) * closed
        final = running[length - 1 :]
        last_factor = jnp.exp(final - running) * tail
        last = (keys * last_factor).astype(BF16)
        scores = (nt(qd, kg) * mask).astype(BF16)
        d_values = tn(scores, g) + nn(last, adjoint)
        d_scores = (nt(g, values) * mask).astype(BF16)
        d_qd = nn(d_scores, kg) + alive * nt(g, state)
        d_kg = tn(d_scores, qd)
        d_last = nt(values, adjoint)
        part_last = d_last * last.astype(F32)
        moved = d_qd * qd.astype(F32) - d_kg * kg.astype(F32) - part_last
        passed = jnp.sum(adjoint.astype(F32) * state.astype(F32), axis=1, keepdims=True)
        passed = jnp.sum(jnp.where(eye, passed, 0.0), axis=0, keepdims=True)
        d_final = jnp.sum(part_last, axis=0, keepdims=True) + passed * jnp.exp(final) * alive_end
        d_log = add_up(later, moved) + d_final
        d_queries = d_qd * jnp.exp(running)
        d_keys = d_kg * jnp.exp(-running) + d_last * last_factor
        common = d_log / decays - d_keys
        s = sigmoid(q_pre)
        d_q_ref[0, :, cut] = (d_queries * (s * (1.0 + q_pre * (1.0 - s)))).astype(BF16)
        d_fv_ref[0, :, cut] = ((1.0 - low) * opened * closed * common).astype(BF16)
        d_fv_ref[0, :, channels + h * HEAD : channels + (h + 1) * HEAD] = d_values.astype(BF16)
        sum_ref[0, :, cut] = jnp.sum(closed * common, axis=0, keepdims=True)
    (w_ref,) = fetch()
    parts = [(0, d_q_ref), (channels, d_fv_ref), (3 * channels, d_o_ref)]
    for a, b in wide_blocks(w_ref.shape[0]):
        value = sum(nt(ref[0], w_ref[a:b, k : k + ref.shape[2]]) for k, ref in parts)
        put_share(step, even_ref, odd_ref, a, b, value)


def share_kernel(step, fetch, piece_refs, left_ref, even_ref, odd_ref):
    (w_ref,) = fetch()
    for a, b in wide_blocks(w_ref.shape[1]):
        put_share(step, even_ref, odd_ref, a, b, nn(left_ref[0], w_ref[:, a:b]))


def over_sequences(kernel, place, chunk, count, ins, outs, held=(), weights=(), pieces=(), flops=0):
    def spec(shape, kind):
        if kind == "scalars":
            return pl.BlockSpec(memory_space=pltpu.SMEM)
        if kind == "whole":
            return pl.BlockSpec(shape, lambda i: (0,) * len(shape), pipeline_mode=pl.Buffered(1))
        if kind == "pair":
            return pl.BlockSpec((1,) + shape[1:], lambda i: (i // 2,) + (0,) * (len(shape) - 1))
        offset = 0 if kind == "part" else chunk * count
        if isinstance(kind, tuple):
            _, width, at = kind
            return pl.BlockSpec((1, shape[1], width), lambda i: (offset + i, 0, at))
        return pl.BlockSpec((1,) + shape[1:], lambda i: (offset + i,) + (0,) * (len(shape) - 1))

    anywhere = pl.BlockSpec(memory_space=pl.ANY)
    arrays, specs = [place], [pl.BlockSpec(memory_space=pltpu.SMEM)]
    for w in weights:
        arrays += w.blocks
        specs += [anywhere] * len(w.blocks)
    for piece in pieces:
        arrays.append(piece)
        specs.append(spec(piece.shape, "whole"))
    arrays += [a for a, _ in ins]
    specs += [spec(a.shape, kind) for a, kind in ins]
    aliases = {}
    for i, array in enumerate(held):
        if array is not None:
            aliases[len(arrays)] = i
            arrays.append(array)
            specs.append(anywhere)

    def body(*refs):
        refs = list(refs)
        place_ref = refs.pop(0)
        block_refs = [[refs.pop(0) for _ in w.blocks] for w in weights]
        piece_refs = [refs.pop(0) for _ in pieces]
        in_refs = [refs.pop(0) for _ in ins]
        del refs[: len(aliases)]
        out_refs = [refs.pop(0) for _ in outs]
        into, sems = refs[: len(weights)], refs[len(weights) :]
        step = pl.program_id(0)

        @pl.when(step == 0)
        def _():
            for w, blocks, ref, sem in zip(weights, block_refs, into, sems):
                w.load(blocks, place_ref, ref, sem)

        def fetch():
            @pl.when(step == 0)
            def _():
                for w, blocks, ref, sem in zip(weights, block_refs, into, sems):
                    for copy in w.copies_of(blocks, place_ref, ref, sem):
                        copy.wait()

            return into

        kernel(step, fetch, piece_refs, *in_refs, *out_refs)

    size = sum(a.size * a.dtype.itemsize for a in arrays)
    return pl.pallas_call(
        body,
        grid=(count,),
        in_specs=specs,
        out_specs=[spec(shape, kind) for shape, _, kind in outs],
        out_shape=[jax.ShapeDtypeStruct(shape, kind) for shape, kind, _ in outs],
        scratch_shapes=[pltpu.VMEM((w.height, w.n), BF16) for w in weights]
        + [pltpu.SemaphoreType.DMA((w.copies,)) for w in weights],
        input_output_aliases=aliases,
        compiler_params=pltpu.CompilerParams(vmem_limit_bytes=VMEM_LIMIT),
        cost_estimate=pl.CostEstimate(flops=flops, bytes_accessed=size // 4, transcendentals=0),
    )(*arrays)


def after(value, *others):
    return lax.optimization_barrier((value,) + others)[0] if others else value


def build(ny, nz):
    def local(block_in, doc_starts, out_grad, w_mix, w_out, w_gu, w_down, attn_gain, ffn_gain, group_gain, lower_logit):
        at = Places(ny, nz)
        micro, length, features = block_in.shape
        rows = w_mix.shape[0]
        own_channels = ny * nz * rows
        heads = own_channels // HEAD
        strip = own_channels // ny
        ff_rows = w_down.shape[0]
        own_ff = ny * nz * ff_rows
        ff_strip = nz * ff_rows
        total = micro * TEAM
        tokens = total * length
        place = jnp.stack([at.rank, at.y, at.z]).astype(jnp.int32)
        team = ("y", "seq")

        def trade(parts, *held):
            return jnp.stack([parts[0]] + [at.swap(after(parts[j], *held), j) for j in range(1, TEAM)])

        def columns_of(matrix, count, width):
            parts = matrix.reshape(rows, count * ny, TEAM, width)
            return [lax.dynamic_index_in_dim(parts, at.rank ^ j, 2, False).reshape(rows, -1) for j in range(TEAM)]

        group_share = jnp.pad(group_gain, (0, rows - group_gain.shape[0]))
        extra = jnp.stack([attn_gain, ffn_gain, lower_logit, group_share], axis=1).astype(BF16)
        extra = jnp.pad(extra, ((0, 0), (0, HEAD - extra.shape[1])))
        mix_width = 4 * own_channels + HEAD
        mix_parts = pl.pallas_call(
            partial(pick_kernel, strip),
            in_specs=[pl.BlockSpec(memory_space=pltpu.SMEM)] + [pl.BlockSpec(memory_space=pltpu.VMEM)] * 2,
            out_specs=[pl.BlockSpec(memory_space=pltpu.VMEM)] * TEAM,
            out_shape=[jax.ShapeDtypeStruct((rows, mix_width), BF16)] * TEAM,
        )(place, w_mix, extra)
        mix_own, out_own = trade(mix_parts), w_out[None]
        starts = doc_starts.astype(BF16)[:, None]
        starts = jnp.concatenate([starts, at.swap(starts, 1)], axis=1)
        starts = jnp.concatenate([starts, at.swap(starts, 2)], axis=1)
        waits = {}
        if (ny, nz) == (2, 4) and micro == 2:
            z1, z2 = (lambda v: at.swap_z(v, 1)), (lambda v: at.swap_z(v, 2))
            cross = lambda v: at.swap_y(v, 1)
            far = lambda v: at.swap(v, 2)
            m1, m2, my = z1(mix_own), z2(mix_own), cross(mix_own)
            oy = cross(after(out_own, mix_own))
            in0 = far(after(block_in[0], mix_own))
            gu_own = trade(columns_of(after(w_gu, mix_own), 2, ff_strip), mix_own)
            done = (m1, m2, my, oy, in0)
            m12, my1, my2 = z1(after(m2, *done)), cross(after(m1, *done)), cross(after(m2, *done))
            o1, o2 = z1(after(out_own, *done)), z2(after(out_own, *done))
            in1 = far(after(block_in[1], *done, gu_own))
            done = (m12, my1, my2, in1, o1, o2)
            my12 = cross(after(m12, *done))
            o12, oy1, oy2 = z1(after(o2, *done)), cross(after(o1, *done)), cross(after(o2, *done))
            g1, g2 = z1(after(gu_own, *done)), z2(after(gu_own, *done))
            gy = cross(after(gu_own, my12))
            cot0 = far(after(out_grad[0], *done))
            oy12 = cross(o12)
            gy1, gy2 = cross(g1), cross(g2)
            cot1 = far(after(out_grad[1], cot0))
            g12 = z1(g2)
            waits["mix", 0] = (o12, g1)
            waits["mix", 1] = (g2, gy, oy1, oy2, oy12)
            waits["hop", 0] = (g12,)
            waits["hop", 1] = (gy1, cot1)
            waits["out", 0] = (gy2,)

            def later(*held):
                gy12 = cross(g12)
                waits["norm", 0] = (gy12,)
                found_gu = found(gu_own, g1, g2, g12, gy, gy1, gy2, gy12)
                return Weight(at, found_gu), Weight(at, lax.all_gather(after(w_down, *held), team)[:, None])

            def found(own, a1, a2, a12, y, y1, y2, y12):
                near = {(0, 0): own, (0, 1): a1, (0, 2): a2, (0, 3): a12}
                return {**near, (1, 0): y, (1, 1): y1, (1, 2): y2, (1, 3): y12}

            mix = Weight(at, found(mix_own, m1, m2, m12, my, my1, my2, my12))
            out = Weight(at, found(out_own, o1, o2, o12, oy, oy1, oy2, oy12))
            inputs, cotangent = (
                [[own, at.swap(own, 1), far_own, at.swap(far_own, 1)] for own, far_own in zip(here, there)]
                for here, there in ((block_in, (in0, in1)), (out_grad, (cot0, cot1)))
            )
        else:
            gu_own = trade(columns_of(w_gu, 2, ff_strip))
            mix, out = (Weight(at, at.gather_blocks(v)) for v in (mix_own, out_own))

            def later(*held):
                return Weight(at, at.gather_blocks(gu_own)), Weight(at, lax.all_gather(w_down, team)[:, None])

            inputs = [at.team_gather(block_in[c]) for c in range(micro)]
            cotangent = [at.team_gather(out_grad[c]) for c in range(micro)]

        def turn(name, c, *others):
            return after(place, *waits.get((name, c), ()), *others)

        upto = (jnp.arange(length)[:, None] <= jnp.arange(length)[None, :]).astype(BF16)
        counts = jnp.dot(starts.reshape(total, length), upto, preferred_element_type=F32)
        count_row = counts.reshape(total, 1, length)
        count_col = counts.reshape(total, length, 1)

        def pass_on(leaving, fade, sign, *held):
            factor = fade.reshape(TEAM, heads, HEAD)[..., None]
            entering = jnp.zeros(leaving.shape, F32)
            hops, moved = [], None
            for k in range(nz - 1):
                if moved is not None:
                    entering = entering + moved.astype(F32)
                pair = (k, k + 1) if sign == 1 else (nz - 1 - k, nz - 2 - k)
                moved = (factor * entering + leaving).astype(BF16)
                moved = lax.ppermute(after(moved, *held) if k == 1 else moved, "seq", [pair])
                hops.append(moved)
            return lambda *held: (entering + after(moved, *held).astype(F32)).astype(BF16), hops

        span, part, pair = (total, length), (TEAM, length), (TEAM // 2, length, features)
        states = (TEAM, heads, HEAD, HEAD)
        wide = 4 * own_channels
        per_matmul = 2 * TEAM * length * features

        normed = proj = running = qd = kg = mixed = gated = None
        normed2 = hidden = first = second = None
        entering, residual, fades, own_normed2 = [], [], [], []
        insides, leavings = [], []
        for c in range(micro):
            rows_c, cols_c = (a[c * TEAM : (c + 1) * TEAM] for a in (count_row, count_col))
            normed, proj, running, qd, kg, inside, leaving, fade, scales, bound = over_sequences(
                partial(mix_kernel, strip), turn("mix", c), c, TEAM,
                [(place, "scalars"), (rows_c, "part"), (cols_c, "part")],
                [
                    (span + (features,), BF16, "all"),
                    (span + (wide,), F32, "all"),
                    (span + (own_channels,), F32, "all"),
                    (span + (own_channels,), BF16, "all"),
                    (span + (own_channels,), BF16, "all"),
                    (part + (own_channels,), F32, "part"),
                    (states, F32, "part"),
                    ((TEAM, 1, own_channels), F32, "part"),
                    ((8, features), F32, "whole"),
                    ((1, own_channels), F32, "whole"),
                ],
                [normed, proj, running, qd, kg], [mix], inputs[c], per_matmul * wide,
            )
            if c == 0:
                attn_scale, ffn_scale = scales[0:1], scales[1:2]
                group_scale = scales[3].reshape(-1, rows)[:, : group_gain.shape[0]].reshape(1, HEAD)
            fades.append(fade)
            insides.append(inside)
            leavings.append(leaving)
            entering.append(pass_on(leaving, fade, 1, *waits.get(("hop", c), ()))[0]())
        gu, down = later(*entering)
        for c in range(micro):
            cols_c = count_col[c * TEAM : (c + 1) * TEAM]
            mixed, gated, even, odd = over_sequences(
                out_kernel, turn("out", c, *leavings), c, TEAM,
                [
                    (insides[c], "part"), (qd, "all"), (proj, ("all", own_channels, 3)), (entering[c], "part"), (cols_c, "part"),
                    (group_scale, "whole"),
                ],
                [
                    (span + (own_channels,), F32, "all"), (span + (own_channels,), BF16, "all"),
                    (pair, BF16, "pair"), (pair, BF16, "pair"),
                ],
                [mixed, gated], [out], (), per_matmul * own_channels,
            )
            summed = at.team_sum(even[None], odd[None], ())[0](*own_normed2)
            residual.append(block_in[c].astype(F32) + summed[0])
            rms_two = lax.rsqrt(jnp.mean(residual[c] * residual[c], axis=-1, keepdims=True) + EPSILON)
            own_normed2.append(after(residual[c] * rms_two * ffn_scale, *waits.get(("norm", c), ())).astype(BF16))

        def flat(a):
            return a.reshape(tokens, a.shape[-1])

        def team_share(left, right, s, *held):
            product = tn(left, right).astype(BF16).reshape(ny, s, nz, -1, right.shape[1])
            product = jnp.swapaxes(product, 1, 2).reshape(ny * nz, -1, right.shape[1])
            summed = lax.psum_scatter(after(product, *held), team, scatter_dimension=0, tiled=False)
            return summed.reshape(s, -1, right.shape[1]), product

        def weight_half(left, right, k):
            size = left.shape[1] // ny
            if ny == 2:
                y = 1 - at.y if k == 0 else at.y
                return tn(lax.dynamic_slice_in_dim(left, y * size, size, 1), right).astype(BF16)
            return tn(left, right).astype(BF16).reshape(ny, size, right.shape[1])

        def weight_halves(left, right):
            return [weight_half(left, right, k) for k in range(2 if ny == 2 else 1)]

        class WeightSum:
            def __init__(self, parts, s, moved=None, hold=()):
                self.s, width = s, parts[0].shape[-1]
                if ny == 2:
                    send, keep = parts
                    terms = [keep, at.swap_y(send, 1) if moved is None else moved]
                else:
                    terms = parts
                    for step in [1 << i for i in reversed(range(ny.bit_length() - 1))]:
                        halves = [t.reshape((t.shape[0] // 2 // step, 2, step) + t.shape[1:])[0] for t in terms]
                        bit = (at.y // step) % 2
                        pick = lambda k: [lax.dynamic_index_in_dim(t, k, 0, False) for t in halves]
                        send = sum(t.astype(F32) for t in pick(1 - bit)).astype(BF16)
                        terms = pick(bit) + [at.swap_y(send, step)]
                    terms = [t[0] for t in terms]
                self.terms = [t.reshape(s, nz, -1, width) for t in terms]
                self.terms[-1] = after(self.terms[-1], *hold)
                self.left, self.bit = nz, 0

            def step(self, *held):
                self.left //= 2
                terms = self.terms[:-1] + [after(self.terms[-1], *held)]
                halves = [t.reshape((self.s, self.left, 2) + t.shape[2:]) for t in terms]
                bit = (at.z // (1 << self.bit)) % 2
                pick = lambda k: [lax.dynamic_index_in_dim(t, k, 2, False) for t in halves]
                send = sum(t.astype(F32) for t in pick(1 - bit)).astype(BF16)
                self.terms = pick(bit) + [at.swap_z(send, 1 << self.bit)]
                self.bit += 1
                return send

            def finish(self, *held):
                while self.left > 1:
                    self.step()
                terms = self.terms[:-1] + [after(self.terms[-1], *held)]
                return lambda i: sum(lax.dynamic_index_in_dim(t[:, 0], i, 0, False).astype(F32) for t in terms)

        def out_of_team(parts, kernel):
            parts = [parts[0]] + [at.swap(parts[j], j) for j in range(1, TEAM)]
            return pl.pallas_call(
                kernel,
                in_specs=[pl.BlockSpec(memory_space=pltpu.SMEM)] + [pl.BlockSpec(memory_space=pltpu.VMEM)] * TEAM,
                out_specs=pl.BlockSpec(memory_space=pltpu.VMEM),
                out_shape=jax.ShapeDtypeStruct((rows, TEAM * parts[0].shape[1]), F32),
                compiler_params=pltpu.CompilerParams(vmem_limit_bytes=VMEM_LIMIT),
            )(place, *parts)

        both = whole_branch = None
        all_cot = jnp.concatenate([jnp.stack(pieces) for pieces in cotangent])
        for c in range(micro):
            normed2, hidden, first, second = over_sequences(
                up_kernel, turn("up", c), c, TEAM,
                [],
                [(span + (features,), BF16, "all")] + [(span + (own_ff,), BF16, "all")] * 3,
                [normed2, hidden, first, second], [gu],
                at.team_gather(own_normed2[c], *(() if hidden is None else (hidden,))), per_matmul * 2 * own_ff,
            )
        d_residual, d_branch, branch_own, gain_sums, sents = [], [], [], [], []
        held, moved, sums_of = (), (), []
        for c in range(micro):
            both, even, odd = over_sequences(
                down_back_kernel, turn("down_back", c, *held), c, TEAM,
                [(all_cot, "all"), (first, "all"), (second, "all")],
                [(span + (2 * own_ff,), BF16, "all"), (pair, BF16, "pair"), (pair, BF16, "pair")],
                [both], [down, gu], (), per_matmul * 3 * own_ff,
            )
            if c == 0:
                grad_down, down_product = team_share(after(flat(hidden), even), flat(all_cot), 1)
                grad_down = grad_down[0].astype(F32)
            else:
                finish(c - 1, even)
            d_normed2_of, sent, far = at.team_sum(even[None], odd[None], moved, *((down_product,) if c == 0 else branch_own))
            held, moved = (down_product, sent), (far,)
            sents.append(sent)
            sums_of.append(d_normed2_of)

            def finish(c, *held):
                d_normed2 = sums_of[c](*held)[0]
                res = residual[c]
                rms_two = lax.rsqrt(jnp.mean(res * res, axis=-1, keepdims=True) + EPSILON)
                gain_sums.append(jnp.sum(d_normed2 * res * rms_two, axis=0))
                scaled = d_normed2 * ffn_scale
                d_residual.append(
                    out_grad[c].astype(F32)
                    + rms_two * (scaled - res * rms_two * rms_two * jnp.mean(scaled * res, axis=-1, keepdims=True))
                )
                branch_own.append(d_residual[c].astype(BF16))
                return branch_own[c]

        finish(micro - 1)

        d_q = d_fv = d_o = None
        gs, group_sums, logit_sums, adjoints = [], [], [], []

        def enter_back(c, whole_branch, d_o, *held):
            cols_c = count_col[c * TEAM : (c + 1) * TEAM]
            whole_branch, d_o, g, toward, group_sum = over_sequences(
                out_back_kernel, turn("out_back", c, *held), c, TEAM,
                [
                    (mixed, "all"), (proj, ("all", own_channels, 3)), (qd, "all"), (cols_c, "part"), (group_scale, "whole"),
                ],
                [
                    (span + (features,), BF16, "all"), (span + (own_channels,), BF16, "all"),
                    (part + (own_channels,), BF16, "part"), (states, F32, "part"), ((TEAM, 1, own_channels), F32, "part"),
                ],
                [whole_branch, d_o], [out], d_branch[c], per_matmul * own_channels,
            )
            gs.append(g)
            group_sums.append(group_sum)
            adjoint, hops = pass_on(toward, fades[c], -1)
            adjoints.append(adjoint)
            return whole_branch, d_o, toward, hops

        toward = place
        gu_send = weight_half(after(flat(normed2), branch_own[0]), flat(both), 0)
        d_branch = [at.team_gather(branch_own[0], gu_send)]
        hops = []
        whole_branch, d_o, toward, hops = enter_back(0, whole_branch, d_o, gu_send, *sents[1:])
        gu_halves = [gu_send] + ([weight_half(after(flat(normed2), toward), flat(both), 1)] if ny == 2 else [])
        last_hops = hops
        for c in range(1, micro):
            d_branch.append(at.team_gather(branch_own[c], gu_halves[-1]))
            whole_branch, d_o, toward, last_hops = enter_back(c, whole_branch, d_o, gu_halves[-1], grad_down, *hops[:1])
        adjoints = [adjoint(toward) if c == 0 else adjoint() for c, adjoint in enumerate(adjoints)]
        gu_rows = sum(t.astype(F32) for t in WeightSum(gu_halves, TEAM, hold=adjoints).terms).astype(BF16)
        gu_rows = jnp.swapaxes(gu_rows, 0, 1).reshape(nz, TEAM * rows, 2 * own_ff)
        gu_sum = lax.psum_scatter(gu_rows, "seq", scatter_dimension=0, tiled=False).reshape(TEAM, rows, 2 * own_ff)
        paired = (micro, TEAM // 2, length, features)

        d_normed, dn_sent = [], []
        for c in range(micro):
            rows_c, cols_c = (a[c * TEAM : (c + 1) * TEAM] for a in (count_row, count_col))
            held = (toward,) if c == 0 else (*ffn_sent, *o_halves, *out_halves)
            d_q, d_fv, logit_sum, even, odd = over_sequences(
                mix_back_kernel, turn("mix_back", c, *held), c, TEAM,
                [
                    (proj, ("all", own_channels, 0)), (proj, ("all", own_channels, 1)), (proj, ("all", own_channels, 2)),
                    (running, "all"), (qd, "all"), (kg, "all"), (gs[c], "part"), (entering[c], "part"), (adjoints[c], "part"),
                    (bound, "whole"), (rows_c, "part"), (cols_c, "part"), (d_o, "all"),
                ],
                [
                    (span + (own_channels,), BF16, "all"), (span + (2 * own_channels,), BF16, "all"),
                    ((TEAM, 1, own_channels), F32, "part"), (pair, BF16, "pair"), (pair, BF16, "pair"),
                ],
                [d_q, d_fv], [mix], (), per_matmul * wide,
            )
            logit_sums.append(logit_sum)
            summed, sent, _ = at.team_sum(even[None], odd[None], ())
            d_normed.append(summed)
            dn_sent.append(sent)
            if c == 0:
                even, odd = over_sequences(
                    share_kernel, after(place, d_q, *last_hops[:1]), 0, total, [(hidden, "part")],
                    [((micro * TEAM // 2, length, features), BF16, "pair")] * 2, (), [down], (), 2 * tokens * own_ff * features,
                )
                o_halves = weight_halves(after(flat(normed), even, *last_hops[1:2], *dn_sent), flat(d_o))
                out_halves = weight_halves(after(flat(gated), *o_halves), flat(whole_branch))
                even, ffn_near = even.reshape(paired), after(at.swap(odd, 1), *o_halves).reshape(paired)
                ffn_sent = [(even[k, 1].astype(F32) + ffn_near[k, 1].astype(F32)).astype(BF16) for k in range(micro)]
                block_out = [
                    residual[k] + (even[k, 0].astype(F32) + ffn_near[k, 0].astype(F32) + at.swap(ffn_sent[k], 2).astype(F32))
                    for k in range(micro)
                ]
                block_out = [a.astype(BF16) for a in block_out]
        last, d_q = d_fv, after(d_q, d_fv)
        d_normed = [summed(last)[0] for summed in d_normed]
        if ny == 2:
            fv_halves = [weight_half(flat(normed), flat(d_fv), 0)]
            q_halves = [weight_half(after(flat(normed), *fv_halves), flat(d_q), 0)]
            fv_moved = at.swap_y(fv_halves[0], 1)
            q_moved = at.swap_y(after(q_halves[0], fv_moved), 1)
            out_halves[0] = after(out_halves[0], q_moved)
            left = after(flat(normed), *q_halves, *dn_sent)
            fv_halves.append(weight_half(left, flat(d_fv), 1))
            q_halves.append(weight_half(left, flat(d_q), 1))
        else:
            fv_halves, q_halves = weight_halves(flat(normed), flat(d_fv)), weight_halves(flat(normed), flat(d_q))
            fv_moved, q_moved = None, None
        o_part, out_part = WeightSum(o_halves, TEAM), WeightSum(out_halves, 1)
        fv_part, q_part = WeightSum(fv_halves, TEAM, fv_moved), WeightSum(q_halves, TEAM, q_moved)
        sent = o_part.step(fv_halves[-1], q_halves[-1])
        sent = fv_part.step(sent, *d_normed)
        q_sent = q_part.step(sent)
        sent = o_part.step(q_sent)
        sent = out_part.step(sent)
        gu_final = lambda i: lax.dynamic_index_in_dim(after(gu_sum, q_sent), i, 0, False)
        sent = fv_part.step(sent)
        sent = q_part.step(sent)
        sent = out_part.step(sent)
        d_normed, block_out = jnp.stack(d_normed), jnp.stack(block_out)
        x = block_in.astype(F32)
        rms_one = lax.rsqrt(jnp.mean(x * x, axis=-1, keepdims=True) + EPSILON)
        attn_sum = jnp.sum(d_normed * x * rms_one, axis=(0, 1))
        scaled = d_normed * attn_scale
        in_grad = jnp.stack(d_residual) + rms_one * (
            scaled - x * rms_one * rms_one * jnp.mean(scaled * x, axis=-1, keepdims=True)
        )

        logit_sum = bound[0] * (1.0 - bound[0]) * sum(jnp.sum(a, axis=(0, 1)) for a in logit_sums)
        logit_all = jnp.where(
            jnp.arange(TEAM)[None, :, None] == at.rank, logit_sum.reshape(ny, 1, strip), 0.0
        ).reshape(features)
        group_all = jnp.sum(sum(jnp.sum(a, axis=(0, 1)) for a in group_sums).reshape(heads, HEAD), axis=0)
        sums = at.everyone_sum(after(jnp.concatenate([attn_sum, sum(gain_sums), logit_all, group_all]), q_sent))

        grad_gu = out_of_team(
            [gu_final(at.rank ^ j).astype(BF16) for j in range(TEAM)], partial(place_cases_kernel, ff_strip)
        )
        parts = [part.finish(sums, grad_gu) for part in (q_part, fv_part, o_part)]
        grad_mix = out_of_team(
            [jnp.concatenate([part(at.rank ^ j) for part in parts], axis=1).astype(BF16) for j in range(TEAM)],
            partial(place_kernel, strip),
        )
        grad_out = out_part.finish(sums)(0)
        here = (at.y * TEAM + at.rank) * nz + at.z

        def mine(start, size):
            return lax.dynamic_slice_in_dim(sums, start + here * size, size)

        return (
            block_out,
            in_grad,
            grad_mix,
            grad_out,
            grad_gu,
            grad_down,
            mine(0, rows),
            mine(features, rows),
            mine(3 * features, group_gain.shape[0]),
            mine(2 * features, rows),
        )

    return local


def solution(mesh):
    devices = mesh.devices.reshape(-1, TEAM, mesh.shape["seq"])
    tokens = P(("y", "team"), "seq", None)
    matrix = P(("y", "team", "seq"), None)
    vector = P(("y", "team", "seq"))
    return jax.shard_map(
        build(devices.shape[0], devices.shape[2]),
        mesh=Mesh(devices, ("y", "team", "seq")),
        in_specs=(tokens, P(("y", "team"), "seq"), tokens) + (matrix,) * 4 + (vector,) * 4,
        out_specs=(tokens, tokens) + (matrix,) * 4 + (vector,) * 4,
        check_vma=False,
    )
```

```python
from functools import partial

import jax
import jax.numpy as jnp
from jax import lax
from jax.experimental import pallas as pl
from jax.experimental.pallas import tpu as pltpu
from jax.sharding import Mesh, PartitionSpec as P

HEAD = 128
TEAM = 4
EPSILON = 1e-06
SCALE = HEAD**-0.5
F32 = jnp.float32
BF16 = jnp.bfloat16
VMEM_LIMIT = 60 * 1024 * 1024


class Places:
    def __init__(self, ny, nz):
        self.ny, self.nz = ny, nz
        self.rank, self.y, self.z = lax.axis_index("team"), lax.axis_index("y"), lax.axis_index("seq")

    def swap(self, value, bits):
        return lax.ppermute(value, "team", [(i, i ^ bits) for i in range(TEAM)])

    def swap_y(self, value, bits):
        return lax.ppermute(value, "y", [(i, i ^ bits) for i in range(self.ny)])

    def swap_z(self, value, bits):
        return lax.ppermute(value, "seq", [(i, i ^ bits) for i in range(self.nz)])

    def by_rank(self, stack):
        odd, high = (self.rank & 1) == 1, (self.rank & 2) == 2
        stack = jnp.where(odd, jnp.concatenate([stack[1:2], stack[0:1], stack[3:4], stack[2:3]]), stack)
        return jnp.where(high, jnp.concatenate([stack[2:], stack[:2]]), stack)

    def team_gather(self, own, *held):
        one, two = self.swap(own, 1), self.swap(own, 2)
        return [own, one, two, self.swap(after(two, *held), 1)]

    def team_sum(self, even, odd, first_held, *held):
        near = self.swap(after(odd, *first_held), 1)
        sent = (even[:, 1].astype(F32) + after(near, *held)[:, 1].astype(F32)).astype(BF16)
        far = self.swap(sent, 2)
        return lambda *held: even[:, 0].astype(F32) + near[:, 0].astype(F32) + after(far, *held).astype(F32), sent, far


    def gather_blocks(self, own):
        found = {(0, 0): own}
        for step in [1 << i for i in reversed(range(self.nz.bit_length() - 1))]:
            found.update({(0, dz ^ step): self.swap_z(v, step) for (_, dz), v in list(found.items())})
        for step in [1 << i for i in range(self.ny.bit_length() - 1)]:
            found.update({(dy ^ step, dz): self.swap_y(v, step) for (dy, dz), v in list(found.items())})
        return found

    def everyone_sum(self, value):
        for step in (2, 1):
            value = value + self.swap(value, step)
        for step in [1 << i for i in reversed(range(self.ny.bit_length() - 1))]:
            value = value + self.swap_y(value, step)
        for step in [1 << i for i in reversed(range(self.nz.bit_length() - 1))]:
            value = value + self.swap_z(value, step)
        return value


class Weight:
    def __init__(self, at, found):
        self.ny, self.nz = at.ny, at.nz
        if isinstance(found, dict):
            self.s, self.rows, self.n = found[0, 0].shape
            self.keys, self.blocks = list(found), list(found.values())
        else:
            self.s, self.rows, self.n = found.shape[1:]
            self.keys, self.blocks = None, [found]
        self.height = self.ny * self.nz * self.s * self.rows
        self.split = self.rows % 16 == 0
        if not self.split:
            if self.keys:
                found = jnp.zeros((self.ny, self.nz) + self.blocks[0].shape, BF16)
                for (dy, dz), block in zip(self.keys, self.blocks):
                    found = lax.dynamic_update_slice(found, block[None, None], (at.y ^ dy, at.z ^ dz, 0, 0, 0))
            found = found.reshape(self.ny, self.nz, self.s, self.rows, self.n)
            self.blocks = [jnp.swapaxes(found, 1, 2).reshape(self.height, self.n)]

    @property
    def copies(self):
        return self.ny * self.nz * self.s if self.split else 1

    def load(self, refs, place_ref, into, sems):
        for copy in self.copies_of(refs, place_ref, into, sems):
            copy.start()

    def copies_of(self, refs, place_ref, into, sems):
        if not self.split:
            return [pltpu.make_async_copy(refs[0], into, sems.at[0])]
        rank, y, z = place_ref[0], place_ref[1], place_ref[2]
        if self.keys:
            blocks = [(y ^ dy, z ^ dz, ref) for (dy, dz), ref in zip(self.keys, refs)]
        else:
            blocks = [(i // self.nz, i % self.nz, refs[0].at[i]) for i in range(self.ny * self.nz)]
        copies = []
        for there_y, there_z, ref in blocks:
            for j in range(self.s):
                s = rank ^ j if self.s > 1 else 0
                row = ((there_y * self.s + s) * self.nz + there_z) * self.rows
                if not isinstance(row, int):
                    row = pl.multiple_of(row, self.rows)
                copies.append(pltpu.make_async_copy(ref.at[j], into.at[pl.ds(row, self.rows)], sems.at[len(copies)]))
        return copies


def nn(a, b):
    return jnp.dot(a, b, preferred_element_type=F32)


def nt(a, b):
    return lax.dot_general(a, b, (((1,), (1,)), ((), ())), preferred_element_type=F32)


def tn(a, b):
    return lax.dot_general(a, b, (((0,), (0,)), ((), ())), preferred_element_type=F32)


def add_up(matrix, value):
    high = value.astype(BF16)
    rest = value - high.astype(F32)
    mid = rest.astype(BF16)
    low = (rest - mid.astype(F32)).astype(BF16)
    return nn(matrix, high) + nn(matrix, mid) + nn(matrix, low)


def triangle(n, lower):
    row = lax.broadcasted_iota(jnp.int32, (n, n), 0)
    col = lax.broadcasted_iota(jnp.int32, (n, n), 1)
    return row >= col if lower else row <= col


def sigmoid(z):
    return 1.0 / (1.0 + jnp.exp(-z))


def gates(f_pre, lower):
    small = jnp.exp(-jnp.abs(f_pre))
    big_part = 1.0 / (1.0 + small)
    small_part = small * big_part
    positive = f_pre >= 0
    opened = jnp.where(positive, big_part, small_part)
    closed = jnp.where(positive, small_part, big_part)
    return opened, closed, lower + (1.0 - lower) * opened


def wide_blocks(width):
    step = 512
    return [(a, min(a + step, width)) for a in range(0, width, step)]


def take_piece(step, piece_refs, into_ref):
    for j, ref in enumerate(piece_refs):

        @pl.when(step == j)
        def _(ref=ref):
            into_ref[0] = ref[...]


def put_share(step, even_ref, odd_ref, a, b, value):
    value = value.astype(BF16)

    @pl.when(step % 2 == 0)
    def _():
        even_ref[0, :, a:b] = value

    @pl.when(step % 2 == 1)
    def _():
        odd_ref[0, :, a:b] = value


def pick_kernel(strip, place_ref, w_ref, extra_ref, *out_refs):
    rank = place_ref[0]
    count = w_ref.shape[1] // (TEAM * strip)
    for j, out_ref in enumerate(out_refs):
        for k in range(count):
            at = pl.multiple_of((k * TEAM + (rank ^ j)) * strip, strip)
            out_ref[:, k * strip : (k + 1) * strip] = w_ref[:, pl.ds(at, strip)]
        out_ref[:, count * strip :] = extra_ref[...]


def place_kernel(strip, place_ref, *refs):
    out_ref = refs[-1]
    for j, ref in enumerate(refs[:-1]):
        for k in range(ref.shape[1] // strip):
            at = pl.multiple_of((k * TEAM + (place_ref[0] ^ j)) * strip, strip)
            out_ref[:, pl.ds(at, strip)] = ref[:, k * strip : (k + 1) * strip].astype(F32)


def place_cases_kernel(strip, place_ref, *refs):
    out_ref = refs[-1]
    for rank in range(TEAM):

        @pl.when(place_ref[0] == rank)
        def _(rank=rank):
            for j, ref in enumerate(refs[:-1]):
                for k in range(ref.shape[1] // strip):
                    at = (k * TEAM + (rank ^ j)) * strip
                    out_ref[:, at : at + strip] = ref[:, k * strip : (k + 1) * strip].astype(F32)


def mix_kernel(strip, step, fetch, piece_refs, place_ref, row_ref, col_ref, *refs):
    normed_ref, proj_ref, run_ref, qd_ref, kg_ref, ins_ref, leave_ref, fade_ref, scales_ref, lower_ref = refs
    channels = lower_ref.shape[1]
    (w_ref,) = fetch()

    @pl.when(step == 0)
    def _():
        row = lax.broadcasted_iota(jnp.int32, (8, HEAD), 0)
        col = lax.broadcasted_iota(jnp.int32, (8, HEAD), 1)
        pick = jnp.where(row == col, 1.0, 0.0).astype(BF16)
        scales_ref[...] = nt(pick, w_ref[:, 4 * channels :])
        for k in range(channels // strip):
            at = pl.multiple_of((k * TEAM + place_ref[0]) * strip, strip)
            lower_ref[:, k * strip : (k + 1) * strip] = sigmoid(scales_ref[2:3, pl.ds(at, strip)])

    gain = scales_ref[0:1]
    take_piece(step, piece_refs, normed_ref)
    x = normed_ref[0].astype(F32)
    scale = lax.rsqrt(jnp.mean(x * x, axis=-1, keepdims=True) + EPSILON)
    normed_ref[0] = (x * scale * gain).astype(BF16)
    for a, b in wide_blocks(4 * channels):
        proj_ref[0, :, a:b] = nn(normed_ref[0], w_ref[:, a:b])
    lower = lower_ref[...]
    q_pre = proj_ref[0, :, 0:channels]
    f_pre = proj_ref[0, :, channels : 2 * channels]
    _, closed, decays = gates(f_pre, lower)
    keys = (1.0 - lower) * closed
    length = x.shape[0]
    causal = triangle(length, True)
    running = add_up(causal.astype(BF16), jnp.log(decays))
    run_ref[0] = running
    row, col = row_ref[0], col_ref[0]
    alive = (col[length - 1 :] == 0).astype(F32)
    tail = (col == col[length - 1 :]).astype(F32)
    final = running[length - 1 :]
    fade_ref[0] = jnp.exp(final) * alive
    qd_ref[0] = (q_pre * sigmoid(q_pre) * jnp.exp(running)).astype(BF16)
    kg_ref[0] = (keys * jnp.exp(-running)).astype(BF16)
    last = (keys * jnp.exp(final - running) * tail).astype(BF16)
    mask = jnp.where(causal & (col == row), 1.0, 0.0)
    for h in range(channels // HEAD):
        cut = slice(h * HEAD, (h + 1) * HEAD)
        values = proj_ref[0, :, 2 * channels + h * HEAD : 2 * channels + (h + 1) * HEAD].astype(BF16)
        scores = (nt(qd_ref[0, :, cut], kg_ref[0, :, cut]) * mask).astype(BF16)
        ins_ref[0, :, cut] = nn(scores, values) * SCALE
        leave_ref[0, h] = tn(last[:, cut], values)


def out_kernel(step, fetch, piece_refs, ins_ref, qd_ref, o_ref, state_ref, col_ref, group_ref, *refs):
    mixed_ref, gated_ref, even_ref, odd_ref = refs
    channels = ins_ref.shape[2]
    alive = (col_ref[0] == 0).astype(F32) * SCALE
    for h in range(channels // HEAD):
        cut = slice(h * HEAD, (h + 1) * HEAD)
        mixed = ins_ref[0, :, cut] + alive * nn(qd_ref[0, :, cut], state_ref[0, h])
        mixed_ref[0, :, cut] = mixed
        scale = lax.rsqrt(jnp.mean(mixed * mixed, axis=-1, keepdims=True) + EPSILON)
        o_pre = o_ref[0, :, cut]
        gated_ref[0, :, cut] = (mixed * scale * group_ref[...] * (o_pre * sigmoid(o_pre))).astype(BF16)
    (w_ref,) = fetch()
    for a, b in wide_blocks(w_ref.shape[1]):
        put_share(step, even_ref, odd_ref, a, b, nn(gated_ref[0], w_ref[:, a:b]))


def up_kernel(step, fetch, piece_refs, normed_ref, hidden_ref, first_ref, second_ref):
    width = hidden_ref.shape[2]
    take_piece(step, piece_refs, normed_ref)
    (w_ref,) = fetch()
    for a, b in wide_blocks(width):
        gate = nn(normed_ref[0], w_ref[:, a:b])
        up = nn(normed_ref[0], w_ref[:, width + a : width + b])
        s = sigmoid(gate)
        silu = gate * s
        hidden_ref[0, :, a:b] = (silu * up).astype(BF16)
        first_ref[0, :, a:b] = (up * (s * (1.0 + gate * (1.0 - s)))).astype(BF16)
        second_ref[0, :, a:b] = silu.astype(BF16)


def down_back_kernel(step, fetch, piece_refs, cot_ref, first_ref, second_ref, both_ref, even_ref, odd_ref):
    width = first_ref.shape[2]
    down_ref, w_ref = fetch()
    for a, b in wide_blocks(width):
        d_hidden = nt(cot_ref[0], down_ref[a:b, :])
        both_ref[0, :, a:b] = (d_hidden * first_ref[0, :, a:b].astype(F32)).astype(BF16)
        both_ref[0, :, width + a : width + b] = (d_hidden * second_ref[0, :, a:b].astype(F32)).astype(BF16)
    for a, b in wide_blocks(w_ref.shape[0]):
        put_share(step, even_ref, odd_ref, a, b, nt(both_ref[0], w_ref[a:b, :]))


def out_back_kernel(step, fetch, piece_refs, mixed_ref, o_ref, qd_ref, col_ref, group_ref, *refs):
    branch_ref, d_o_ref, g_ref, toward_ref, sum_ref = refs
    channels = mixed_ref.shape[2]
    take_piece(step, piece_refs, branch_ref)
    alive = (col_ref[0] == 0).astype(F32)
    group = group_ref[...]
    (w_ref,) = fetch()
    d_gated_all = nt(branch_ref[0], w_ref[...])
    for h in range(channels // HEAD):
        cut = slice(h * HEAD, (h + 1) * HEAD)
        d_gated = d_gated_all[:, cut]
        mixed = mixed_ref[0, :, cut]
        scale = lax.rsqrt(jnp.mean(mixed * mixed, axis=-1, keepdims=True) + EPSILON)
        unit = mixed * scale
        o_pre = o_ref[0, :, cut]
        s = sigmoid(o_pre)
        silu = o_pre * s
        both = d_gated * unit
        d_o_ref[0, :, cut] = (both * group * (s * (1.0 + o_pre * (1.0 - s)))).astype(BF16)
        sum_ref[0, :, cut] = jnp.sum(both * silu, axis=0, keepdims=True)
        d_unit = d_gated * group * silu
        d_mixed = scale * (d_unit - unit * jnp.mean(d_unit * unit, axis=-1, keepdims=True))
        g = (d_mixed * SCALE).astype(BF16)
        g_ref[0, :, cut] = g
        reach = (qd_ref[0, :, cut].astype(F32) * alive).astype(BF16)
        toward_ref[0, h] = tn(reach, g)


def mix_back_kernel(
    step, fetch, piece_refs, q_ref, f_ref, v_ref, run_ref, qd_ref, kg_ref, g_ref, state_ref, adjoint_ref, lower_ref,
    row_ref, col_ref, d_o_ref, d_q_ref, d_fv_ref, sum_ref, even_ref, odd_ref,
):
    channels = lower_ref.shape[1]
    length = row_ref.shape[2]
    lower = lower_ref[...]
    row, col = row_ref[0], col_ref[0]
    alive = (col == 0).astype(F32)
    alive_end = alive[length - 1 :]
    tail = (col == col[length - 1 :]).astype(F32)
    mask = jnp.where(triangle(length, True) & (col == row), 1.0, 0.0)
    later = triangle(length, False).astype(BF16)
    eye = lax.broadcasted_iota(jnp.int32, (HEAD, HEAD), 0) == lax.broadcasted_iota(jnp.int32, (HEAD, HEAD), 1)
    for h in range(channels // HEAD):
        cut = slice(h * HEAD, (h + 1) * HEAD)
        q_pre, f_pre = q_ref[0, :, cut], f_ref[0, :, cut]
        values = v_ref[0, :, cut].astype(BF16)
        running = run_ref[0, :, cut]
        qd, kg, g = qd_ref[0, :, cut], kg_ref[0, :, cut], g_ref[0, :, cut]
        state, adjoint = state_ref[0, h], adjoint_ref[0, h]
        low = lower[:, cut]
        opened, closed, decays = gates(f_pre, low)
        keys = (1.0 - low) * closed
        final = running[length - 1 :]
        last_factor = jnp.exp(final - running) * tail
        last = (keys * last_factor).astype(BF16)
        scores = (nt(qd, kg) * mask).astype(BF16)
        d_values = tn(scores, g) + nn(last, adjoint)
        d_scores = (nt(g, values) * mask).astype(BF16)
        d_qd = nn(d_scores, kg) + alive * nt(g, state)
        d_kg = tn(d_scores, qd)
        d_last = nt(values, adjoint)
        part_last = d_last * last.astype(F32)
        moved = d_qd * qd.astype(F32) - d_kg * kg.astype(F32) - part_last
        passed = jnp.sum(adjoint.astype(F32) * state.astype(F32), axis=1, keepdims=True)
        passed = jnp.sum(jnp.where(eye, passed, 0.0), axis=0, keepdims=True)
        d_final = jnp.sum(part_last, axis=0, keepdims=True) + passed * jnp.exp(final) * alive_end
        d_log = add_up(later, moved) + d_final
        d_queries = d_qd * jnp.exp(running)
        d_keys = d_kg * jnp.exp(-running) + d_last * last_factor
        common = d_log / decays - d_keys
        s = sigmoid(q_pre)
        d_q_ref[0, :, cut] = (d_queries * (s * (1.0 + q_pre * (1.0 - s)))).astype(BF16)
        d_fv_ref[0, :, cut] = ((1.0 - low) * opened * closed * common).astype(BF16)
        d_fv_ref[0, :, channels + h * HEAD : channels + (h + 1) * HEAD] = d_values.astype(BF16)
        sum_ref[0, :, cut] = jnp.sum(closed * common, axis=0, keepdims=True)
    (w_ref,) = fetch()
    parts = [(0, d_q_ref), (channels, d_fv_ref), (3 * channels, d_o_ref)]
    for a, b in wide_blocks(w_ref.shape[0]):
        value = sum(nt(ref[0], w_ref[a:b, k : k + ref.shape[2]]) for k, ref in parts)
        put_share(step, even_ref, odd_ref, a, b, value)


def share_kernel(step, fetch, piece_refs, left_ref, even_ref, odd_ref):
    (w_ref,) = fetch()
    for a, b in wide_blocks(w_ref.shape[1]):
        put_share(step, even_ref, odd_ref, a, b, nn(left_ref[0], w_ref[:, a:b]))


def over_sequences(kernel, place, chunk, count, ins, outs, held=(), weights=(), pieces=(), flops=0):
    def spec(shape, kind):
        if kind == "scalars":
            return pl.BlockSpec(memory_space=pltpu.SMEM)
        if kind == "whole":
            return pl.BlockSpec(shape, lambda i: (0,) * len(shape), pipeline_mode=pl.Buffered(1))
        if kind == "pair":
            return pl.BlockSpec((1,) + shape[1:], lambda i: (i // 2,) + (0,) * (len(shape) - 1))
        offset = 0 if kind == "part" else chunk * count
        if isinstance(kind, tuple):
            _, width, at = kind
            return pl.BlockSpec((1, shape[1], width), lambda i: (offset + i, 0, at))
        return pl.BlockSpec((1,) + shape[1:], lambda i: (offset + i,) + (0,) * (len(shape) - 1))

    anywhere = pl.BlockSpec(memory_space=pl.ANY)
    arrays, specs = [place], [pl.BlockSpec(memory_space=pltpu.SMEM)]
    for w in weights:
        arrays += w.blocks
        specs += [anywhere] * len(w.blocks)
    for piece in pieces:
        arrays.append(piece)
        specs.append(spec(piece.shape, "whole"))
    arrays += [a for a, _ in ins]
    specs += [spec(a.shape, kind) for a, kind in ins]
    aliases = {}
    for i, array in enumerate(held):
        if array is not None:
            aliases[len(arrays)] = i
            arrays.append(array)
            specs.append(anywhere)

    def body(*refs):
        refs = list(refs)
        place_ref = refs.pop(0)
        block_refs = [[refs.pop(0) for _ in w.blocks] for w in weights]
        piece_refs = [refs.pop(0) for _ in pieces]
        in_refs = [refs.pop(0) for _ in ins]
        del refs[: len(aliases)]
        out_refs = [refs.pop(0) for _ in outs]
        into, sems = refs[: len(weights)], refs[len(weights) :]
        step = pl.program_id(0)

        @pl.when(step == 0)
        def _():
            for w, blocks, ref, sem in zip(weights, block_refs, into, sems):
                w.load(blocks, place_ref, ref, sem)

        def fetch():
            @pl.when(step == 0)
            def _():
                for w, blocks, ref, sem in zip(weights, block_refs, into, sems):
                    for copy in w.copies_of(blocks, place_ref, ref, sem):
                        copy.wait()

            return into

        kernel(step, fetch, piece_refs, *in_refs, *out_refs)

    size = sum(a.size * a.dtype.itemsize for a in arrays)
    return pl.pallas_call(
        body,
        grid=(count,),
        in_specs=specs,
        out_specs=[spec(shape, kind) for shape, _, kind in outs],
        out_shape=[jax.ShapeDtypeStruct(shape, kind) for shape, kind, _ in outs],
        scratch_shapes=[pltpu.VMEM((w.height, w.n), BF16) for w in weights]
        + [pltpu.SemaphoreType.DMA((w.copies,)) for w in weights],
        input_output_aliases=aliases,
        compiler_params=pltpu.CompilerParams(vmem_limit_bytes=VMEM_LIMIT),
        cost_estimate=pl.CostEstimate(flops=flops, bytes_accessed=size // 4, transcendentals=0),
    )(*arrays)


def after(value, *others):
    return lax.optimization_barrier((value,) + others)[0] if others else value


def build(ny, nz):
    def local(block_in, doc_starts, out_grad, w_mix, w_out, w_gu, w_down, attn_gain, ffn_gain, group_gain, lower_logit):
        at = Places(ny, nz)
        micro, length, features = block_in.shape
        rows = w_mix.shape[0]
        own_channels = ny * nz * rows
        heads = own_channels // HEAD
        strip = own_channels // ny
        ff_rows = w_down.shape[0]
        own_ff = ny * nz * ff_rows
        ff_strip = nz * ff_rows
        total = micro * TEAM
        tokens = total * length
        place = jnp.stack([at.rank, at.y, at.z]).astype(jnp.int32)
        team = ("y", "seq")

        def trade(parts, *held):
            return jnp.stack([parts[0]] + [at.swap(after(parts[j], *held), j) for j in range(1, TEAM)])

        def columns_of(matrix, count, width):
            parts = matrix.reshape(rows, count * ny, TEAM, width)
            return [lax.dynamic_index_in_dim(parts, at.rank ^ j, 2, False).reshape(rows, -1) for j in range(TEAM)]

        group_share = jnp.pad(group_gain, (0, rows - group_gain.shape[0]))
        extra = jnp.stack([attn_gain, ffn_gain, lower_logit, group_share], axis=1).astype(BF16)
        extra = jnp.pad(extra, ((0, 0), (0, HEAD - extra.shape[1])))
        mix_width = 4 * own_channels + HEAD
        mix_parts = pl.pallas_call(
            partial(pick_kernel, strip),
            in_specs=[pl.BlockSpec(memory_space=pltpu.SMEM)] + [pl.BlockSpec(memory_space=pltpu.VMEM)] * 2,
            out_specs=[pl.BlockSpec(memory_space=pltpu.VMEM)] * TEAM,
            out_shape=[jax.ShapeDtypeStruct((rows, mix_width), BF16)] * TEAM,
        )(place, w_mix, extra)
        mix_own, out_own = trade(mix_parts), w_out[None]
        starts = doc_starts.astype(BF16)[:, None]
        starts = jnp.concatenate([starts, at.swap(starts, 1)], axis=1)
        starts = jnp.concatenate([starts, at.swap(starts, 2)], axis=1)
        waits = {}
        if (ny, nz) == (2, 4) and micro == 2:
            z1, z2 = (lambda v: at.swap_z(v, 1)), (lambda v: at.swap_z(v, 2))
            cross = lambda v: at.swap_y(v, 1)
            far = lambda v: at.swap(v, 2)
            m1, m2, my = z1(mix_own), z2(mix_own), cross(mix_own)
            oy = cross(after(out_own, mix_own))
            in0 = far(after(block_in[0], mix_own))
            gu_own = trade(columns_of(after(w_gu, mix_own), 2, ff_strip), mix_own)
            done = (m1, m2, my, oy, in0)
            m12, my1, my2 = z1(after(m2, *done)), cross(after(m1, *done)), cross(after(m2, *done))
            o1, o2 = z1(after(out_own, *done)), z2(after(out_own, *done))
            in1 = far(after(block_in[1], *done, gu_own))
            done = (m12, my1, my2, in1, o1, o2)
            my12 = cross(after(m12, *done))
            o12, oy1, oy2 = z1(after(o2, *done)), cross(after(o1, *done)), cross(after(o2, *done))
            g1, g2 = z1(after(gu_own, *done)), z2(after(gu_own, *done))
            gy = cross(after(gu_own, my12))
            cot0 = far(after(out_grad[0], *done))
            oy12 = cross(o12)
            gy1, gy2 = cross(g1), cross(g2)
            cot1 = far(after(out_grad[1], cot0))
            g12 = z1(g2)
            waits["mix", 0] = (o12, g1)
            waits["mix", 1] = (g2, gy, oy1, oy2, oy12)
            waits["hop", 0] = (g12,)
            waits["hop", 1] = (gy1, cot1)
            waits["out", 0] = (gy2,)

            def later(*held):
                gy12 = cross(g12)
                waits["norm", 0] = (gy12,)
                found_gu = found(gu_own, g1, g2, g12, gy, gy1, gy2, gy12)
                return Weight(at, found_gu), Weight(at, lax.all_gather(after(w_down, *held), team)[:, None])

            def found(own, a1, a2, a12, y, y1, y2, y12):
                near = {(0, 0): own, (0, 1): a1, (0, 2): a2, (0, 3): a12}
                return {**near, (1, 0): y, (1, 1): y1, (1, 2): y2, (1, 3): y12}

            mix = Weight(at, found(mix_own, m1, m2, m12, my, my1, my2, my12))
            out = Weight(at, found(out_own, o1, o2, o12, oy, oy1, oy2, oy12))
            inputs, cotangent = (
                [[own, at.swap(own, 1), far_own, at.swap(far_own, 1)] for own, far_own in zip(here, there)]
                for here, there in ((block_in, (in0, in1)), (out_grad, (cot0, cot1)))
            )
        else:
            gu_own = trade(columns_of(w_gu, 2, ff_strip))
            mix, out = (Weight(at, at.gather_blocks(v)) for v in (mix_own, out_own))

            def later(*held):
                return Weight(at, at.gather_blocks(gu_own)), Weight(at, lax.all_gather(w_down, team)[:, None])

            inputs = [at.team_gather(block_in[c]) for c in range(micro)]
            cotangent = [at.team_gather(out_grad[c]) for c in range(micro)]

        def turn(name, c, *others):
            return after(place, *waits.get((name, c), ()), *others)

        upto = (jnp.arange(length)[:, None] <= jnp.arange(length)[None, :]).astype(BF16)
        counts = jnp.dot(starts.reshape(total, length), upto, preferred_element_type=F32)
        count_row = counts.reshape(total, 1, length)
        count_col = counts.reshape(total, length, 1)

        def pass_on(leaving, fade, sign, *held):
            factor = fade.reshape(TEAM, heads, HEAD)[..., None]
            entering = jnp.zeros(leaving.shape, F32)
            hops, moved = [], None
            for k in range(nz - 1):
                if moved is not None:
                    entering = entering + moved.astype(F32)
                pair = (k, k + 1) if sign == 1 else (nz - 1 - k, nz - 2 - k)
                moved = (factor * entering + leaving).astype(BF16)
                moved = lax.ppermute(after(moved, *held) if k == 1 else moved, "seq", [pair])
                hops.append(moved)
            return lambda *held: (entering + after(moved, *held).astype(F32)).astype(BF16), hops

        span, part, pair = (total, length), (TEAM, length), (TEAM // 2, length, features)
        states = (TEAM, heads, HEAD, HEAD)
        wide = 4 * own_channels
        per_matmul = 2 * TEAM * length * features

        normed = proj = running = qd = kg = mixed = gated = None
        normed2 = hidden = first = second = None
        entering, residual, fades, own_normed2 = [], [], [], []
        insides, leavings = [], []
        for c in range(micro):
            rows_c, cols_c = (a[c * TEAM : (c + 1) * TEAM] for a in (count_row, count_col))
            normed, proj, running, qd, kg, inside, leaving, fade, scales, bound = over_sequences(
                partial(mix_kernel, strip), turn("mix", c), c, TEAM,
                [(place, "scalars"), (rows_c, "part"), (cols_c, "part")],
                [
                    (span + (features,), BF16, "all"),
                    (span + (wide,), F32, "all"),
                    (span + (own_channels,), F32, "all"),
                    (span + (own_channels,), BF16, "all"),
                    (span + (own_channels,), BF16, "all"),
                    (part + (own_channels,), F32, "part"),
                    (states, F32, "part"),
                    ((TEAM, 1, own_channels), F32, "part"),
                    ((8, features), F32, "whole"),
                    ((1, own_channels), F32, "whole"),
                ],
                [normed, proj, running, qd, kg], [mix], inputs[c], per_matmul * wide,
            )
            if c == 0:
                attn_scale, ffn_scale = scales[0:1], scales[1:2]
                group_scale = scales[3].reshape(-1, rows)[:, : group_gain.shape[0]].reshape(1, HEAD)
            fades.append(fade)
            insides.append(inside)
            leavings.append(leaving)
            entering.append(pass_on(leaving, fade, 1, *waits.get(("hop", c), ()))[0]())
        gu, down = later(*entering)
        for c in range(micro):
            cols_c = count_col[c * TEAM : (c + 1) * TEAM]
            mixed, gated, even, odd = over_sequences(
                out_kernel, turn("out", c, *leavings), c, TEAM,
                [
                    (insides[c], "part"), (qd, "all"), (proj, ("all", own_channels, 3)), (entering[c], "part"), (cols_c, "part"),
                    (group_scale, "whole"),
                ],
                [
                    (span + (own_channels,), F32, "all"), (span + (own_channels,), BF16, "all"),
                    (pair, BF16, "pair"), (pair, BF16, "pair"),
                ],
                [mixed, gated], [out], (), per_matmul * own_channels,
            )
            summed = at.team_sum(even[None], odd[None], ())[0](*own_normed2)
            residual.append(block_in[c].astype(F32) + summed[0])
            rms_two = lax.rsqrt(jnp.mean(residual[c] * residual[c], axis=-1, keepdims=True) + EPSILON)
            own_normed2.append(after(residual[c] * rms_two * ffn_scale, *waits.get(("norm", c), ())).astype(BF16))

        def flat(a):
            return a.reshape(tokens, a.shape[-1])

        def team_share(left, right, s, *held):
            product = tn(left, right).astype(BF16).reshape(ny, s, nz, -1, right.shape[1])
            product = jnp.swapaxes(product, 1, 2).reshape(ny * nz, -1, right.shape[1])
            summed = lax.psum_scatter(after(product, *held), team, scatter_dimension=0, tiled=False)
            return summed.reshape(s, -1, right.shape[1]), product

        def weight_half(left, right, k):
            size = left.shape[1] // ny
            if ny == 2:
                y = 1 - at.y if k == 0 else at.y
                return tn(lax.dynamic_slice_in_dim(left, y * size, size, 1), right).astype(BF16)
            return tn(left, right).astype(BF16).reshape(ny, size, right.shape[1])

        def weight_halves(left, right):
            return [weight_half(left, right, k) for k in range(2 if ny == 2 else 1)]

        class WeightSum:
            def __init__(self, parts, s, moved=None, hold=()):
                self.s, width = s, parts[0].shape[-1]
                if ny == 2:
                    send, keep = parts
                    terms = [keep, at.swap_y(send, 1) if moved is None else moved]
                else:
                    terms = parts
                    for step in [1 << i for i in reversed(range(ny.bit_length() - 1))]:
                        halves = [t.reshape((t.shape[0] // 2 // step, 2, step) + t.shape[1:])[0] for t in terms]
                        bit = (at.y // step) % 2
                        pick = lambda k: [lax.dynamic_index_in_dim(t, k, 0, False) for t in halves]
                        send = sum(t.astype(F32) for t in pick(1 - bit)).astype(BF16)
                        terms = pick(bit) + [at.swap_y(send, step)]
                    terms = [t[0] for t in terms]
                self.terms = [t.reshape(s, nz, -1, width) for t in terms]
                self.terms[-1] = after(self.terms[-1], *hold)
                self.left, self.bit = nz, 0

            def step(self, *held):
                self.left //= 2
                terms = self.terms[:-1] + [after(self.terms[-1], *held)]
                halves = [t.reshape((self.s, self.left, 2) + t.shape[2:]) for t in terms]
                bit = (at.z // (1 << self.bit)) % 2
                pick = lambda k: [lax.dynamic_index_in_dim(t, k, 2, False) for t in halves]
                send = sum(t.astype(F32) for t in pick(1 - bit)).astype(BF16)
                self.terms = pick(bit) + [at.swap_z(send, 1 << self.bit)]
                self.bit += 1
                return send

            def finish(self, *held):
                while self.left > 1:
                    self.step()
                terms = self.terms[:-1] + [after(self.terms[-1], *held)]
                return lambda i: sum(lax.dynamic_index_in_dim(t[:, 0], i, 0, False).astype(F32) for t in terms)

        def out_of_team(parts, kernel):
            parts = [parts[0]] + [at.swap(parts[j], j) for j in range(1, TEAM)]
            return pl.pallas_call(
                kernel,
                in_specs=[pl.BlockSpec(memory_space=pltpu.SMEM)] + [pl.BlockSpec(memory_space=pltpu.VMEM)] * TEAM,
                out_specs=pl.BlockSpec(memory_space=pltpu.VMEM),
                out_shape=jax.ShapeDtypeStruct((rows, TEAM * parts[0].shape[1]), F32),
                compiler_params=pltpu.CompilerParams(vmem_limit_bytes=VMEM_LIMIT),
            )(place, *parts)

        both = whole_branch = None
        all_cot = jnp.concatenate([jnp.stack(pieces) for pieces in cotangent])
        for c in range(micro):
            normed2, hidden, first, second = over_sequences(
                up_kernel, turn("up", c, all_cot), c, TEAM,
                [],
                [(span + (features,), BF16, "all")] + [(span + (own_ff,), BF16, "all")] * 3,
                [normed2, hidden, first, second], [gu],
                at.team_gather(own_normed2[c], *(() if hidden is None else (hidden,))), per_matmul * 2 * own_ff,
            )
        d_residual, d_branch, branch_own, gain_sums, sents = [], [], [], [], []
        held, moved, sums_of = (), (), []
        for c in range(micro):
            both, even, odd = over_sequences(
                down_back_kernel, turn("down_back", c, *held), c, TEAM,
                [(all_cot, "all"), (first, "all"), (second, "all")],
                [(span + (2 * own_ff,), BF16, "all"), (pair, BF16, "pair"), (pair, BF16, "pair")],
                [both], [down, gu], (), per_matmul * 3 * own_ff,
            )
            if c == 0:
                grad_down, down_product = team_share(after(flat(hidden), even), flat(all_cot), 1)
                grad_down = grad_down[0].astype(F32)
            else:
                finish(c - 1, even)
            d_normed2_of, sent, far = at.team_sum(even[None], odd[None], moved, *((down_product,) if c == 0 else branch_own))
            held, moved = (down_product, sent), (far,)
            sents.append(sent)
            sums_of.append(d_normed2_of)

            def finish(c, *held):
                d_normed2 = sums_of[c](*held)[0]
                res = residual[c]
                rms_two = lax.rsqrt(jnp.mean(res * res, axis=-1, keepdims=True) + EPSILON)
                gain_sums.append(jnp.sum(d_normed2 * res * rms_two, axis=0))
                scaled = d_normed2 * ffn_scale
                d_residual.append(
                    out_grad[c].astype(F32)
                    + rms_two * (scaled - res * rms_two * rms_two * jnp.mean(scaled * res, axis=-1, keepdims=True))
                )
                branch_own.append(d_residual[c].astype(BF16))
                return branch_own[c]

        finish(micro - 1)

        d_q = d_fv = d_o = None
        gs, group_sums, logit_sums, adjoints = [], [], [], []

        def enter_back(c, whole_branch, d_o, *held):
            cols_c = count_col[c * TEAM : (c + 1) * TEAM]
            whole_branch, d_o, g, toward, group_sum = over_sequences(
                out_back_kernel, turn("out_back", c, *held), c, TEAM,
                [
                    (mixed, "all"), (proj, ("all", own_channels, 3)), (qd, "all"), (cols_c, "part"), (group_scale, "whole"),
                ],
                [
                    (span + (features,), BF16, "all"), (span + (own_channels,), BF16, "all"),
                    (part + (own_channels,), BF16, "part"), (states, F32, "part"), ((TEAM, 1, own_channels), F32, "part"),
                ],
                [whole_branch, d_o], [out], d_branch[c], per_matmul * own_channels,
            )
            gs.append(g)
            group_sums.append(group_sum)
            adjoint, hops = pass_on(toward, fades[c], -1)
            adjoints.append(adjoint)
            return whole_branch, d_o, toward, hops

        toward = place
        gu_send = weight_half(after(flat(normed2), branch_own[0]), flat(both), 0)
        d_branch = [at.team_gather(branch_own[0], gu_send)]
        hops = []
        whole_branch, d_o, toward, hops = enter_back(0, whole_branch, d_o, gu_send, *sents[1:])
        gu_halves = [gu_send] + ([weight_half(after(flat(normed2), toward), flat(both), 1)] if ny == 2 else [])
        last_hops = hops
        for c in range(1, micro):
            d_branch.append(at.team_gather(branch_own[c], gu_halves[-1]))
            whole_branch, d_o, toward, last_hops = enter_back(c, whole_branch, d_o, gu_halves[-1], grad_down, *hops[:1])
        adjoints = [adjoint(toward) if c == 0 else adjoint() for c, adjoint in enumerate(adjoints)]
        gu_rows = sum(t.astype(F32) for t in WeightSum(gu_halves, TEAM, hold=adjoints).terms).astype(BF16)
        gu_rows = jnp.swapaxes(gu_rows, 0, 1).reshape(nz, TEAM * rows, 2 * own_ff)
        gu_sum = lax.psum_scatter(gu_rows, "seq", scatter_dimension=0, tiled=False).reshape(TEAM, rows, 2 * own_ff)
        paired = (micro, TEAM // 2, length, features)

        d_normed, dn_sent = [], []
        for c in range(micro):
            rows_c, cols_c = (a[c * TEAM : (c + 1) * TEAM] for a in (count_row, count_col))
            held = (toward,) if c == 0 else (*ffn_sent, *o_halves, *out_halves)
            d_q, d_fv, logit_sum, even, odd = over_sequences(
                mix_back_kernel, turn("mix_back", c, *held), c, TEAM,
                [
                    (proj, ("all", own_channels, 0)), (proj, ("all", own_channels, 1)), (proj, ("all", own_channels, 2)),
                    (running, "all"), (qd, "all"), (kg, "all"), (gs[c], "part"), (entering[c], "part"), (adjoints[c], "part"),
                    (bound, "whole"), (rows_c, "part"), (cols_c, "part"), (d_o, "all"),
                ],
                [
                    (span + (own_channels,), BF16, "all"), (span + (2 * own_channels,), BF16, "all"),
                    ((TEAM, 1, own_channels), F32, "part"), (pair, BF16, "pair"), (pair, BF16, "pair"),
                ],
                [d_q, d_fv], [mix], (), per_matmul * wide,
            )
            logit_sums.append(logit_sum)
            summed, sent, _ = at.team_sum(even[None], odd[None], ())
            d_normed.append(summed)
            dn_sent.append(sent)
            if c == 0:
                even, odd = over_sequences(
                    share_kernel, after(place, d_q, *last_hops[:1]), 0, total, [(hidden, "part")],
                    [((micro * TEAM // 2, length, features), BF16, "pair")] * 2, (), [down], (), 2 * tokens * own_ff * features,
                )
                o_halves = weight_halves(after(flat(normed), even, *last_hops[1:2], *dn_sent), flat(d_o))
                out_halves = weight_halves(after(flat(gated), *o_halves), flat(whole_branch))
                even, ffn_near = even.reshape(paired), after(at.swap(odd, 1), *o_halves).reshape(paired)
                ffn_sent = [(even[k, 1].astype(F32) + ffn_near[k, 1].astype(F32)).astype(BF16) for k in range(micro)]
                block_out = [
                    residual[k] + (even[k, 0].astype(F32) + ffn_near[k, 0].astype(F32) + at.swap(ffn_sent[k], 2).astype(F32))
                    for k in range(micro)
                ]
                block_out = [a.astype(BF16) for a in block_out]
        last, d_q = d_fv, after(d_q, d_fv)
        d_normed = [summed(last)[0] for summed in d_normed]
        if ny == 2:
            fv_halves = [weight_half(flat(normed), flat(d_fv), 0)]
            q_halves = [weight_half(after(flat(normed), *fv_halves), flat(d_q), 0)]
            fv_moved = at.swap_y(fv_halves[0], 1)
            q_moved = at.swap_y(after(q_halves[0], fv_moved), 1)
            out_halves[0] = after(out_halves[0], q_moved)
            left = after(flat(normed), *q_halves, *dn_sent)
            fv_halves.append(weight_half(left, flat(d_fv), 1))
            q_halves.append(weight_half(left, flat(d_q), 1))
        else:
            fv_halves, q_halves = weight_halves(flat(normed), flat(d_fv)), weight_halves(flat(normed), flat(d_q))
            fv_moved, q_moved = None, None
        o_part, out_part = WeightSum(o_halves, TEAM), WeightSum(out_halves, 1)
        fv_part, q_part = WeightSum(fv_halves, TEAM, fv_moved), WeightSum(q_halves, TEAM, q_moved)
        sent = o_part.step(fv_halves[-1], q_halves[-1])
        sent = fv_part.step(sent, *d_normed)
        q_sent = q_part.step(sent)
        sent = o_part.step(q_sent)
        sent = out_part.step(sent)
        gu_final = lambda i: lax.dynamic_index_in_dim(after(gu_sum, q_sent), i, 0, False)
        sent = fv_part.step(sent)
        sent = q_part.step(sent)
        sent = out_part.step(sent)
        d_normed, block_out = jnp.stack(d_normed), jnp.stack(block_out)
        x = block_in.astype(F32)
        rms_one = lax.rsqrt(jnp.mean(x * x, axis=-1, keepdims=True) + EPSILON)
        attn_sum = jnp.sum(d_normed * x * rms_one, axis=(0, 1))
        scaled = d_normed * attn_scale
        in_grad = jnp.stack(d_residual) + rms_one * (
            scaled - x * rms_one * rms_one * jnp.mean(scaled * x, axis=-1, keepdims=True)
        )

        logit_sum = bound[0] * (1.0 - bound[0]) * sum(jnp.sum(a, axis=(0, 1)) for a in logit_sums)
        logit_all = jnp.where(
            jnp.arange(TEAM)[None, :, None] == at.rank, logit_sum.reshape(ny, 1, strip), 0.0
        ).reshape(features)
        group_all = jnp.sum(sum(jnp.sum(a, axis=(0, 1)) for a in group_sums).reshape(heads, HEAD), axis=0)
        sums = at.everyone_sum(after(jnp.concatenate([attn_sum, sum(gain_sums), logit_all, group_all]), q_sent))

        grad_gu = out_of_team(
            [gu_final(at.rank ^ j).astype(BF16) for j in range(TEAM)], partial(place_cases_kernel, ff_strip)
        )
        parts = [part.finish(sums, grad_gu) for part in (q_part, fv_part, o_part)]
        grad_mix = out_of_team(
            [jnp.concatenate([part(at.rank ^ j) for part in parts], axis=1).astype(BF16) for j in range(TEAM)],
            partial(place_kernel, strip),
        )
        grad_out = out_part.finish(sums)(0)
        here = (at.y * TEAM + at.rank) * nz + at.z

        def mine(start, size):
            return lax.dynamic_slice_in_dim(sums, start + here * size, size)

        return (
            block_out,
            in_grad,
            grad_mix,
            grad_out,
            grad_gu,
            grad_down,
            mine(0, rows),
            mine(features, rows),
            mine(3 * features, group_gain.shape[0]),
            mine(2 * features, rows),
        )

    return local


def solution(mesh):
    devices = mesh.devices.reshape(-1, TEAM, mesh.shape["seq"])
    tokens = P(("y", "team"), "seq", None)
    matrix = P(("y", "team", "seq"), None)
    vector = P(("y", "team", "seq"))
    return jax.shard_map(
        build(devices.shape[0], devices.shape[2]),
        mesh=Mesh(devices, ("y", "team", "seq")),
        in_specs=(tokens, P(("y", "team"), "seq"), tokens) + (matrix,) * 4 + (vector,) * 4,
        out_specs=(tokens, tokens) + (matrix,) * 4 + (vector,) * 4,
        check_vma=False,
    )
```
